32 devices in a mesh: ctx: 8 (over y, x, core), fsdp: 4 (over z).
Axes of the slice: x: 2, y: 2, z: 4, core: 2. Of those that a mesh axis runs over, the one named last changes fastest.
Arguments:
- inputs: float32 [4, 1024, 1536], P('fsdp', 'ctx'), may hold values from -6 to 6
- teacher: float32 [4, 1024, 1536], P('fsdp', 'ctx'), may hold values from -6 to 6
- lengths: int32 [4], P('fsdp'), may hold values from 897 to 1024, as said below
- w_query: bfloat16 [1536, 1536], P('fsdp'), may hold values from -0.15625 to 0.15625
- w_key: bfloat16 [1536, 768], P('fsdp'), may hold values from -0.15625 to 0.15625
- w_value: bfloat16 [1536, 768], P('fsdp'), may hold values from -0.15625 to 0.15625
- w_out: bfloat16 [1536, 1536], P('fsdp'), may hold values from -1.25 to 1.25
- w_gate: bfloat16 [1536, 4096], P('fsdp'), may hold values from -0.15625 to 0.15625
- w_up: bfloat16 [1536, 4096], P('fsdp'), may hold values from -0.15625 to 0.15625
- w_down: bfloat16 [4096, 1536], P('fsdp'), may hold values from -0.09375 to 0.09375
- gain_attn: bfloat16 [1536], P('fsdp'), may hold values from 0.5 to 1.5
- gain_ffn: bfloat16 [1536], P('fsdp'), may hold values from 0.5 to 1.5
Outputs:
- output: float32 [4, 1024, 1536], P('fsdp', 'ctx')
- loss_value: float32 [], replicated
- grad_inputs: float32 [4, 1024, 1536], P('fsdp', 'ctx')
- grad_query: float32 [1536, 1536], P('fsdp')
- grad_key: float32 [1536, 768], P('fsdp')
- grad_value: float32 [1536, 768], P('fsdp')
- grad_out: float32 [1536, 1536], P('fsdp')
- grad_gate: float32 [1536, 4096], P('fsdp')
- grad_up: float32 [1536, 4096], P('fsdp')
- grad_down: float32 [4096, 1536], P('fsdp')
- grad_gain_attn: float32 [1536], P('fsdp')
- grad_gain_ffn: float32 [1536], P('fsdp')
The draws below stay inside these ranges and needn't reach their ends.
Inputs may be any that keep to these rules, and one draw needn't show every extreme that they name: `lengths`: each sequence has more than 896 valid tokens, and some sequence fills all 1024.
All inputs are finite; a program needn't handle non-finite values.
Results may differ from the reference program's by a relative error of at most 0.023.
Values may be sent and summed in bfloat16 or wider, within the bound.
No kernel may reach another device: no remote copies, remote signals or barrier semaphores. Data moves between devices by JAX's collectives and lax.ppermute only.
A program may use at most 320 MiB of HBM per device.

```python
import jax
import jax.numpy as jnp
from jax import lax

D = 1536
HEADS = 16
KV_HEADS = 8
HEAD_DIM = 96
FF = 4096
TOK_DEV = 128
SEQ_LEN = 1024
SEQS = 4


def draw_lengths(key, part):
    key = jax.random.fold_in(key, 11)
    short_key, pick_key = jax.random.split(key)
    shortened = SEQ_LEN - jax.random.randint(short_key, (SEQS,), 0, TOK_DEV)
    chosen = jax.random.randint(pick_key, (), 0, SEQS)
    return jnp.where(jnp.arange(SEQS) == chosen, SEQ_LEN, shortened).astype(jnp.int32)


def block_scale(key, extent, pieces, low, largest):
    level, own = 1.0, jax.random.fold_in(key, 6)
    for dim, parts in pieces:
        draws = jnp.exp(jax.random.uniform(jax.random.fold_in(own, dim), (parts,), jnp.float32, low / len(pieces), largest / len(pieces)))
        level = level * jnp.repeat(draws, extent[dim] // parts).reshape([-1 if axis == dim else 1 for axis in range(len(extent))])
    return level


def centred(own_key, extent, spread, limit, pieces=(), kind=jnp.bfloat16):
    result = spread * jax.random.normal(own_key, extent, jnp.float32)
    if pieces:
        result = result * block_scale(own_key, extent, pieces, -0.22, 0.18)
    return jnp.clip(result, -limit, limit).astype(kind)


def setup_inputs(seed: int = 0) -> dict:
    keys = jax.random.split(jax.random.key(seed), 13)
    return {
        "inputs": centred(keys[0], (SEQS, SEQ_LEN, D), 1.0, 6.0, ((0, 4), (1, 8)), jnp.float32),
        "teacher": centred(keys[1], (SEQS, SEQ_LEN, D), 1.0, 6.0, ((0, 4), (1, 8)), jnp.float32),
        "lengths": draw_lengths(jax.random.fold_in(keys[12], 71), 0),
        "w_query": centred(keys[3], (D, HEADS * HEAD_DIM), D ** -0.5, 0.15625, ((0, 4),)),
        "w_key": centred(keys[4], (D, KV_HEADS * HEAD_DIM), D ** -0.5, 0.15625, ((0, 4),)),
        "w_value": centred(keys[5], (D, KV_HEADS * HEAD_DIM), D ** -0.5, 0.15625, ((0, 4),)),
        "w_out": centred(keys[6], (HEADS * HEAD_DIM, D), (max(1, D // 64)) ** -0.5, 1.25, ((0, 4),)),
        "w_gate": centred(keys[7], (D, FF), D ** -0.5, 0.15625, ((0, 4),)),
        "w_up": centred(keys[8], (D, FF), D ** -0.5, 0.15625, ((0, 4),)),
        "w_down": centred(keys[9], (FF, D), FF ** -0.5, 0.09375, ((0, 4),)),
        "gain_attn": jnp.clip(1.0 + 0.1 * jax.random.normal(keys[10], (D,), jnp.float32), 0.5, 1.5).astype(jnp.bfloat16),
        "gain_ffn": jnp.clip(1.0 + 0.1 * jax.random.normal(keys[11], (D,), jnp.float32), 0.5, 1.5).astype(jnp.bfloat16),
    }


eps_norm = 1e-05
rope_base = 100000.0
highest_level = lax.Precision.HIGHEST

@jax.custom_vjp
def low(v):
    return lax.optimization_barrier(v.astype(jnp.bfloat16)).astype(jnp.float32)

@jax.custom_vjp
def low_back(v):
    return v

def low_keep(v):
    return (low(v), None)

def low_pass(kept, grad):
    return (grad,)

def back_keep(v):
    return (v, None)

def back_low(kept, grad):
    return (low(grad),)
low.defvjp(low_keep, low_pass)
low_back.defvjp(back_keep, back_low)

def norm_scale(features):
    return lax.rsqrt(lax.optimization_barrier(jnp.mean(features * features, axis=-1, keepdims=True)) + eps_norm)

def rotate(features, positions, sign):
    half_dim = features.shape[-1] // 2
    frequencies = rope_base ** (-(jnp.arange(half_dim, dtype=jnp.float32) * 2.0) / features.shape[-1])
    angles = positions.astype(jnp.float32)[:, None] * frequencies[None, :]
    angles = jnp.concatenate([angles, angles], axis=-1)[:, None, :]
    turned = jnp.concatenate([-features[..., half_dim:], features[..., :half_dim]], axis=-1)
    return features * jnp.cos(angles) + sign * turned * jnp.sin(angles)

def attend(queries, key_row_block, value_row_block, seq_length):
    block_rows = min(512, SEQ_LEN)
    grouped_rows = queries.reshape(SEQ_LEN // block_rows, block_rows, KV_HEADS, HEADS // KV_HEADS, HEAD_DIM)
    block_starts = jnp.arange(SEQ_LEN // block_rows, dtype=jnp.int32) * block_rows
    key_positions = jnp.arange(SEQ_LEN, dtype=jnp.int32)

    def score_block(block_item):
        query_tile_rows, block_start = block_item
        logit_scores = jnp.einsum('oqkj,lqj->qkol', query_tile_rows, key_row_block, precision=highest_level)
        logit_scores = low_back(HEAD_DIM ** (-0.5) * logit_scores)
        query_positions = block_start + jnp.arange(block_rows, dtype=jnp.int32)
        allowed = (key_positions[None, :] <= query_positions[:, None]) & (key_positions[None, :] < seq_length)
        probability_narrow = low(jax.nn.softmax(jnp.where(allowed, logit_scores, -1e+30), axis=-1))
        mixed_heads = jnp.einsum('lqpc,cli->plqi', probability_narrow, value_row_block, precision=highest_level)
        return mixed_heads.reshape(block_rows, HEADS * HEAD_DIM)
    blocks = lax.map(jax.checkpoint(score_block), (grouped_rows, block_starts))
    return blocks.reshape(SEQ_LEN, HEADS * HEAD_DIM)

def layer_forward(block_in, target, seq_length, w_query, w_key, w_value, w_out, w_gate, w_up, w_down, gain_attn, gain_ffn):
    positions = jnp.arange(SEQ_LEN, dtype=jnp.int32)
    normed_one = low(block_in * norm_scale(block_in) * gain_attn)
    query_lin = low_back(jnp.dot(normed_one, w_query, precision=highest_level))
    key_lin = low_back(jnp.dot(normed_one, w_key, precision=highest_level))
    value_row_block = low_back(low(jnp.dot(normed_one, w_value, precision=highest_level))).reshape(SEQ_LEN, KV_HEADS, HEAD_DIM)
    queries = low(rotate(query_lin.reshape(SEQ_LEN, HEADS, HEAD_DIM), positions, 1.0))
    key_row_block = low(rotate(key_lin.reshape(SEQ_LEN, KV_HEADS, HEAD_DIM), positions, 1.0))
    attended = low_back(low(attend(queries, key_row_block, value_row_block, seq_length)))
    middle = block_in + low_back(jnp.dot(attended, w_out, precision=highest_level))
    normed_two = low(middle * norm_scale(middle) * gain_ffn)
    gate_pre = low_back(jnp.dot(normed_two, w_gate, precision=highest_level))
    up_value = low_back(jnp.dot(normed_two, w_up, precision=highest_level))
    activated = low(jax.nn.silu(gate_pre) * up_value)
    output = middle + low_back(jnp.dot(activated, w_down, precision=highest_level))
    valid_rows = (positions < seq_length).astype(jnp.float32)
    residual_error = output - target
    return (output, jnp.sum(valid_rows[:, None] * residual_error * residual_error))

def reference(inputs, teacher, lengths, w_query, w_key, w_value, w_out, w_gate, w_up, w_down, gain_attn, gain_ffn):
    params = tuple((weight.astype(jnp.float32) for weight in (w_query, w_key, w_value, w_out, w_gate, w_up, w_down, gain_attn, gain_ffn)))
    valid_count = jnp.sum(lengths).astype(jnp.float32)
    checked_layer = jax.checkpoint(layer_forward)

    def whole_batch(all_inputs, *weights):

        def sequence_step(running_sum, seq_item):
            block_in, target, seq_length = seq_item
            output, squares = checked_layer(block_in, target, seq_length, *weights)
            return (running_sum + squares, output)
        running_sum, outputs = lax.scan(sequence_step, jnp.zeros((), jnp.float32), (all_inputs, teacher, lengths))
        return (outputs, running_sum / valid_count)
    (outputs, loss_value), pullback = jax.vjp(whole_batch, inputs, *params)
    grads = pullback((jnp.zeros_like(outputs), jnp.ones((), jnp.float32)))
    return (outputs, loss_value, grads[0], grads[1], grads[2], grads[3], grads[4], grads[5], grads[6], grads[7], grads[8], grads[9])
```

```python
import jax
import jax.numpy as jnp
from jax import lax
from jax.sharding import PartitionSpec as P

HEADS = 16
KV_HEADS = 8
HEAD_DIM = 96

eps_norm = 1e-05
rope_base = 100000.0
masked_value = -1e30

f32 = jnp.float32
bf16 = jnp.bfloat16


def times(left, right):
    return jnp.dot(left, right, preferred_element_type=f32)


def times_transposed(left, right):
    return lax.dot_general(left, right, (((1,), (1,)), ((), ())), preferred_element_type=f32)


def transposed_times(left, right):
    return lax.dot_general(left, right, (((0,), (0,)), ((), ())), preferred_element_type=f32)


def norm_scale(features):
    return lax.rsqrt(jnp.mean(features * features, axis=-1, keepdims=True) + eps_norm)


def norm_back(upstream, features, row_scale, gain_vector):
    weighted = upstream * gain_vector
    inner_mean = jnp.mean(weighted * features, axis=-1, keepdims=True)
    grad_rows = row_scale * weighted - features * (row_scale * row_scale * row_scale) * inner_mean
    return (grad_rows, jnp.sum(upstream * (features * row_scale), axis=0))


def partner(x, axis, mask):
    return lax.ppermute(x, axis, [(i, i ^ mask) for i in range(lax.axis_size(axis))])


def plane_blocks(x):
    count = lax.axis_size("ctx")
    mine = jnp.stack([x] + [partner(x, "ctx", 2 * s) for s in range(1, count // 2)])
    other = partner(mine, "ctx", 1)
    return jnp.stack([mine, other], axis=1).reshape((count,) + x.shape)


def plane_reduce(parts):
    count = parts.shape[0]
    split = parts.reshape((count // 2, 2) + parts.shape[1:])
    got = partner(split[:, 1], "ctx", 1)
    chip = (split[:, 0].astype(f32) + got.astype(f32)).astype(bf16)
    total = chip[0].astype(f32)
    for s in range(1, count // 2):
        total = total + partner(chip[s], "ctx", 2 * s).astype(f32)
    return total


def butterfly(x, axis):
    mask = 1
    while mask < lax.axis_size(axis):
        x = x + partner(x, axis, mask)
        mask *= 2
    return x


def line_blocks(x):
    return jnp.stack([x] + [partner(x, "fsdp", s) for s in range(1, lax.axis_size("fsdp"))])


def line_reduce(parts):
    total = parts[0].astype(f32)
    for s in range(1, parts.shape[0]):
        total = total + partner(parts[s], "fsdp", s).astype(f32)
    return total


def rope_tables(count):
    half_dim = HEAD_DIM // 2
    frequencies = rope_base ** (-(jnp.arange(half_dim, dtype=f32) * 2.0) / HEAD_DIM)
    angles = jnp.arange(count, dtype=f32)[:, None] * frequencies[None, :]
    angles = jnp.concatenate([angles, angles], axis=-1)[:, None, :]
    return jnp.cos(angles), jnp.sin(angles)


def rotate(features, cosines, sines):
    half_dim = HEAD_DIM // 2
    turned = jnp.concatenate([-features[..., half_dim:], features[..., :half_dim]], axis=-1)
    return features * cosines + turned * sines


def local(
    inputs,
    teacher,
    lengths,
    w_query,
    w_key,
    w_value,
    w_out,
    w_gate,
    w_up,
    w_down,
    gain_attn,
    gain_ffn,
):
    hidden_in = inputs[0]
    target = teacher[0]
    seq_length = lengths[0]
    tokens, width = hidden_in.shape
    C = lax.axis_size("ctx")
    Z = lax.axis_size("fsdp")
    p = lax.axis_index("ctx")
    z = lax.axis_index("fsdp")
    rows_z = width // Z
    seq = C * tokens
    q_heads = HEADS // C
    kv_heads = max(1, KV_HEADS // C)
    kv_copies = max(1, C // KV_HEADS)
    group = q_heads // kv_heads
    q_cols = q_heads * HEAD_DIM
    kv_cols = kv_heads * HEAD_DIM
    ff = w_gate.shape[1]
    ff_piece = ff // (Z * C)
    scale_attn = HEAD_DIM ** (-0.5)
    plane_order = jnp.arange(C, dtype=jnp.int32) ^ p
    line_order = jnp.arange(Z, dtype=jnp.int32) ^ z
    positions = p * tokens + jnp.arange(tokens, dtype=jnp.int32)

    def reorder(x, order):
        return jnp.take(x, order, axis=0)

    def line_columns(x, inverse=False):
        cut = x.reshape(x.shape[0], Z, rows_z)
        return jnp.take(cut, line_order, axis=1).reshape(x.shape)

    gains = reorder(line_blocks(jnp.stack([gain_attn, gain_ffn])), line_order)
    gain_one = gains[:, 0].reshape(width).astype(f32)
    gain_two = gains[:, 1].reshape(width).astype(f32)
    kv_start = (p * KV_HEADS // C) * HEAD_DIM
    qkv_own = jnp.concatenate(
        [
            lax.dynamic_slice_in_dim(w_query, p * q_cols, q_cols, 1),
            lax.dynamic_slice_in_dim(w_key, kv_start, kv_cols, 1),
            lax.dynamic_slice_in_dim(w_value, kv_start, kv_cols, 1),
        ],
        axis=1,
    )
    w_qkv = line_blocks(qkv_own).reshape(width, q_cols + 2 * kv_cols)
    out_cols = width // C
    out_own = lax.dynamic_slice_in_dim(w_out, p * out_cols, out_cols, 1)
    out_mine = reorder(line_blocks(out_own), line_order).reshape(C, q_cols, out_cols)
    out_sent = reorder(out_mine, plane_order)
    out_got = jnp.stack([out_sent[0]] + [partner(out_sent[i], "ctx", i) for i in range(1, C)])
    w_out_rows = reorder(out_got, plane_order).transpose(1, 0, 2).reshape(q_cols, width)

    def ff_columns(w):
        cut = w.reshape(rows_z, Z, C, ff_piece)
        return lax.dynamic_index_in_dim(cut, p, 2, False).reshape(rows_z, Z * ff_piece)

    def ff_rows(w):
        return lax.dynamic_slice_in_dim(w, p * ff_piece, ff_piece, 0)

    ff_own = Z * ff_piece
    gate_up = lax.all_gather(
        jnp.concatenate([ff_columns(w_gate), ff_columns(w_up)], axis=1), "fsdp", axis=0, tiled=True
    )
    w_gate_cols = gate_up[:, :ff_own]
    w_up_cols = gate_up[:, ff_own:]
    w_down_rows = lax.all_gather(ff_rows(w_down), "fsdp", axis=0, tiled=True)
    valid_count = butterfly(lengths.astype(f32), "fsdp")[0]

    scale_one = norm_scale(hidden_in)
    normed_one = (hidden_in * scale_one * gain_one).astype(bf16)
    normed_all = plane_blocks(line_columns(normed_one)).reshape(seq, width)
    qkv = times(normed_all, w_qkv).reshape(C, tokens, q_cols + 2 * kv_cols)
    qkv = reorder(qkv, plane_order).reshape(seq, q_cols + 2 * kv_cols)
    cosines, sines = rope_tables(seq)
    queries = rotate(qkv[:, :q_cols].reshape(seq, q_heads, HEAD_DIM), cosines, sines)
    queries = queries.astype(bf16).reshape(seq, kv_heads, group, HEAD_DIM)
    keys = rotate(
        qkv[:, q_cols : q_cols + kv_cols].reshape(seq, kv_heads, HEAD_DIM), cosines, sines
    ).astype(bf16)
    values = qkv[:, q_cols + kv_cols :].reshape(seq, kv_heads, HEAD_DIM).astype(bf16)
    scores = scale_attn * jnp.einsum(
        "qhgd,khd->hgqk", queries, keys, preferred_element_type=f32
    )
    at = jnp.arange(seq, dtype=jnp.int32)
    allowed = (at[None, :] <= at[:, None]) & (at[None, :] < seq_length)
    scores = jnp.where(allowed, scores, masked_value)
    row_max = jnp.max(scores, axis=-1, keepdims=True)
    weights = jnp.exp(scores - row_max)
    row_sum = jnp.sum(weights, axis=-1, keepdims=True)
    probs = weights / row_sum
    probs_low = probs.astype(bf16)
    attended = jnp.einsum("hgqk,khd->qhgd", probs_low, values, preferred_element_type=f32)
    attended_low = attended.astype(bf16).reshape(seq, q_cols)

    def to_plane(x):
        return reorder(x.reshape((C, tokens) + x.shape[1:]), plane_order)

    attended_plane = to_plane(attended_low).reshape(seq, q_cols)
    mixed = plane_reduce(times(attended_plane, w_out_rows).astype(bf16).reshape(C, tokens, width))
    middle = hidden_in + mixed

    scale_two = norm_scale(middle)
    normed_two = plane_blocks((middle * scale_two * gain_two).astype(bf16)).reshape(seq, width)
    gate_pre = times(normed_two, w_gate_cols)
    up_value = times(normed_two, w_up_cols)
    sigmoid_gate = jax.nn.sigmoid(gate_pre)
    silu_gate = gate_pre * sigmoid_gate
    activated = (silu_gate * up_value).astype(bf16)
    output = middle + plane_reduce(
        times(activated, w_down_rows).astype(bf16).reshape(C, tokens, width)
    )

    valid_rows = (positions < seq_length).astype(f32)
    residual_error = output - target
    squares = jnp.sum(valid_rows[:, None] * residual_error * residual_error)
    loss_value = butterfly(butterfly(squares.reshape(1), "ctx"), "fsdp")[0] / valid_count
    grad_output = valid_rows[:, None] * (2.0 * residual_error) / valid_count

    grad_low = plane_blocks(grad_output.astype(bf16)).reshape(seq, width)
    grad_act = times_transposed(grad_low, w_down_rows)
    grad_gate_pre = (
        grad_act * up_value * (sigmoid_gate * (1.0 + gate_pre * (1.0 - sigmoid_gate)))
    ).astype(bf16)
    grad_up_value = (grad_act * silu_gate).astype(bf16)
    grad_normed_two = plane_reduce(
        (
            times_transposed(grad_gate_pre, w_gate_cols) + times_transposed(grad_up_value, w_up_cols)
        )
        .astype(bf16)
        .reshape(C, tokens, width)
    )
    grad_down = transposed_times(activated, grad_low).astype(bf16)
    grad_gate_up = transposed_times(
        normed_two, jnp.concatenate([grad_gate_pre, grad_up_value], axis=1)
    ).astype(bf16)
    shard_down = lax.psum_scatter(grad_down, "fsdp", scatter_dimension=0, tiled=True)
    shard_gate_up = lax.psum_scatter(grad_gate_up, "fsdp", scatter_dimension=0, tiled=True)
    back_two, grad_gain_two = norm_back(grad_normed_two, middle, scale_two, gain_two)
    grad_middle = grad_output + back_two

    m_low = plane_blocks(grad_middle.astype(bf16)).reshape(seq, width)
    grad_attended = times_transposed(m_low, w_out_rows).astype(bf16)
    grad_out = transposed_times(attended_plane, m_low).astype(bf16)
    grad_attended = reorder(grad_attended.reshape(C, tokens, q_cols), plane_order).reshape(
        seq, kv_heads, group, HEAD_DIM
    )
    row_delta = jnp.einsum("qhgd,qhgd->hgq", grad_attended.astype(f32), attended)
    grad_probs = jnp.einsum(
        "qhgd,khd->hgqk", grad_attended, values, preferred_element_type=f32
    )
    grad_scores = (probs * (grad_probs - row_delta[..., None])).astype(bf16)
    grad_values = jnp.einsum(
        "hgqk,qhgd->khd", probs_low, grad_attended, preferred_element_type=f32
    )
    grad_queries = scale_attn * jnp.einsum(
        "hgqk,khd->qhgd", grad_scores, keys, preferred_element_type=f32
    )
    grad_keys = scale_attn * jnp.einsum(
        "hgqk,qhgd->khd", grad_scores, queries, preferred_element_type=f32
    )
    grad_qkv = jnp.concatenate(
        [
            rotate(grad_queries.reshape(seq, q_heads, HEAD_DIM), cosines, -sines)
            .astype(bf16)
            .reshape(seq, q_cols),
            rotate(grad_keys, cosines, -sines).astype(bf16).reshape(seq, kv_cols),
            grad_values.astype(bf16).reshape(seq, kv_cols),
        ],
        axis=1,
    )
    grad_qkv = to_plane(grad_qkv).reshape(seq, q_cols + 2 * kv_cols)
    grad_w_qkv = transposed_times(normed_all, grad_qkv).astype(bf16)
    grad_normed_one = line_columns(
        plane_reduce(times_transposed(grad_qkv, w_qkv).astype(bf16).reshape(C, tokens, width))
    )
    back_one, grad_gain_one = norm_back(grad_normed_one, hidden_in, scale_one, gain_one)
    grad_hidden = grad_middle + back_one

    shard_qkv = line_reduce(grad_w_qkv.reshape(Z, rows_z, q_cols + 2 * kv_cols)).astype(bf16)
    out_parts = reorder(grad_out.reshape(q_cols, C, out_cols).transpose(1, 0, 2), plane_order)
    out_parts = jnp.stack([out_parts[0]] + [partner(out_parts[i], "ctx", i) for i in range(1, C)])
    out_parts = reorder(out_parts, plane_order).reshape(Z, rows_z, out_cols)
    shard_out = line_reduce(reorder(out_parts, line_order)).astype(bf16)

    ffn_all = reorder(
        plane_blocks(
            jnp.concatenate([shard_gate_up.reshape(-1), shard_down.reshape(-1)]).reshape(-1, width)
        ),
        plane_order,
    ).reshape(C, -1)
    cut = 2 * rows_z * ff_own
    gate_up_all = ffn_all[:, :cut].reshape(C, rows_z, 2, Z, ff_piece)
    gate_up_all = gate_up_all.transpose(2, 1, 3, 0, 4).reshape(2, rows_z, ff).astype(f32)
    down_all = ffn_all[:, cut:].reshape(C * ff_piece, width).astype(f32)
    attn_all = reorder(plane_blocks(jnp.concatenate([shard_qkv, shard_out], axis=1)), plane_order)
    attn_all = attn_all.astype(f32).transpose(1, 0, 2)
    final_query = attn_all[:, :, :q_cols].reshape(rows_z, width)

    def kv_final(start):
        part = attn_all[:, :, start : start + kv_cols]
        part = part.reshape(rows_z, C // kv_copies, kv_copies, kv_cols)
        return jnp.sum(part, axis=2).reshape(rows_z, KV_HEADS * HEAD_DIM)

    final_key = kv_final(q_cols)
    final_value = kv_final(q_cols + kv_cols)
    final_out = attn_all[:, :, q_cols + 2 * kv_cols :].reshape(rows_z, width)

    def gain_final(grad):
        whole = butterfly(grad.reshape(Z, rows_z), "ctx")
        return line_reduce(reorder(whole, line_order))

    return (
        output[None],
        loss_value,
        grad_hidden[None],
        final_query,
        final_key,
        final_value,
        final_out,
        gate_up_all[0],
        gate_up_all[1],
        down_all,
        gain_final(grad_gain_one),
        gain_final(grad_gain_two),
    )


def solution(mesh):
    return jax.shard_map(
        local,
        mesh=mesh,
        in_specs=(
            P("fsdp", "ctx", None),
            P("fsdp", "ctx", None),
            P("fsdp"),
            P("fsdp", None),
            P("fsdp", None),
            P("fsdp", None),
            P("fsdp", None),
            P("fsdp", None),
            P("fsdp", None),
            P("fsdp", None),
            P("fsdp"),
            P("fsdp"),
        ),
        out_specs=(
            P("fsdp", "ctx", None),
            P(),
            P("fsdp", "ctx", None),
            P("fsdp", None),
            P("fsdp", None),
            P("fsdp", None),
            P("fsdp", None),
            P("fsdp", None),
            P("fsdp", None),
            P("fsdp", None),
            P("fsdp"),
            P("fsdp"),
        ),
        check_vma=False,
    )
```

```python
import functools

import jax
import jax.numpy as jnp
from jax import lax
from jax.experimental import pallas as pl
from jax.experimental.pallas import tpu as pltpu
from jax.sharding import PartitionSpec as P

HEADS = 16
KV_HEADS = 8
HEAD_DIM = 96
LANES = 128

eps_norm = 1e-05
rope_base = 100000.0
masked_value = -1e30

f32 = jnp.float32
bf16 = jnp.bfloat16

VMEM = pl.BlockSpec(memory_space=pltpu.VMEM)
SMEM = pl.BlockSpec(memory_space=pltpu.SMEM)
ANY = pl.BlockSpec(memory_space=pl.ANY)
KERNEL_VMEM = 56 * 1024 * 1024


def times(left, right):
    return jnp.dot(left, right, preferred_element_type=f32)


def times_transposed(left, right):
    return lax.dot_general(left, right, (((1,), (1,)), ((), ())), preferred_element_type=f32)


def transposed_times(left, right):
    return lax.dot_general(left, right, (((0,), (0,)), ((), ())), preferred_element_type=f32)


def norm_scale(features):
    return lax.rsqrt(jnp.mean(features * features, axis=-1, keepdims=True) + eps_norm)


def norm_back(upstream, features, row_scale, gain_vector):
    weighted = upstream * gain_vector
    inner_mean = jnp.mean(weighted * features, axis=-1, keepdims=True)
    grad_rows = row_scale * weighted - features * (row_scale * row_scale * row_scale) * inner_mean
    return (grad_rows, jnp.sum(upstream * (features * row_scale), axis=0))


def partner(x, axis, mask):
    return lax.ppermute(x, axis, [(i, i ^ mask) for i in range(lax.axis_size(axis))])


def plane_blocks(x):
    blocks = []
    for s in range(lax.axis_size("ctx") // 2):
        mine = partner(x, "ctx", 2 * s) if s else x
        blocks += [mine, partner(mine, "ctx", 1)]
    return blocks


def plane_reduce(keep, give):
    sent = []
    for s in range(len(keep) - 1, 0, -1):
        chip = keep[s].astype(f32) + partner(give[s], "ctx", 1).astype(f32)
        sent.append(partner(chip.astype(bf16), "ctx", 2 * s))
    total = keep[0].astype(f32) + partner(give[0], "ctx", 1).astype(f32)
    for got in sent:
        total = total + got.astype(f32)
    return total


def tree_sum(x, axis):
    mask = 1
    while mask < lax.axis_size(axis):
        x = x + partner(x, axis, mask)
        mask *= 2
    return x


def line_blocks(x):
    return [x] + [partner(x, "fsdp", s) for s in range(1, lax.axis_size("fsdp"))]


def line_reduce(parts):
    total = parts[0].astype(f32)
    for s in range(1, len(parts)):
        total = total + partner(parts[s], "fsdp", s).astype(f32)
    return total


def pick(x, index, axis=0):
    return lax.dynamic_index_in_dim(x, index, axis, False)


def unsort(blocks, me):
    stacked = jnp.stack(blocks)
    return [pick(stacked, me ^ b) for b in range(len(blocks))]


def rope_tables(count):
    half_dim = HEAD_DIM // 2
    frequencies = rope_base ** (-(jnp.arange(half_dim, dtype=f32) * 2.0) / HEAD_DIM)
    angles = jnp.arange(count, dtype=f32)[:, None] * frequencies[None, :]
    cosines, sines = jnp.cos(angles), jnp.sin(angles)
    pad = jnp.zeros((count, LANES - HEAD_DIM), f32)
    return (
        jnp.concatenate([cosines, cosines, pad], axis=1),
        jnp.concatenate([-sines, sines, pad], axis=1),
    )


def turned(x):
    lane = lax.broadcasted_iota(jnp.int32, x.shape, 1)
    half_dim = HEAD_DIM // 2
    return jnp.where(
        lane < half_dim, pltpu.roll(x, LANES - half_dim, 1), pltpu.roll(x, half_dim, 1)
    )


def head_of(x, head):
    if head:
        x = pltpu.roll(x, x.shape[1] - head * HEAD_DIM, 1)
    return x[:, :LANES]


def packed(heads):
    wide = -(-len(heads) * HEAD_DIM // LANES) * LANES
    total = None
    for index, head in enumerate(heads):
        if wide > LANES:
            head = jnp.concatenate([head, jnp.zeros((head.shape[0], wide - LANES), f32)], axis=1)
        if index:
            head = pltpu.roll(head, index * HEAD_DIM, 1)
        total = head if total is None else total + head
    return total


def attention_forward_kernel(C, tokens, q_heads, kv_heads, block, info_ref, *refs):
    n_refs = refs[:C]
    w_ref, cos_ref, sin_ref = refs[C : C + 3]
    n_all_ref, qkv_ref, att_ref, lse_ref = refs[C + 3 : C + 7]
    keep_refs = refs[C + 7 : C + 7 + C // 2]
    give_refs = refs[C + 7 + C // 2 : C + 7 + C]
    lin_ref = refs[C + 7 + C]
    me, length = info_ref[0], info_ref[1]
    seq = C * tokens
    group = q_heads // kv_heads
    width_low = q_heads * HEAD_DIM
    for i in range(C):
        n_all_ref[i * tokens : (i + 1) * tokens, :] = n_refs[i][...]
    step = 4 * tokens
    for start in range(0, seq, step):
        lin_ref[start : start + step, :] = times(n_all_ref[start : start + step, :], w_ref[...])
    lane = lax.broadcasted_iota(jnp.int32, (tokens, LANES), 1)
    for i in range(C):
        rows = pl.ds(pl.multiple_of((me ^ i) * tokens, tokens), tokens)
        lin = lin_ref[i * tokens : (i + 1) * tokens, :]
        cosines, sines = cos_ref[rows, :], sin_ref[rows, :]
        for head in range(q_heads + 2 * kv_heads):
            x = head_of(lin, head)
            if head < q_heads + kv_heads:
                x = x * cosines + turned(x) * sines
            else:
                x = jnp.where(lane < HEAD_DIM, x, 0.0)
            qkv_ref[rows, head * LANES : (head + 1) * LANES] = x.astype(bf16)
    scale = HEAD_DIM ** (-0.5)
    for head in range(q_heads):
        k_at = (q_heads + head // group) * LANES
        v_at = k_at + kv_heads * LANES
        for start in range(0, seq, block):
            end = start + block
            q = qkv_ref[start:end, head * LANES : (head + 1) * LANES]
            scores = times_transposed(q, qkv_ref[:end, k_at : k_at + LANES]) * scale
            row = start + lax.broadcasted_iota(jnp.int32, (block, end), 0)
            col = lax.broadcasted_iota(jnp.int32, (block, end), 1)
            scores = jnp.where((col <= row) & (col < length), scores, masked_value)
            row_max = jnp.max(scores, axis=1, keepdims=True)
            weights = jnp.exp(scores - row_max)
            row_sum = jnp.sum(weights, axis=1, keepdims=True)
            probs = (weights * (1.0 / row_sum)).astype(bf16)
            att_ref[start:end, head * LANES : (head + 1) * LANES] = times(
                probs, qkv_ref[:end, v_at : v_at + LANES]
            )
            lse_ref[start:end, head : head + 1] = row_max + jnp.log(row_sum)
    for i in range(C):
        rows = pl.ds(pl.multiple_of((me ^ i) * tokens, tokens), tokens)
        x = att_ref[rows, :]
        low = packed([x[:, h * LANES : (h + 1) * LANES] for h in range(q_heads)])
        (give_refs if i % 2 else keep_refs)[i // 2][...] = low[:, :width_low].astype(bf16)


def attention_forward(blocks, w_qkv, tables, me, length, q_heads, kv_heads):
    C = len(blocks)
    tokens, width = blocks[0].shape
    seq = C * tokens
    heads = q_heads + 2 * kv_heads
    part = jax.ShapeDtypeStruct((tokens, q_heads * HEAD_DIM), bf16)
    result = pl.pallas_call(
        functools.partial(attention_forward_kernel, C, tokens, q_heads, kv_heads, 2 * tokens),
        out_shape=[
            jax.ShapeDtypeStruct((seq, width), bf16),
            jax.ShapeDtypeStruct((seq, heads * LANES), bf16),
            jax.ShapeDtypeStruct((seq, q_heads * LANES), f32),
            jax.ShapeDtypeStruct((seq, LANES), f32),
        ]
        + [part] * C,
        in_specs=[SMEM] + [VMEM] * (C + 3),
        out_specs=[VMEM] * (C + 4),
        scratch_shapes=[pltpu.VMEM((seq, w_qkv.shape[1]), f32)],
        compiler_params=pltpu.CompilerParams(vmem_limit_bytes=KERNEL_VMEM),
        name="attention_forward",
    )(jnp.stack([me, length]).astype(jnp.int32), *blocks, w_qkv, *tables)
    return result[:4], result[4 : 4 + C // 2], result[4 + C // 2 :]


def attention_backward_kernel(C, tokens, q_heads, kv_heads, block, info_ref, *refs):
    grad_refs = refs[:C]
    qkv_ref, att_ref, lse_ref, w_ref, cos_ref, sin_ref = refs[C : C + 6]
    dqkv_ref = refs[C + 6]
    keep_refs = refs[C + 7 : C + 7 + C // 2]
    give_refs = refs[C + 7 + C // 2 : C + 7 + C]
    wide_ref, grad_ref, dq_ref, dkv_ref = refs[C + 7 + C :]
    me, length = info_ref[0], info_ref[1]
    seq = C * tokens
    group = q_heads // kv_heads
    width_low = q_heads * HEAD_DIM
    lane = lax.broadcasted_iota(jnp.int32, (tokens, LANES), 1)
    wide_ref[...] = jnp.zeros_like(wide_ref)
    for i in range(C):
        rows = pl.ds(pl.multiple_of((me ^ i) * tokens, tokens), tokens)
        wide_ref[:, :width_low] = grad_refs[i][...].astype(f32)
        wide = wide_ref[...]
        for head in range(q_heads):
            x = jnp.where(lane < HEAD_DIM, head_of(wide, head), 0.0)
            grad_ref[rows, head * LANES : (head + 1) * LANES] = x.astype(bf16)
    dkv_ref[...] = jnp.zeros_like(dkv_ref)
    scale = HEAD_DIM ** (-0.5)
    for start in range(0, seq, block):
        end = start + block
        lane_b = lax.broadcasted_iota(jnp.int32, (block, LANES), 1)
        delta = jnp.zeros((block, LANES), f32)
        for head in range(q_heads):
            at = slice(head * LANES, (head + 1) * LANES)
            one = jnp.sum(
                grad_ref[start:end, at].astype(f32) * att_ref[start:end, at], axis=1, keepdims=True
            )
            delta = jnp.where(lane_b == head, one, delta)
        delta_t = delta.T
        lse_t = lse_ref[start:end, :].T
        key = lax.broadcasted_iota(jnp.int32, (end, block), 0)
        query = start + lax.broadcasted_iota(jnp.int32, (end, block), 1)
        allowed = (key <= query) & (key < length)
        for head in range(q_heads):
            at = slice(head * LANES, (head + 1) * LANES)
            kv = head // group
            k_at = slice((q_heads + kv) * LANES, (q_heads + kv + 1) * LANES)
            v_at = slice((q_heads + kv_heads + kv) * LANES, (q_heads + kv_heads + kv + 1) * LANES)
            q, grad = qkv_ref[start:end, at], grad_ref[start:end, at]
            k, v = qkv_ref[:end, k_at], qkv_ref[:end, v_at]
            scores = times_transposed(k, q) * scale
            probs = jnp.where(allowed, jnp.exp(scores - lse_t[head : head + 1, :]), 0.0)
            grad_probs = times_transposed(v, grad)
            grad_scores = (probs * (grad_probs - delta_t[head : head + 1, :])).astype(bf16)
            dq_ref[start:end, at] = transposed_times(grad_scores, k) * scale
            dk_at = slice(kv * LANES, (kv + 1) * LANES)
            dv_at = slice((kv_heads + kv) * LANES, (kv_heads + kv + 1) * LANES)
            dkv_ref[:end, dk_at] += times(grad_scores, q) * scale
            dkv_ref[:end, dv_at] += times(probs.astype(bf16), grad)
    for i in range(C):
        rows = pl.ds(pl.multiple_of((me ^ i) * tokens, tokens), tokens)
        cosines, sines = cos_ref[rows, :], sin_ref[rows, :]
        heads = []
        for head in range(q_heads + 2 * kv_heads):
            if head < q_heads:
                x = dq_ref[rows, head * LANES : (head + 1) * LANES]
            else:
                x = dkv_ref[rows, (head - q_heads) * LANES : (head - q_heads + 1) * LANES]
            if head < q_heads + kv_heads:
                x = x * cosines - turned(x) * sines
            heads.append(x)
        dqkv_ref[i * tokens : (i + 1) * tokens, :] = packed(heads).astype(bf16)
    step = 4
    for first in range(0, C, step):
        part = times_transposed(dqkv_ref[first * tokens : (first + step) * tokens, :], w_ref[...])
        for i in range(first, first + step):
            at = (i - first) * tokens
            (give_refs if i % 2 else keep_refs)[i // 2][...] = part[at : at + tokens, :].astype(bf16)


def attention_backward(grads, saved, w_qkv, tables, me, length, q_heads, kv_heads):
    C = len(grads)
    tokens = grads[0].shape[0]
    seq = C * tokens
    width, cols = w_qkv.shape
    part = jax.ShapeDtypeStruct((tokens, width), bf16)
    wide = -(-q_heads * HEAD_DIM // LANES) * LANES
    result = pl.pallas_call(
        functools.partial(attention_backward_kernel, C, tokens, q_heads, kv_heads, 2 * tokens),
        out_shape=[jax.ShapeDtypeStruct((seq, cols), bf16)] + [part] * C,
        in_specs=[SMEM] + [VMEM] * (C + 6),
        out_specs=[VMEM] * (C + 1),
        scratch_shapes=[
            pltpu.VMEM((tokens, wide), f32),
            pltpu.VMEM((seq, q_heads * LANES), bf16),
            pltpu.VMEM((seq, q_heads * LANES), f32),
            pltpu.VMEM((seq, 2 * kv_heads * LANES), f32),
        ],
        compiler_params=pltpu.CompilerParams(vmem_limit_bytes=KERNEL_VMEM),
        name="attention_backward",
    )(jnp.stack([me, length]).astype(jnp.int32), *grads, *saved, w_qkv, *tables)
    return result[0], result[1 : 1 + C // 2], result[1 + C // 2 :]


def ffn_forward_kernel(C, tokens, *refs):
    n_refs = refs[:C]
    gu_ref, down_ref = refs[C : C + 2]
    n_all_ref, act_ref, coef_ref = refs[C + 2 : C + 5]
    keep_refs = refs[C + 5 : C + 5 + C // 2]
    give_refs = refs[C + 5 + C // 2 :]
    own = down_ref.shape[0]
    for i in range(C):
        n_all_ref[i * tokens : (i + 1) * tokens, :] = n_refs[i][...]
    step = 4
    for first in range(0, C, step):
        rows = slice(first * tokens, (first + step) * tokens)
        both = times(n_all_ref[rows, :], gu_ref[...])
        gate, up = both[:, :own], both[:, own:]
        sigmoid = jax.nn.sigmoid(gate)
        silu = gate * sigmoid
        act = (silu * up).astype(bf16)
        act_ref[rows, :] = act
        coef_ref[rows, :own] = (up * (sigmoid * (1.0 + gate * (1.0 - sigmoid)))).astype(bf16)
        coef_ref[rows, own:] = silu.astype(bf16)
        part = times(act, down_ref[...])
        for i in range(first, first + step):
            at = (i - first) * tokens
            (give_refs if i % 2 else keep_refs)[i // 2][...] = part[at : at + tokens, :].astype(bf16)


def ffn_forward(blocks, gate_up, down):
    C = len(blocks)
    tokens, width = blocks[0].shape
    seq, own = C * tokens, down.shape[0]
    part = jax.ShapeDtypeStruct((tokens, width), bf16)
    result = pl.pallas_call(
        functools.partial(ffn_forward_kernel, C, tokens),
        out_shape=[
            jax.ShapeDtypeStruct((seq, width), bf16),
            jax.ShapeDtypeStruct((seq, own), bf16),
            jax.ShapeDtypeStruct((seq, 2 * own), bf16),
        ]
        + [part] * C,
        in_specs=[VMEM] * (C + 2),
        out_specs=[VMEM] * (C + 3),
        compiler_params=pltpu.CompilerParams(vmem_limit_bytes=KERNEL_VMEM),
        name="ffn_forward",
    )(*blocks, gate_up, down)
    return result[:3], result[3 : 3 + C // 2], result[3 + C // 2 :]


def ffn_backward_kernel(C, tokens, *refs):
    g_refs = refs[:C]
    gu_ref, down_ref, coef_ref = refs[C : C + 3]
    g_all_ref, dgu_ref = refs[C + 3 : C + 5]
    keep_refs = refs[C + 5 : C + 5 + C // 2]
    give_refs = refs[C + 5 + C // 2 :]
    own = down_ref.shape[0]
    for i in range(C):
        g_all_ref[i * tokens : (i + 1) * tokens, :] = g_refs[i][...]
    step = 4
    for first in range(0, C, step):
        rows = slice(first * tokens, (first + step) * tokens)
        grad_act = times_transposed(g_all_ref[rows, :], down_ref[...])
        dgu_ref[rows, :own] = (grad_act * coef_ref[rows, :own].astype(f32)).astype(bf16)
        dgu_ref[rows, own:] = (grad_act * coef_ref[rows, own:].astype(f32)).astype(bf16)
        part = times_transposed(dgu_ref[rows, :], gu_ref[...])
        for i in range(first, first + step):
            at = (i - first) * tokens
            (give_refs if i % 2 else keep_refs)[i // 2][...] = part[at : at + tokens, :].astype(bf16)


def ffn_backward(blocks, gate_up, down, coef):
    C = len(blocks)
    tokens, width = blocks[0].shape
    seq, own = C * tokens, down.shape[0]
    part = jax.ShapeDtypeStruct((tokens, width), bf16)
    result = pl.pallas_call(
        functools.partial(ffn_backward_kernel, C, tokens),
        out_shape=[
            jax.ShapeDtypeStruct((seq, width), bf16),
            jax.ShapeDtypeStruct((seq, 2 * own), bf16),
        ]
        + [part] * C,
        in_specs=[VMEM] * (C + 3),
        out_specs=[VMEM] * (C + 2),
        compiler_params=pltpu.CompilerParams(vmem_limit_bytes=KERNEL_VMEM),
        name="ffn_backward",
    )(*blocks, gate_up, down, coef)
    return result[:2], result[2 : 2 + C // 2], result[2 + C // 2 :]


def ffn_slices_kernel(Z, piece, me_ref, gate_ref, up_ref, down_ref, gu_ref, rows_ref, sems):
    me = me_ref[0]
    stride = gate_ref.shape[1] // Z
    copies = []
    for a, ref in enumerate((gate_ref, up_ref)):
        for zz in range(Z):
            at = pl.multiple_of(zz * stride + me * piece, piece)
            copies.append((ref.at[:, pl.ds(at, piece)], gu_ref.at[:, pl.ds((a * Z + zz) * piece, piece)]))
    at = pl.multiple_of(me * piece, piece)
    copies.append((down_ref.at[pl.ds(at, piece), :], rows_ref))
    copies = [pltpu.make_async_copy(a, b, sems.at[n]) for n, (a, b) in enumerate(copies)]
    for copy in copies:
        copy.start()
    for copy in copies:
        copy.wait()


def ffn_slices(w_gate, w_up, w_down, me, C, Z):
    rows, ff = w_gate.shape
    piece = ff // (Z * C)
    if piece % LANES:
        cut = [pick(w.reshape(rows, Z, C, piece), me, 2).reshape(rows, -1) for w in (w_gate, w_up)]
        return jnp.concatenate(cut, axis=1), lax.dynamic_slice_in_dim(w_down, me * piece, piece, 0)
    return pl.pallas_call(
        functools.partial(ffn_slices_kernel, Z, piece),
        out_shape=[
            jax.ShapeDtypeStruct((rows, 2 * Z * piece), bf16),
            jax.ShapeDtypeStruct((piece, w_down.shape[1]), bf16),
        ],
        in_specs=[SMEM, ANY, ANY, ANY],
        out_specs=[ANY, ANY],
        scratch_shapes=[pltpu.SemaphoreType.DMA((2 * Z + 1,))],
        name="ffn_slices",
    )(me.reshape(1), w_gate, w_up, w_down)


def ffn_grads_kernel(C, Z, piece, me_ref, *refs):
    gu_refs, rows_refs = refs[:C], refs[C : 2 * C]
    gate_ref, up_ref, down_ref, wide_ref, tall_ref, sems = refs[2 * C :]
    me = me_ref[0]
    stride = gate_ref.shape[1] // Z
    flying = [None, None]
    for i in range(C):
        slot = i % 2
        for copy in flying[slot] or ():
            copy.wait()
        owner = me ^ i
        wide_ref[slot] = gu_refs[i][...].astype(f32)
        tall_ref[slot] = rows_refs[i][...].astype(f32)
        copies = []
        for a, ref in enumerate((gate_ref, up_ref)):
            for zz in range(Z):
                at = pl.multiple_of(zz * stride + owner * piece, piece)
                copies.append(
                    pltpu.make_async_copy(
                        wide_ref.at[slot, :, pl.ds((a * Z + zz) * piece, piece)],
                        ref.at[:, pl.ds(at, piece)],
                        sems.at[slot, a * Z + zz],
                    )
                )
        at = pl.multiple_of(owner * piece, piece)
        copies.append(
            pltpu.make_async_copy(
                tall_ref.at[slot], down_ref.at[pl.ds(at, piece), :], sems.at[slot, 2 * Z]
            )
        )
        for copy in copies:
            copy.start()
        flying[slot] = copies
    for copies in flying:
        for copy in copies or ():
            copy.wait()


def ffn_grads(gu_blocks, row_blocks, me, Z):
    C = len(gu_blocks)
    rows, cols = gu_blocks[0].shape
    piece, width = row_blocks[0].shape
    ff = C * cols // 2
    if piece % LANES:
        gu = jnp.stack(unsort(gu_blocks, me)).astype(f32).reshape(C, rows, 2, Z, piece)
        gu = gu.transpose(2, 1, 3, 0, 4).reshape(2, rows, ff)
        return gu[0], gu[1], jnp.concatenate(unsort(row_blocks, me), axis=0).astype(f32)
    return pl.pallas_call(
        functools.partial(ffn_grads_kernel, C, Z, piece),
        out_shape=[
            jax.ShapeDtypeStruct((rows, ff), f32),
            jax.ShapeDtypeStruct((rows, ff), f32),
            jax.ShapeDtypeStruct((C * piece, width), f32),
        ],
        in_specs=[SMEM] + [VMEM] * (2 * C),
        out_specs=[ANY] * 3,
        scratch_shapes=[
            pltpu.VMEM((2, rows, cols), f32),
            pltpu.VMEM((2, piece, width), f32),
            pltpu.SemaphoreType.DMA((2, 2 * Z + 1)),
        ],
        compiler_params=pltpu.CompilerParams(vmem_limit_bytes=KERNEL_VMEM),
        name="ffn_grads",
    )(me.reshape(1), *gu_blocks, *row_blocks)


def local(
    inputs,
    teacher,
    lengths,
    w_query,
    w_key,
    w_value,
    w_out,
    w_gate,
    w_up,
    w_down,
    gain_attn,
    gain_ffn,
):
    hidden_in = inputs[0]
    target = teacher[0]
    seq_length = lengths[0]
    tokens, width = hidden_in.shape
    C = lax.axis_size("ctx")
    Z = lax.axis_size("fsdp")
    R = C // 2
    p = lax.axis_index("ctx")
    z = lax.axis_index("fsdp")
    chip, core = p // 2, p % 2
    rows_z = width // Z
    seq = C * tokens
    q_heads = HEADS // C
    kv_heads = max(1, KV_HEADS // C)
    kv_copies = max(1, C // KV_HEADS)
    q_cols = q_heads * HEAD_DIM
    kv_cols = kv_heads * HEAD_DIM
    qkv_cols = q_cols + 2 * kv_cols
    positions = p * tokens + jnp.arange(tokens, dtype=jnp.int32)

    def line_columns(x):
        cut = x.reshape(x.shape[0], Z, rows_z)
        return jnp.concatenate([pick(cut, z ^ i, 1) for i in range(Z)], axis=1)

    gains = jnp.stack(unsort(line_blocks(jnp.stack([gain_attn, gain_ffn])), z))
    gain_one = gains[:, 0].reshape(width).astype(f32)
    gain_two = gains[:, 1].reshape(width).astype(f32)
    gate_up_own, down_own = ffn_slices(w_gate, w_up, w_down, p, C, Z)
    gate_up = lax.all_gather(gate_up_own, "fsdp", axis=0, tiled=True)
    down_rows = lax.all_gather(down_own, "fsdp", axis=0, tiled=True)
    kv_start = (p * KV_HEADS // C) * HEAD_DIM
    qkv_own = jnp.concatenate(
        [
            lax.dynamic_slice_in_dim(w_query, p * q_cols, q_cols, 1),
            lax.dynamic_slice_in_dim(w_key, kv_start, kv_cols, 1),
            lax.dynamic_slice_in_dim(w_value, kv_start, kv_cols, 1),
            jnp.zeros((rows_z, -qkv_cols % LANES), bf16),
        ],
        axis=1,
    )
    w_qkv = jnp.concatenate(line_blocks(qkv_own), axis=0)

    scale_one = norm_scale(hidden_in)
    normed_one = (hidden_in * scale_one * gain_one).astype(bf16)
    normed_blocks = plane_blocks(line_columns(normed_one))
    tables = rope_tables(seq)
    (normed_all, qkv, attended, lse), att_keep, att_give = attention_forward(
        normed_blocks, w_qkv, tables, p, seq_length, q_heads, kv_heads
    )

    out_piece = rows_z // C
    out_own = lax.dynamic_slice_in_dim(w_out, p * out_piece, out_piece, 0)
    out_line = jnp.stack(unsort(line_blocks(out_own), z))
    out_all = jnp.stack(unsort(plane_blocks(out_line), p), axis=1).reshape(width, width)
    valid_count = tree_sum(lengths.astype(f32), "fsdp")[0]

    def heads_of_chip(own, other):
        return jnp.where(
            core == 0,
            jnp.concatenate([own, other], axis=1),
            jnp.concatenate([other, own], axis=1),
        )

    pairs = []
    for s in range(R):
        pair = heads_of_chip(att_keep[s], partner(att_give[s], "ctx", 1))
        pairs.append(partner(pair, "ctx", 2 * s) if s else pair)
    attended_tokens = jnp.concatenate(unsort(pairs, chip), axis=1)
    middle = hidden_in + times(attended_tokens, out_all)

    scale_two = norm_scale(middle)
    normed_two_blocks = plane_blocks((middle * scale_two * gain_two).astype(bf16))
    (normed_two, activated, coef), keep, give = ffn_forward(normed_two_blocks, gate_up, down_rows)
    output = middle + plane_reduce(keep, give)

    valid_rows = (positions < seq_length).astype(f32)
    residual_error = output - target
    squares = jnp.sum(valid_rows[:, None] * residual_error * residual_error)
    grad_output = valid_rows[:, None] * (2.0 * residual_error) / valid_count

    grad_blocks = plane_blocks(grad_output.astype(bf16))
    (grad_low, grad_gu), keep, give = ffn_backward(grad_blocks, gate_up, down_rows, coef)
    grad_normed_two = plane_reduce(keep, give)
    grad_down = transposed_times(activated, grad_low).astype(bf16)
    grad_gate_up = transposed_times(normed_two, grad_gu).astype(bf16)
    shard_down = lax.psum_scatter(grad_down, "fsdp", scatter_dimension=0, tiled=True)
    shard_gate_up = lax.psum_scatter(grad_gate_up, "fsdp", scatter_dimension=0, tiled=True)
    back_two, grad_gain_two = norm_back(grad_normed_two, middle, scale_two, gain_two)
    grad_middle = grad_output + back_two

    m_low = grad_middle.astype(bf16)
    grad_attended = times_transposed(m_low, out_all).astype(bf16)
    cut = grad_attended.reshape(tokens, R, 2 * q_cols)
    blocks = []
    for s in range(R):
        pair = pick(cut, chip ^ s, 1)
        pair = partner(pair, "ctx", 2 * s) if s else pair
        own = jnp.where(core == 0, pair[:, :q_cols], pair[:, q_cols:])
        other = jnp.where(core == 0, pair[:, q_cols:], pair[:, :q_cols])
        blocks += [own, partner(other, "ctx", 1)]
    grad_qkv, keep, give = attention_backward(
        blocks, (qkv, attended, lse), w_qkv, tables, p, seq_length, q_heads, kv_heads
    )
    grad_normed_one = line_columns(plane_reduce(keep, give))
    back_one, grad_gain_one = norm_back(grad_normed_one, hidden_in, scale_one, gain_one)
    grad_hidden = grad_middle + back_one

    grad_out = transposed_times(attended_tokens, m_low).astype(bf16).reshape(Z, C, out_piece, width)
    grad_out = [pick(grad_out, p ^ i, 1).reshape(Z * out_piece, width) for i in range(C)]
    grad_out = plane_reduce(grad_out[0::2], grad_out[1::2]).astype(bf16)
    grad_out = grad_out.reshape(Z, out_piece, width)
    shard_out = line_reduce([pick(grad_out, z ^ i) for i in range(Z)]).astype(bf16)
    grad_w_qkv = transposed_times(normed_all, grad_qkv).astype(bf16)
    shard_qkv = line_reduce(
        [grad_w_qkv[i * rows_z : (i + 1) * rows_z] for i in range(Z)]
    ).astype(bf16)

    final_gate, final_up, final_down = ffn_grads(
        plane_blocks(shard_gate_up), plane_blocks(shard_down), p, Z
    )
    final_out = jnp.concatenate(unsort(plane_blocks(shard_out), p), axis=0).astype(f32)
    qkv_all = unsort(plane_blocks(shard_qkv), p)
    final_query = jnp.concatenate([part[:, :q_cols] for part in qkv_all], axis=1).astype(f32)

    def kv_final(start):
        parts = [part[:, start : start + kv_cols].astype(f32) for part in qkv_all]
        parts = [sum(parts[n : n + kv_copies]) for n in range(0, C, kv_copies)]
        return jnp.concatenate(parts, axis=1)

    final_key = kv_final(q_cols)
    final_value = kv_final(q_cols + kv_cols)

    loss_value = tree_sum(tree_sum(squares.reshape(1), "ctx"), "fsdp")[0] / valid_count

    def gain_final(grad):
        whole = tree_sum(grad.reshape(Z, rows_z), "ctx")
        return line_reduce([pick(whole, z ^ i) for i in range(Z)])

    return (
        output[None],
        loss_value,
        grad_hidden[None],
        final_query,
        final_key,
        final_value,
        final_out,
        final_gate,
        final_up,
        final_down,
        gain_final(grad_gain_one),
        gain_final(grad_gain_two),
    )


def solution(mesh):
    return jax.shard_map(
        local,
        mesh=mesh,
        in_specs=(
            P("fsdp", "ctx", None),
            P("fsdp", "ctx", None),
            P("fsdp"),
            P("fsdp", None),
            P("fsdp", None),
            P("fsdp", None),
            P("fsdp", None),
            P("fsdp", None),
            P("fsdp", None),
            P("fsdp", None),
            P("fsdp"),
            P("fsdp"),
        ),
        out_specs=(
            P("fsdp", "ctx", None),
            P(),
            P("fsdp", "ctx", None),
            P("fsdp", None),
            P("fsdp", None),
            P("fsdp", None),
            P("fsdp", None),
            P("fsdp", None),
            P("fsdp", None),
            P("fsdp", None),
            P("fsdp"),
            P("fsdp"),
        ),
        check_vma=False,
    )
```

```python
import functools

import jax
import jax.numpy as jnp
from jax import lax
from jax.experimental import pallas as pl
from jax.experimental.pallas import tpu as pltpu
from jax.sharding import PartitionSpec as P

HEADS = 16
KV_HEADS = 8
HEAD_DIM = 96
LANES = 128

eps_norm = 1e-05
rope_base = 100000.0
masked_value = -1e30

f32 = jnp.float32
bf16 = jnp.bfloat16

VMEM = pl.BlockSpec(memory_space=pltpu.VMEM)
SMEM = pl.BlockSpec(memory_space=pltpu.SMEM)
ANY = pl.BlockSpec(memory_space=pl.ANY)
KERNEL_VMEM = 16 * 1024 * 1024


def cost(multiply_adds, values):
    return pl.CostEstimate(flops=2 * multiply_adds, bytes_accessed=2 * values, transcendentals=0)


def times(left, right):
    return jnp.dot(left, right, preferred_element_type=f32)


def times_transposed(left, right):
    return lax.dot_general(left, right, (((1,), (1,)), ((), ())), preferred_element_type=f32)


def transposed_times(left, right):
    return lax.dot_general(left, right, (((0,), (0,)), ((), ())), preferred_element_type=f32)


def norm_scale(features):
    return lax.rsqrt(jnp.mean(features * features, axis=-1, keepdims=True) + eps_norm)


def norm_back(upstream, features, row_scale, gain_vector):
    weighted = upstream * gain_vector
    inner_mean = jnp.mean(weighted * features, axis=-1, keepdims=True)
    grad_rows = row_scale * weighted - features * (row_scale * row_scale * row_scale) * inner_mean
    return (grad_rows, jnp.sum(upstream * (features * row_scale), axis=0))


def partner(x, axis, mask):
    return lax.ppermute(x, axis, [(i, i ^ mask) for i in range(lax.axis_size(axis))])


def plane_sends(x):
    return [partner(x, "ctx", 2 * s) for s in range(1, lax.axis_size("ctx") // 2)]


def core_blocks(mine):
    blocks = []
    for x in mine:
        blocks += [x, partner(x, "ctx", 1)]
    return blocks


def plane_blocks(x):
    return core_blocks([x] + plane_sends(x))


def line_sends(x):
    return [partner(x, "fsdp", s) for s in range(1, lax.axis_size("fsdp"))]


def plane_reduce(keep, give):
    chips = chip_sums(keep, give)
    return total(chips[0], chip_sends(chips))


def chip_sums(keep, give):
    got = [partner(x, "ctx", 1) for x in give[::-1]][::-1]
    own = keep[0].astype(f32) + got[0].astype(f32)
    return [own] + [
        (a.astype(f32) + b.astype(f32)).astype(bf16) for a, b in zip(keep[1:], got[1:], strict=True)
    ]


def chip_sends(chips):
    return together([partner(chips[s], "ctx", 2 * s) for s in range(len(chips) - 1, 0, -1)])


def total(own, got):
    for x in got:
        own = own + x.astype(f32)
    return own


def tree_sum(x, axis):
    mask = 1
    while mask < lax.axis_size(axis):
        x = x + partner(x, axis, mask)
        mask *= 2
    return x


def line_blocks(x):
    return [x] + together(line_sends(x))


def line_reduce(parts):
    got = together([partner(parts[s], "fsdp", s) for s in range(1, len(parts))])
    return total(parts[0].astype(f32), got)


def together(xs):
    return list(lax.optimization_barrier(tuple(xs)))


def after(x, *done):
    return lax.optimization_barrier((x, done))[0]


def pick(x, index, axis=0):
    return lax.dynamic_index_in_dim(x, index, axis, False)


def unsort(blocks, me):
    stacked = jnp.stack(blocks)
    return [pick(stacked, me ^ b) for b in range(len(blocks))]


def rope_tables(count):
    half_dim = HEAD_DIM // 2
    frequencies = rope_base ** (-(jnp.arange(half_dim, dtype=f32) * 2.0) / HEAD_DIM)
    angles = jnp.arange(count, dtype=f32)[:, None] * frequencies[None, :]
    cosines, sines = jnp.cos(angles), jnp.sin(angles)
    pad = jnp.zeros((count, LANES - HEAD_DIM), f32)
    return (
        jnp.concatenate([cosines, cosines, pad], axis=1),
        jnp.concatenate([-sines, sines, pad], axis=1),
    )


def turned(x):
    lane = lax.broadcasted_iota(jnp.int32, x.shape, 1)
    half_dim = HEAD_DIM // 2
    return jnp.where(
        lane < half_dim, pltpu.roll(x, LANES - half_dim, 1), pltpu.roll(x, half_dim, 1)
    )


def head_of(x, head):
    if head:
        x = pltpu.roll(x, x.shape[1] - head * HEAD_DIM, 1)
    return x[:, :LANES]


def packed(heads):
    wide = -(-len(heads) * HEAD_DIM // LANES) * LANES
    total = None
    for index, head in enumerate(heads):
        if wide > LANES:
            head = jnp.concatenate([head, jnp.zeros((head.shape[0], wide - LANES), f32)], axis=1)
        if index:
            head = pltpu.roll(head, index * HEAD_DIM, 1)
        total = head if total is None else total + head
    return total


def attention_forward_kernel(C, tokens, q_heads, kv_heads, block, info_ref, *refs):
    n_refs = refs[:C]
    w_ref, cos_ref, sin_ref = refs[C : C + 3]
    n_all_ref, qkv_ref, att_ref, lse_ref = refs[C + 3 : C + 7]
    keep_refs = refs[C + 7 : C + 7 + C // 2]
    give_refs = refs[C + 7 + C // 2 : C + 7 + C]
    lin_ref = refs[C + 7 + C]
    me, length = info_ref[0], info_ref[1]
    seq = C * tokens
    group = q_heads // kv_heads
    width_low = q_heads * HEAD_DIM
    for i in range(C):
        n_all_ref[i * tokens : (i + 1) * tokens, :] = n_refs[i][...]
    step = 4 * tokens
    for start in range(0, seq, step):
        lin_ref[start : start + step, :] = times(n_all_ref[start : start + step, :], w_ref[...])
    lane = lax.broadcasted_iota(jnp.int32, (tokens, LANES), 1)
    for i in range(C):
        rows = pl.ds(pl.multiple_of((me ^ i) * tokens, tokens), tokens)
        lin = lin_ref[i * tokens : (i + 1) * tokens, :]
        cosines, sines = cos_ref[rows, :], sin_ref[rows, :]
        for head in range(q_heads + 2 * kv_heads):
            x = head_of(lin, head)
            if head < q_heads + kv_heads:
                x = x * cosines + turned(x) * sines
            else:
                x = jnp.where(lane < HEAD_DIM, x, 0.0)
            qkv_ref[rows, head * LANES : (head + 1) * LANES] = x.astype(bf16)
    scale = HEAD_DIM ** (-0.5)
    for head in range(q_heads):
        k_at = (q_heads + head // group) * LANES
        v_at = k_at + kv_heads * LANES
        for start in range(0, seq, block):
            end = start + block
            q = qkv_ref[start:end, head * LANES : (head + 1) * LANES]
            scores = times_transposed(q, qkv_ref[:end, k_at : k_at + LANES]) * scale
            row = start + lax.broadcasted_iota(jnp.int32, (block, end), 0)
            col = lax.broadcasted_iota(jnp.int32, (block, end), 1)
            scores = jnp.where((col <= row) & (col < length), scores, masked_value)
            row_max = jnp.max(scores, axis=1, keepdims=True)
            weights = jnp.exp(scores - row_max)
            row_sum = jnp.sum(weights, axis=1, keepdims=True)
            probs = (weights * (1.0 / row_sum)).astype(bf16)
            att_ref[start:end, head * LANES : (head + 1) * LANES] = times(
                probs, qkv_ref[:end, v_at : v_at + LANES]
            )
            lse_ref[start:end, head : head + 1] = row_max + jnp.log(row_sum)
    for i in range(C):
        rows = pl.ds(pl.multiple_of((me ^ i) * tokens, tokens), tokens)
        x = att_ref[rows, :]
        low = packed([x[:, h * LANES : (h + 1) * LANES] for h in range(q_heads)])
        (give_refs if i % 2 else keep_refs)[i // 2][...] = low[:, :width_low].astype(bf16)


def attention_forward(blocks, w_qkv, tables, me, length, q_heads, kv_heads):
    C = len(blocks)
    tokens, width = blocks[0].shape
    seq = C * tokens
    heads = q_heads + 2 * kv_heads
    part = jax.ShapeDtypeStruct((tokens, q_heads * HEAD_DIM), bf16)
    result = pl.pallas_call(
        functools.partial(attention_forward_kernel, C, tokens, q_heads, kv_heads, 2 * tokens),
        out_shape=[
            jax.ShapeDtypeStruct((seq, width), bf16),
            jax.ShapeDtypeStruct((seq, heads * LANES), bf16),
            jax.ShapeDtypeStruct((seq, q_heads * LANES), f32),
            jax.ShapeDtypeStruct((seq, LANES), f32),
        ]
        + [part] * C,
        in_specs=[SMEM] + [VMEM] * (C + 3),
        out_specs=[VMEM] * (C + 4),
        scratch_shapes=[pltpu.VMEM((seq, w_qkv.shape[1]), f32)],
        compiler_params=pltpu.CompilerParams(vmem_limit_bytes=KERNEL_VMEM),
        cost_estimate=cost(seq * width * w_qkv.shape[1] + 2 * seq * seq * heads * LANES, 3 * seq * width),
        name="attention_forward",
    )(jnp.stack([me, length]).astype(jnp.int32), *blocks, w_qkv, *tables)
    return result[:4], result[4 : 4 + C // 2], result[4 + C // 2 :]


def attention_backward_kernel(C, tokens, q_heads, kv_heads, block, info_ref, *refs):
    grad_refs = refs[:C]
    qkv_ref, att_ref, lse_ref, w_ref, cos_ref, sin_ref = refs[C : C + 6]
    dqkv_ref = refs[C + 6]
    keep_refs = refs[C + 7 : C + 7 + C // 2]
    give_refs = refs[C + 7 + C // 2 : C + 7 + C]
    wide_ref, grad_ref, dq_ref, dkv_ref = refs[C + 7 + C :]
    me, length = info_ref[0], info_ref[1]
    seq = C * tokens
    group = q_heads // kv_heads
    width_low = q_heads * HEAD_DIM
    lane = lax.broadcasted_iota(jnp.int32, (tokens, LANES), 1)
    wide_ref[...] = jnp.zeros_like(wide_ref)
    for i in range(C):
        rows = pl.ds(pl.multiple_of((me ^ i) * tokens, tokens), tokens)
        wide_ref[:, :width_low] = grad_refs[i][...].astype(f32)
        wide = wide_ref[...]
        for head in range(q_heads):
            x = jnp.where(lane < HEAD_DIM, head_of(wide, head), 0.0)
            grad_ref[rows, head * LANES : (head + 1) * LANES] = x.astype(bf16)
    dkv_ref[...] = jnp.zeros_like(dkv_ref)
    scale = HEAD_DIM ** (-0.5)
    for start in range(0, seq, block):
        end = start + block
        lane_b = lax.broadcasted_iota(jnp.int32, (block, LANES), 1)
        delta = jnp.zeros((block, LANES), f32)
        for head in range(q_heads):
            at = slice(head * LANES, (head + 1) * LANES)
            one = jnp.sum(
                grad_ref[start:end, at].astype(f32) * att_ref[start:end, at], axis=1, keepdims=True
            )
            delta = jnp.where(lane_b == head, one, delta)
        delta_t = delta.T
        lse_t = lse_ref[start:end, :].T
        key = lax.broadcasted_iota(jnp.int32, (end, block), 0)
        query = start + lax.broadcasted_iota(jnp.int32, (end, block), 1)
        allowed = (key <= query) & (key < length)
        for head in range(q_heads):
            at = slice(head * LANES, (head + 1) * LANES)
            kv = head // group
            k_at = slice((q_heads + kv) * LANES, (q_heads + kv + 1) * LANES)
            v_at = slice((q_heads + kv_heads + kv) * LANES, (q_heads + kv_heads + kv + 1) * LANES)
            q, grad = qkv_ref[start:end, at], grad_ref[start:end, at]
            k, v = qkv_ref[:end, k_at], qkv_ref[:end, v_at]
            scores = times_transposed(k, q) * scale
            probs = jnp.where(allowed, jnp.exp(scores - lse_t[head : head + 1, :]), 0.0)
            grad_probs = times_transposed(v, grad)
            grad_scores = (probs * (grad_probs - delta_t[head : head + 1, :])).astype(bf16)
            dq_ref[start:end, at] = transposed_times(grad_scores, k) * scale
            dk_at = slice(kv * LANES, (kv + 1) * LANES)
            dv_at = slice((kv_heads + kv) * LANES, (kv_heads + kv + 1) * LANES)
            dkv_ref[:end, dk_at] += times(grad_scores, q) * scale
            dkv_ref[:end, dv_at] += times(probs.astype(bf16), grad)
    for i in range(C):
        rows = pl.ds(pl.multiple_of((me ^ i) * tokens, tokens), tokens)
        cosines, sines = cos_ref[rows, :], sin_ref[rows, :]
        heads = []
        for head in range(q_heads + 2 * kv_heads):
            if head < q_heads:
                x = dq_ref[rows, head * LANES : (head + 1) * LANES]
            else:
                x = dkv_ref[rows, (head - q_heads) * LANES : (head - q_heads + 1) * LANES]
            if head < q_heads + kv_heads:
                x = x * cosines - turned(x) * sines
            heads.append(x)
        dqkv_ref[i * tokens : (i + 1) * tokens, :] = packed(heads).astype(bf16)
    step = 4
    for first in range(0, C, step):
        part = times_transposed(dqkv_ref[first * tokens : (first + step) * tokens, :], w_ref[...])
        for i in range(first, first + step):
            at = (i - first) * tokens
            (give_refs if i % 2 else keep_refs)[i // 2][...] = part[at : at + tokens, :].astype(bf16)


def attention_backward(grads, saved, w_qkv, tables, me, length, q_heads, kv_heads):
    C = len(grads)
    tokens = grads[0].shape[0]
    seq = C * tokens
    width, cols = w_qkv.shape
    heads_all = q_heads + 2 * kv_heads
    part = jax.ShapeDtypeStruct((tokens, width), bf16)
    wide = -(-q_heads * HEAD_DIM // LANES) * LANES
    result = pl.pallas_call(
        functools.partial(attention_backward_kernel, C, tokens, q_heads, kv_heads, 2 * tokens),
        out_shape=[jax.ShapeDtypeStruct((seq, cols), bf16)] + [part] * C,
        in_specs=[SMEM] + [VMEM] * (C + 6),
        out_specs=[VMEM] * (C + 1),
        scratch_shapes=[
            pltpu.VMEM((tokens, wide), f32),
            pltpu.VMEM((seq, q_heads * LANES), bf16),
            pltpu.VMEM((seq, q_heads * LANES), f32),
            pltpu.VMEM((seq, 2 * kv_heads * LANES), f32),
        ],
        compiler_params=pltpu.CompilerParams(vmem_limit_bytes=KERNEL_VMEM),
        cost_estimate=cost(seq * width * cols + 4 * seq * seq * heads_all * LANES, 3 * seq * width),
        name="attention_backward",
    )(jnp.stack([me, length]).astype(jnp.int32), *grads, *saved, w_qkv, *tables)
    return result[0], result[1 : 1 + C // 2], result[1 + C // 2 :]


def ffn_forward_kernel(C, tokens, cuts, *refs):
    n_refs = refs[:C]
    gu_ref, down_ref = refs[C : C + 2]
    n_all_ref, act_ref, coef_ref = refs[C + 2 : C + 5]
    keep_refs = refs[C + 5 : C + 5 + C // 2]
    give_refs = refs[C + 5 + C // 2 :]
    w = down_ref.shape[0] // cuts
    for i in range(C):
        n_all_ref[i * tokens : (i + 1) * tokens, :] = n_refs[i][...]
    step = 4
    for first in range(0, C, step):
        rows = slice(first * tokens, (first + step) * tokens)
        both = times(n_all_ref[rows, :], gu_ref[...])
        for j in range(cuts):
            gate_at = slice(2 * j * w, (2 * j + 1) * w)
            up_at = slice((2 * j + 1) * w, (2 * j + 2) * w)
            gate, up = both[:, gate_at], both[:, up_at]
            sigmoid = jax.nn.sigmoid(gate)
            silu = gate * sigmoid
            act_ref[rows, j * w : (j + 1) * w] = (silu * up).astype(bf16)
            coef_ref[rows, gate_at] = (up * (sigmoid * (1.0 + gate * (1.0 - sigmoid)))).astype(bf16)
            coef_ref[rows, up_at] = silu.astype(bf16)
        part = times(act_ref[rows, :], down_ref[...])
        for i in range(first, first + step):
            at = (i - first) * tokens
            (give_refs if i % 2 else keep_refs)[i // 2][...] = part[at : at + tokens, :].astype(bf16)


def ffn_forward(blocks, gate_up, down, cuts):
    C = len(blocks)
    tokens, width = blocks[0].shape
    seq, own = C * tokens, down.shape[0]
    part = jax.ShapeDtypeStruct((tokens, width), bf16)
    result = pl.pallas_call(
        functools.partial(ffn_forward_kernel, C, tokens, cuts),
        out_shape=[
            jax.ShapeDtypeStruct((seq, width), bf16),
            jax.ShapeDtypeStruct((seq, own), bf16),
            jax.ShapeDtypeStruct((seq, 2 * own), bf16),
        ]
        + [part] * C,
        in_specs=[VMEM] * (C + 2),
        out_specs=[VMEM] * (C + 3),
        compiler_params=pltpu.CompilerParams(vmem_limit_bytes=KERNEL_VMEM),
        cost_estimate=cost(3 * seq * width * own, 3 * seq * width),
        name="ffn_forward",
    )(*blocks, gate_up, down)
    return result[:3], result[3 : 3 + C // 2], result[3 + C // 2 :]


def ffn_backward_kernel(C, tokens, cuts, g_ref, gu_ref, down_ref, coef_ref, dgu_ref, *refs):
    keep_refs, give_refs = refs[: C // 2], refs[C // 2 : C]
    gu_t_ref, down_t_ref = refs[C:]
    gu_t_ref[...] = gu_ref[...].T
    down_t_ref[...] = down_ref[...].T
    w = down_ref.shape[0] // cuts
    step = 4
    for first in range(0, C, step):
        rows = slice(first * tokens, (first + step) * tokens)
        grad_act = times(g_ref[rows, :], down_t_ref[...])
        for j in range(2 * cuts):
            at = slice(j * w, (j + 1) * w)
            part = grad_act[:, (j // 2) * w : (j // 2 + 1) * w]
            dgu_ref[rows, at] = (part * coef_ref[rows, at].astype(f32)).astype(bf16)
        part = times(dgu_ref[rows, :], gu_t_ref[...])
        for i in range(first, first + step):
            at = (i - first) * tokens
            (give_refs if i % 2 else keep_refs)[i // 2][...] = part[at : at + tokens, :].astype(bf16)


def ffn_backward(grad_all, gate_up, down, coef, cuts, C):
    seq, width = grad_all.shape
    tokens, own = seq // C, down.shape[0]
    part = jax.ShapeDtypeStruct((tokens, width), bf16)
    result = pl.pallas_call(
        functools.partial(ffn_backward_kernel, C, tokens, cuts),
        out_shape=[jax.ShapeDtypeStruct((seq, 2 * own), bf16)] + [part] * C,
        in_specs=[VMEM] * 4,
        out_specs=[VMEM] * (C + 1),
        scratch_shapes=[pltpu.VMEM((2 * own, width), bf16), pltpu.VMEM((width, own), bf16)],
        compiler_params=pltpu.CompilerParams(vmem_limit_bytes=KERNEL_VMEM),
        cost_estimate=cost(3 * seq * width * own, 3 * seq * width),
        name="ffn_backward",
    )(grad_all, gate_up, down, coef)
    return result[0], result[1 : 1 + C // 2], result[1 + C // 2 :]


def ffn_slices_kernel(me_ref, gate_ref, up_ref, down_ref, gu_ref, rows_ref):
    piece = gate_ref.shape[1]
    gu_ref[:, :piece] = gate_ref[...]
    gu_ref[:, piece:] = up_ref[...]
    rows_ref[...] = down_ref[...]


def ffn_slices(w_gate, w_up, w_down, me, C, Z):
    rows, ff = w_gate.shape
    width = w_down.shape[1]
    piece = ff // (Z * C)
    if piece % LANES:
        cut = [pick(w.reshape(rows, Z, C, piece), me, 2).reshape(rows, -1) for w in (w_gate, w_up)]
        return jnp.concatenate(cut, axis=1), lax.dynamic_slice_in_dim(w_down, me * piece, piece, 0)
    return pl.pallas_call(
        ffn_slices_kernel,
        out_shape=[
            jax.ShapeDtypeStruct((rows, 2 * Z * piece), bf16),
            jax.ShapeDtypeStruct((piece, width), bf16),
        ],
        grid_spec=pltpu.PrefetchScalarGridSpec(
            num_scalar_prefetch=1,
            grid=(Z,),
            in_specs=[
                pl.BlockSpec((rows, piece), lambda j, me: (0, j * C + me[0])),
                pl.BlockSpec((rows, piece), lambda j, me: (0, j * C + me[0])),
                pl.BlockSpec((piece // Z, width), lambda j, me: (me[0] * Z + j, 0)),
            ],
            out_specs=[
                pl.BlockSpec((rows, 2 * piece), lambda j, me: (0, j)),
                pl.BlockSpec((piece // Z, width), lambda j, me: (j, 0)),
            ],
        ),
        compiler_params=pltpu.CompilerParams(vmem_limit_bytes=56 * 1024 * 1024),
        cost_estimate=cost(0, 6 * rows * ff // C),
        name="ffn_slices",
    )(me.reshape(1), w_gate, w_up, w_down)


def column_grads_kernel(C, Z, piece, me_ref, *refs):
    gu_refs = refs[:C]
    gate_ref, up_ref, wide_ref, sems = refs[C:]
    me = me_ref[0]
    stride = gate_ref.shape[1] // Z
    flying = [(), ()]
    for i in range(C):
        slot = i % 2
        for copy in flying[slot]:
            copy.wait()
        wide_ref[slot] = gu_refs[i][...].astype(f32)
        copies = []
        for j in range(Z):
            at = pl.multiple_of(j * stride + (me ^ i) * piece, piece)
            for a, ref in enumerate((gate_ref, up_ref)):
                copies.append(
                    pltpu.make_async_copy(
                        wide_ref.at[slot, :, pl.ds((2 * j + a) * piece, piece)],
                        ref.at[:, pl.ds(at, piece)],
                        sems.at[slot, 2 * j + a],
                    )
                )
        for copy in copies:
            copy.start()
        flying[slot] = copies
    for copies in flying:
        for copy in copies:
            copy.wait()


def column_grads(blocks, me, Z):
    C = len(blocks)
    rows, cols = blocks[0].shape
    ff = C * cols // 2
    piece = ff // (Z * C)
    if piece % LANES:
        gu = jnp.stack(unsort(blocks, me)).astype(f32).reshape(C, rows, 2, Z, piece)
        gu = gu.transpose(2, 1, 3, 0, 4).reshape(2, rows, ff)
        return gu[0], gu[1]
    return pl.pallas_call(
        functools.partial(column_grads_kernel, C, Z, piece),
        out_shape=[jax.ShapeDtypeStruct((rows, ff), f32)] * 2,
        in_specs=[SMEM] + [VMEM] * C,
        out_specs=[ANY] * 2,
        scratch_shapes=[
            pltpu.VMEM((2, rows, cols), f32),
            pltpu.SemaphoreType.DMA((2, 2 * Z)),
        ],
        compiler_params=pltpu.CompilerParams(vmem_limit_bytes=KERNEL_VMEM),
        cost_estimate=cost(0, 6 * rows * ff),
        name="column_grads",
    )(me.reshape(1), *blocks)


def row_grads_kernel(C, me_ref, *refs):
    row_refs = refs[:C]
    out_ref, tall_ref, sems = refs[C:]
    me = me_ref[0]
    piece = row_refs[0].shape[0]
    copies = []
    for i in range(C):
        tall_ref[i] = row_refs[i][...].astype(f32)
        at = pl.multiple_of((me ^ i) * piece, piece)
        copies.append(
            pltpu.make_async_copy(tall_ref.at[i], out_ref.at[pl.ds(at, piece), :], sems.at[i])
        )
        copies[-1].start()
    for copy in copies:
        copy.wait()


def row_grads(blocks, me):
    C = len(blocks)
    piece, width = blocks[0].shape
    if piece % 16:
        return jnp.concatenate(unsort(blocks, me), axis=0).astype(f32)
    return pl.pallas_call(
        functools.partial(row_grads_kernel, C),
        out_shape=jax.ShapeDtypeStruct((C * piece, width), f32),
        in_specs=[SMEM] + [VMEM] * C,
        out_specs=ANY,
        scratch_shapes=[
            pltpu.VMEM((C, piece, width), f32),
            pltpu.SemaphoreType.DMA((C,)),
        ],
        compiler_params=pltpu.CompilerParams(vmem_limit_bytes=KERNEL_VMEM),
        cost_estimate=cost(0, 4 * C * piece * width),
        name="row_grads",
    )(me.reshape(1), *blocks)


def middle_forward_kernel(C, Z, piece, info_ref, *refs):
    R = C // 2
    pair_refs, w_refs = refs[:R], refs[R : R + C]
    hidden_ref, gain_ref = refs[R + C : R + C + 2]
    middle_ref, normed_ref, att_ref, out_ref = refs[R + C + 2 :]
    me, line = info_ref[0], info_ref[1]
    pair_cols = pair_refs[0].shape[1]
    rows_z = C * piece
    for i in range(C):
        for j in range(Z):
            at = pl.multiple_of((line ^ j) * rows_z + (me ^ i) * piece, piece)
            out_ref[pl.ds(at, piece), :] = w_refs[i][j * piece : (j + 1) * piece, :]
    for s in range(R):
        at = pl.multiple_of(((me // 2) ^ s) * pair_cols, pair_cols)
        att_ref[:, pl.ds(at, pair_cols)] = pair_refs[s][...]
    middle = hidden_ref[...] + times(att_ref[...], out_ref[...])
    middle_ref[...] = middle
    normed_ref[...] = (middle * norm_scale(middle) * gain_ref[...]).astype(bf16)


def middle_forward(pairs, w_blocks, hidden, gain, me, line, Z):
    C = len(w_blocks)
    tokens, width = hidden.shape
    piece = w_blocks[0].shape[0] // Z
    if piece % 16 or pairs[0].shape[1] % LANES:
        cut = [x.reshape(Z, piece, width) for x in w_blocks]
        rows = jnp.stack(unsort(cut, me))
        out_all = jnp.stack([pick(rows, line ^ j, 1) for j in range(Z)]).reshape(width, width)
        attended = jnp.concatenate(unsort(pairs, me // 2), axis=1)
        middle = hidden + times(attended, out_all)
        return middle, (middle * norm_scale(middle) * gain).astype(bf16), attended, out_all
    return pl.pallas_call(
        functools.partial(middle_forward_kernel, C, Z, piece),
        out_shape=[
            jax.ShapeDtypeStruct((tokens, width), f32),
            jax.ShapeDtypeStruct((tokens, width), bf16),
            jax.ShapeDtypeStruct((tokens, width), bf16),
            jax.ShapeDtypeStruct((width, width), bf16),
        ],
        in_specs=[SMEM] + [VMEM] * (C // 2 + C + 2),
        out_specs=[VMEM] * 4,
        compiler_params=pltpu.CompilerParams(vmem_limit_bytes=KERNEL_VMEM),
        cost_estimate=cost(tokens * width * width, 3 * width * width),
        name="middle_forward",
    )(jnp.stack([me, line]), *pairs, *w_blocks, hidden, gain.reshape(1, width))


def middle_backward_kernel(R, info_ref, *refs):
    own_ref, got_refs = refs[0], refs[1:R]
    middle_ref, gain_ref, grad_out_ref, out_ref = refs[R : R + 4]
    grad_ref, low_ref, gain_grad_ref = refs[R + 4 : R + 7]
    pair_refs, att_ref = refs[R + 7 : 2 * R + 7], refs[2 * R + 7]
    upstream = own_ref[...]
    for ref in got_refs:
        upstream = upstream + ref[...].astype(f32)
    middle = middle_ref[...]
    back, gain_grad = norm_back(upstream, middle, norm_scale(middle), gain_ref[...])
    gain_grad_ref[...] = gain_grad.reshape(gain_grad_ref.shape)
    grad = grad_out_ref[...] + back
    grad_ref[...] = grad
    low = grad.astype(bf16)
    low_ref[...] = low
    att_ref[...] = times_transposed(low, out_ref[...]).astype(bf16)
    pair_cols = pair_refs[0].shape[1]
    for s in range(R):
        at = pl.multiple_of(((info_ref[0] // 2) ^ s) * pair_cols, pair_cols)
        pair_refs[s][...] = att_ref[:, pl.ds(at, pair_cols)]


def middle_backward(own, got, middle, gain, grad_output, out_all, me):
    R = len(got) + 1
    tokens, width = middle.shape
    pair_cols = width // R
    if pair_cols % LANES:
        upstream = own
        for x in got:
            upstream = upstream + x.astype(f32)
        back, gain_grad = norm_back(upstream, middle, norm_scale(middle), gain)
        grad = grad_output + back
        low = grad.astype(bf16)
        cut = times_transposed(low, out_all).astype(bf16).reshape(tokens, R, pair_cols)
        return grad, low, gain_grad, [pick(cut, (me // 2) ^ s, 1) for s in range(R)]
    result = pl.pallas_call(
        functools.partial(middle_backward_kernel, R),
        out_shape=[
            jax.ShapeDtypeStruct((tokens, width), f32),
            jax.ShapeDtypeStruct((tokens, width), bf16),
            jax.ShapeDtypeStruct((1, width), f32),
        ]
        + [jax.ShapeDtypeStruct((tokens, pair_cols), bf16)] * R,
        in_specs=[SMEM] + [VMEM] * (R + 4),
        out_specs=[VMEM] * (3 + R),
        scratch_shapes=[pltpu.VMEM((tokens, width), bf16)],
        compiler_params=pltpu.CompilerParams(vmem_limit_bytes=KERNEL_VMEM),
        cost_estimate=cost(tokens * width * width, 3 * width * width),
        name="middle_backward",
    )(me.reshape(1), own, *got, middle, gain.reshape(1, width), grad_output, out_all)
    return result[0], result[1], result[2].reshape(width), result[3:]


def out_grads_kernel(C, Z, piece, info_ref, att_ref, low_ref, *refs):
    keep_refs, give_refs, sum_ref = refs[: C // 2], refs[C // 2 : C], refs[C]
    me, line = info_ref[0], info_ref[1]
    rows_z = C * piece
    sum_ref[...] = transposed_times(att_ref[...], low_ref[...])
    for i in range(C):
        ref = (give_refs if i % 2 else keep_refs)[i // 2]
        for j in range(Z):
            at = pl.multiple_of((line ^ j) * rows_z + (me ^ i) * piece, piece)
            ref[j * piece : (j + 1) * piece, :] = sum_ref[pl.ds(at, piece), :].astype(bf16)


def out_grads(attended, low, me, line, C, Z):
    width = attended.shape[1]
    piece = width // (C * Z)
    if piece % 16:
        grad = transposed_times(attended, low).astype(bf16).reshape(Z, C, piece, width)
        grad = jnp.stack([pick(grad, line ^ j) for j in range(Z)])
        grad = [pick(grad, me ^ i, 1).reshape(Z * piece, width) for i in range(C)]
        return grad[0::2], grad[1::2]
    result = pl.pallas_call(
        functools.partial(out_grads_kernel, C, Z, piece),
        out_shape=[jax.ShapeDtypeStruct((Z * piece, width), bf16)] * C,
        in_specs=[SMEM, VMEM, VMEM],
        out_specs=[VMEM] * C,
        scratch_shapes=[pltpu.VMEM((width, width), f32)],
        compiler_params=pltpu.CompilerParams(vmem_limit_bytes=KERNEL_VMEM),
        cost_estimate=cost(2 * attended.shape[0] * width * width, 3 * width * width),
        name="out_grads",
    )(jnp.stack([me, line]), attended, low)
    return result[: C // 2], result[C // 2 :]


def down_grads_kernel(C, tokens, *refs):
    g_refs, (act_ref, g_all_ref, grad_ref) = refs[:C], refs[C:]
    for i in range(C):
        g_all_ref[i * tokens : (i + 1) * tokens, :] = g_refs[i][...]
    grad_ref[...] = transposed_times(act_ref[...], g_all_ref[...]).astype(bf16)


def down_grads(blocks, activated):
    C = len(blocks)
    tokens, width = blocks[0].shape
    return pl.pallas_call(
        functools.partial(down_grads_kernel, C, tokens),
        out_shape=[
            jax.ShapeDtypeStruct((C * tokens, width), bf16),
            jax.ShapeDtypeStruct((activated.shape[1], width), bf16),
        ],
        in_specs=[VMEM] * (C + 1),
        out_specs=[VMEM] * 2,
        compiler_params=pltpu.CompilerParams(vmem_limit_bytes=KERNEL_VMEM),
        cost_estimate=cost(C * tokens * width * activated.shape[1], 2 * C * tokens * width),
        name="down_grads",
    )(*blocks, activated)


def qkv_grads_kernel(C, q_cols, kv_cols, me_ref, *refs):
    blocks, (query_ref, key_ref, value_ref, sort_ref) = refs[:C], refs[C:]
    cols = sort_ref.shape[2]
    for i in range(C):
        sort_ref[me_ref[0] ^ i] = blocks[i][...].astype(f32)
    lane = lax.broadcasted_iota(jnp.int32, sort_ref.shape[1:], 1)
    for ref, first, size in (
        (query_ref, 0, q_cols),
        (key_ref, q_cols, kv_cols),
        (value_ref, q_cols + kv_cols, kv_cols),
    ):
        many = cols // size
        for group in range(C // many):
            total = None
            for j in range(many):
                x = sort_ref[group * many + j]
                shift = (j * size - first) % cols
                x = pltpu.roll(x, shift, 1) if shift else x
                total = x if total is None else jnp.where(lane < j * size, total, x)
            ref[:, group * cols : (group + 1) * cols] = total


def qkv_grads(blocks, me, q_cols, kv_cols, kv_copies):
    C = len(blocks)
    rows, cols = blocks[0].shape
    many = C // kv_copies
    if kv_copies > 1 or cols % q_cols or cols % kv_cols or q_cols + 2 * kv_cols != cols:
        parts = unsort(blocks, me)

        def kv_final(start):
            own = [part[:, start : start + kv_cols].astype(f32) for part in parts]
            own = [sum(own[n : n + kv_copies]) for n in range(0, C, kv_copies)]
            return jnp.concatenate(own, axis=1)

        query = jnp.concatenate([part[:, :q_cols] for part in parts], axis=1).astype(f32)
        return query, kv_final(q_cols), kv_final(q_cols + kv_cols)
    return pl.pallas_call(
        functools.partial(qkv_grads_kernel, C, q_cols, kv_cols),
        out_shape=[
            jax.ShapeDtypeStruct((rows, C * q_cols), f32),
            jax.ShapeDtypeStruct((rows, many * kv_cols), f32),
            jax.ShapeDtypeStruct((rows, many * kv_cols), f32),
        ],
        in_specs=[SMEM] + [VMEM] * C,
        out_specs=[VMEM] * 3,
        scratch_shapes=[pltpu.VMEM((C, rows, cols), f32)],
        compiler_params=pltpu.CompilerParams(vmem_limit_bytes=KERNEL_VMEM),
        cost_estimate=cost(0, 8 * rows * C * cols),
        name="qkv_grads",
    )(me.reshape(1), *blocks)


def local(
    inputs,
    teacher,
    lengths,
    w_query,
    w_key,
    w_value,
    w_out,
    w_gate,
    w_up,
    w_down,
    gain_attn,
    gain_ffn,
):
    hidden_in = inputs[0]
    target = teacher[0]
    seq_length = lengths[0]
    tokens, width = hidden_in.shape
    C = lax.axis_size("ctx")
    Z = lax.axis_size("fsdp")
    R = C // 2
    p = lax.axis_index("ctx")
    z = lax.axis_index("fsdp")
    core = p % 2
    rows_z = width // Z
    seq = C * tokens
    q_heads = HEADS // C
    kv_heads = max(1, KV_HEADS // C)
    kv_copies = max(1, C // KV_HEADS)
    q_cols = q_heads * HEAD_DIM
    kv_cols = kv_heads * HEAD_DIM
    qkv_cols = q_cols + 2 * kv_cols
    positions = p * tokens + jnp.arange(tokens, dtype=jnp.int32)

    def line_columns(x):
        cut = x.reshape(x.shape[0], Z, rows_z)
        return jnp.concatenate([pick(cut, z ^ i, 1) for i in range(Z)], axis=1)

    small = jnp.concatenate(
        [gain_attn.astype(f32), gain_ffn.astype(f32), jnp.full((LANES,), seq_length).astype(f32)]
    )
    small = jnp.stack(unsort(line_blocks(small.reshape(1, -1)), z)).reshape(Z, -1)
    gain_one = small[:, :rows_z].reshape(width)
    gain_two = small[:, rows_z : 2 * rows_z].reshape(width)
    valid_count = jnp.sum(small[:, 2 * rows_z])
    cuts = 1 if (w_gate.shape[1] // (Z * C)) % LANES else Z
    gate_up_own, down_own = ffn_slices(w_gate, w_up, w_down, p, C, Z)
    gate_up = lax.all_gather(gate_up_own, "fsdp", axis=0, tiled=True)
    down_rows = lax.all_gather(down_own, "fsdp", axis=0, tiled=True)
    kv_start = (p * KV_HEADS // C) * HEAD_DIM
    qkv_own = jnp.concatenate(
        [
            lax.dynamic_slice_in_dim(w_query, p * q_cols, q_cols, 1),
            lax.dynamic_slice_in_dim(w_key, kv_start, kv_cols, 1),
            lax.dynamic_slice_in_dim(w_value, kv_start, kv_cols, 1),
            jnp.zeros((rows_z, -qkv_cols % LANES), bf16),
        ],
        axis=1,
    )

    scale_one = norm_scale(hidden_in)
    normed_one = line_columns((hidden_in * scale_one * gain_one).astype(bf16))
    normed_one, qkv_own = together([normed_one, qkv_own])
    got = together(plane_sends(normed_one) + line_sends(qkv_own))
    normed_blocks = core_blocks([normed_one] + got[: R - 1])
    w_qkv = jnp.concatenate([qkv_own] + got[R - 1 :], axis=0)
    tables = rope_tables(seq)
    (normed_all, qkv, attended, lse), att_keep, att_give = attention_forward(
        normed_blocks, w_qkv, tables, p, seq_length, q_heads, kv_heads
    )

    out_piece = rows_z // C
    out_own = lax.dynamic_slice_in_dim(w_out, p * out_piece, out_piece, 0)
    out_own = after(out_own, got)
    out_blocks = plane_blocks(jnp.concatenate(line_blocks(out_own), axis=0))

    def heads_of_chip(own, other):
        return jnp.where(
            core == 0,
            jnp.concatenate([own, other], axis=1),
            jnp.concatenate([other, own], axis=1),
        )

    pairs = [heads_of_chip(a, partner(b, "ctx", 1)) for a, b in zip(att_keep, att_give, strict=True)]
    pairs = [pairs[0]] + together([partner(pairs[s], "ctx", 2 * s) for s in range(1, R)])
    middle, normed_two_own, attended_tokens, out_all = middle_forward(
        pairs, out_blocks, hidden_in, gain_two, p, z, Z
    )

    normed_two_blocks = plane_blocks(normed_two_own)
    (normed_two, activated, coef), keep, give = ffn_forward(
        normed_two_blocks, gate_up, down_rows, cuts
    )
    output = middle + plane_reduce(keep, give)

    valid_rows = (positions < seq_length).astype(f32)
    residual_error = output - target
    squares = jnp.sum(valid_rows[:, None] * residual_error * residual_error)
    grad_output = valid_rows[:, None] * (2.0 * residual_error) / valid_count

    grad_low, grad_down = down_grads(plane_blocks(grad_output.astype(bf16)), activated)
    shard_down = lax.psum_scatter(grad_down, "fsdp", scatter_dimension=0, tiled=True)
    grad_gu, keep, give = ffn_backward(grad_low, gate_up, down_rows, coef, cuts, C)
    chips = chip_sums(keep, give)
    grad_gate_up = transposed_times(normed_two, after(grad_gu, chips)).astype(bf16)
    shard_gate_up = lax.psum_scatter(grad_gate_up, "fsdp", scatter_dimension=0, tiled=True)
    grad_middle, m_low, grad_gain_two, pairs = middle_backward(
        chips[0], after(chip_sends(chips), grad_gate_up), middle, gain_two, grad_output, out_all, p
    )

    out_keep, out_give = out_grads(attended_tokens, after(m_low, pairs), p, z, C, Z)
    pairs = [pairs[0]] + together([partner(pairs[s], "ctx", 2 * s) for s in range(1, R)])
    blocks = []
    for pair in after(pairs, out_keep):
        own = jnp.where(core == 0, pair[:, :q_cols], pair[:, q_cols:])
        other = jnp.where(core == 0, pair[:, q_cols:], pair[:, :q_cols])
        blocks += [own, partner(other, "ctx", 1)]
    out_chips = chip_sums(out_keep, out_give)
    blocks = after(blocks, out_chips, shard_down)
    grad_qkv, keep, give = attention_backward(
        blocks, (qkv, attended, lse), w_qkv, tables, p, seq_length, q_heads, kv_heads
    )
    grad_w_qkv = transposed_times(normed_all, grad_qkv).astype(bf16)
    keep, give = after((keep, give), grad_w_qkv)
    shard_qkv = line_reduce(
        [grad_w_qkv[i * rows_z : (i + 1) * rows_z] for i in range(Z)]
    ).astype(bf16)
    chips = chip_sums(keep, give)
    out_got = after(chip_sends(out_chips), chips)
    grad_normed_one = line_columns(total(chips[0], chip_sends(chips)))
    back_one, grad_gain_one = norm_back(grad_normed_one, hidden_in, scale_one, gain_one)
    grad_hidden = grad_middle + back_one

    grad_out = total(out_chips[0], out_got).astype(bf16)
    shard_out = line_reduce(
        [grad_out[j * out_piece : (j + 1) * out_piece] for j in range(Z)]
    ).astype(bf16)
    final_down = row_grads(plane_blocks(shard_down), p)
    gate_up_blocks = plane_blocks(after(shard_gate_up, chips))
    final_gate, final_up = column_grads(gate_up_blocks, p, Z)
    final_out = row_grads(plane_blocks(shard_out), p)
    qkv_blocks = plane_blocks(after(shard_qkv, gate_up_blocks))
    final_query, final_key, final_value = qkv_grads(qkv_blocks, p, q_cols, kv_cols, kv_copies)

    sums = jnp.stack([grad_gain_one, grad_gain_two, jnp.full((width,), squares)])
    sums = tree_sum(tree_sum(sums, "ctx"), "fsdp")
    loss_value = sums[2, 0] / valid_count
    gain_grads = lax.dynamic_slice_in_dim(sums[:2], z * rows_z, rows_z, 1)

    return (
        output[None],
        loss_value,
        grad_hidden[None],
        final_query,
        final_key,
        final_value,
        final_out,
        final_gate,
        final_up,
        final_down,
        gain_grads[0],
        gain_grads[1],
    )


def solution(mesh):
    return jax.shard_map(
        local,
        mesh=mesh,
        in_specs=(
            P("fsdp", "ctx", None),
            P("fsdp", "ctx", None),
            P("fsdp"),
            P("fsdp", None),
            P("fsdp", None),
            P("fsdp", None),
            P("fsdp", None),
            P("fsdp", None),
            P("fsdp", None),
            P("fsdp", None),
            P("fsdp"),
            P("fsdp"),
        ),
        out_specs=(
            P("fsdp", "ctx", None),
            P(),
            P("fsdp", "ctx", None),
            P("fsdp", None),
            P("fsdp", None),
            P("fsdp", None),
            P("fsdp", None),
            P("fsdp", None),
            P("fsdp", None),
            P("fsdp", None),
            P("fsdp"),
            P("fsdp"),
        ),
        check_vma=False,
    )
```

```python
import functools

import jax
import jax.numpy as jnp
from jax import lax
from jax.experimental import pallas as pl
from jax.experimental.pallas import tpu as pltpu
from jax.sharding import PartitionSpec as P

HEADS = 16
KV_HEADS = 8
HEAD_DIM = 96
LANES = 128

eps_norm = 1e-05
rope_base = 100000.0
masked_value = -1e30

f32 = jnp.float32
bf16 = jnp.bfloat16

VMEM = pl.BlockSpec(memory_space=pltpu.VMEM)
SMEM = pl.BlockSpec(memory_space=pltpu.SMEM)
HBM = pl.BlockSpec(memory_space=pltpu.HBM)
MIB = 1024 * 1024


def cost(multiply_adds, values):
    return pl.CostEstimate(flops=1, bytes_accessed=1, transcendentals=0)


def in_hbm(*xs):
    return [pltpu.with_memory_space_constraint(x, pltpu.HBM) for x in xs]


def started(sems, first, *pairs):
    copies = [pltpu.make_async_copy(a, b, sems.at[first + n]) for n, (a, b) in enumerate(pairs)]
    for copy in copies:
        copy.start()
    return copies


def times(left, right):
    return jnp.dot(left, right, preferred_element_type=f32)


def times_transposed(left, right):
    return lax.dot_general(left, right, (((1,), (1,)), ((), ())), preferred_element_type=f32)


def transposed_times(left, right):
    return lax.dot_general(left, right, (((0,), (0,)), ((), ())), preferred_element_type=f32)


def norm_scale(features):
    return lax.rsqrt(jnp.mean(features * features, axis=-1, keepdims=True) + eps_norm)


def norm_back(upstream, features, row_scale, gain_vector):
    weighted = upstream * gain_vector
    inner_mean = jnp.mean(weighted * features, axis=-1, keepdims=True)
    grad_rows = row_scale * weighted - features * (row_scale * row_scale * row_scale) * inner_mean
    return (grad_rows, jnp.sum(upstream * (features * row_scale), axis=0))


def partner(x, axis, mask):
    return lax.ppermute(x, axis, [(i, i ^ mask) for i in range(lax.axis_size(axis))])


def plane_sends(x):
    return [partner(x, "ctx", 2 * s) for s in range(1, lax.axis_size("ctx") // 2)]


def core_blocks(mine):
    blocks = []
    for x in mine:
        blocks += [x, partner(x, "ctx", 1)]
    return blocks


def plane_blocks(x):
    return core_blocks([x] + plane_sends(x))


def near_sends(x):
    return [partner(x, "ctx", 2), partner(x, "ctx", 4)]


def far_sends(near):
    half = near[0].shape[0] // 2
    return [partner(near[0][:half], "ctx", 4), partner(near[1][half:], "ctx", 2)]


def square_pieces(x, near, far):
    half = x.shape[0] // 2
    mine = [(0, 0, x), (1, 0, near[0]), (2, 0, near[1]), (3, 0, far[0]), (3, half, far[1])]
    other = together([partner(block, "ctx", 1) for _, _, block in mine])
    pieces = []
    for (s, first, block), swapped in zip(mine, other, strict=True):
        pieces += [(2 * s, first, block), (2 * s + 1, first, swapped)]
    return pieces


def line_sends(x):
    return [partner(x, "fsdp", s) for s in range(1, lax.axis_size("fsdp"))]


def plane_reduce(keep, give):
    chips = chip_sums(keep, give)
    return total(chips[0], chip_sends(chips))


def chip_sums(keep, give):
    got = [partner(x, "ctx", 1) for x in give[::-1]][::-1]
    own = keep[0].astype(f32) + got[0].astype(f32)
    return [own] + [
        (a.astype(f32) + b.astype(f32)).astype(bf16) for a, b in zip(keep[1:], got[1:], strict=True)
    ]


def chip_sends(chips):
    return together([partner(chips[s], "ctx", 2 * s) for s in range(len(chips) - 1, 0, -1)])


def total(own, got):
    for x in got:
        own = own + x.astype(f32)
    return own


def tree_sum(x, axis):
    mask = 1
    while mask < lax.axis_size(axis):
        x = x + partner(x, axis, mask)
        mask *= 2
    return x


def line_blocks(x):
    return [x] + together(line_sends(x))


def line_reduce(parts):
    got = together([partner(parts[s], "fsdp", s) for s in range(1, len(parts))])
    return total(parts[0].astype(f32), got)


def together(xs):
    return list(lax.optimization_barrier(tuple(xs)))


def after(x, *done):
    return lax.optimization_barrier((x, done))[0]


def pick(x, index, axis=0):
    return lax.dynamic_index_in_dim(x, index, axis, False)


def unsort(blocks, me):
    stacked = jnp.stack(blocks)
    return [pick(stacked, me ^ b) for b in range(len(blocks))]


def rope_tables(count):
    half_dim = HEAD_DIM // 2
    frequencies = rope_base ** (-(jnp.arange(half_dim, dtype=f32) * 2.0) / HEAD_DIM)
    angles = jnp.arange(count, dtype=f32)[:, None] * frequencies[None, :]
    cosines, sines = jnp.cos(angles), jnp.sin(angles)
    pad = jnp.zeros((count, LANES - HEAD_DIM), f32)
    return (
        jnp.concatenate([cosines, cosines, pad], axis=1),
        jnp.concatenate([-sines, sines, pad], axis=1),
    )


def turned(x):
    lane = lax.broadcasted_iota(jnp.int32, x.shape, 1)
    half_dim = HEAD_DIM // 2
    return jnp.where(
        lane < half_dim, pltpu.roll(x, LANES - half_dim, 1), pltpu.roll(x, half_dim, 1)
    )


def head_of(x, head):
    if head:
        x = pltpu.roll(x, x.shape[1] - head * HEAD_DIM, 1)
    return x[:, :LANES]


def packed(heads):
    wide = -(-len(heads) * HEAD_DIM // LANES) * LANES
    total = None
    for index, head in enumerate(heads):
        if wide > LANES:
            head = jnp.concatenate([head, jnp.zeros((head.shape[0], wide - LANES), f32)], axis=1)
        if index:
            head = pltpu.roll(head, index * HEAD_DIM, 1)
        total = head if total is None else total + head
    return total


def attention_forward_kernel(C, Z, tokens, q_heads, kv_heads, block, info_ref, *refs):
    R = C // 2
    n_refs, w_parts = refs[:C], refs[C : C + Z]
    cos_hbm, sin_hbm = refs[C + Z : C + Z + 2]
    n_hbm, w_hbm, qkv_hbm, att_hbm, lse_hbm = refs[C + Z + 2 : C + Z + 7]
    block_refs = refs[C + Z + 7 : C + Z + 7 + R]
    n_all_ref, w_ref, lin_ref, qkv_ref, att_ref, lse_ref, cos_ref, sin_ref, sems = refs[C + Z + 7 + R :]
    me, length = info_ref[0], info_ref[1]
    seq = C * tokens
    group = q_heads // kv_heads
    width_low = q_heads * HEAD_DIM
    rows_z = w_ref.shape[0] // Z
    pairs = []
    for j in range(Z):
        at = pl.multiple_of((info_ref[2] ^ j) * rows_z, rows_z)
        pairs.append((w_parts[j].at[:rows_z, :], w_ref.at[pl.ds(at, rows_z), :]))
    tables = started(sems, 0, (cos_hbm, cos_ref), (sin_hbm, sin_ref), *pairs)
    for i in range(C):
        n_all_ref[i * tokens : (i + 1) * tokens, :] = n_refs[i][...]
    for copy in tables[2:]:
        copy.wait()
    saved = started(sems, 2, (n_all_ref, n_hbm), (w_ref, w_hbm))
    step = 4 * tokens
    for start in range(0, seq, step):
        lin_ref[start : start + step, :] = times(n_all_ref[start : start + step, :], w_ref[...])
    for copy in tables[:2]:
        copy.wait()
    lane = lax.broadcasted_iota(jnp.int32, (tokens, LANES), 1)
    for i in range(C):
        rows = pl.ds(pl.multiple_of((me ^ i) * tokens, tokens), tokens)
        lin = lin_ref[i * tokens : (i + 1) * tokens, :]
        cosines, sines = cos_ref[rows, :], sin_ref[rows, :]
        for head in range(q_heads + 2 * kv_heads):
            x = head_of(lin, head)
            if head < q_heads + kv_heads:
                x = x * cosines + turned(x) * sines
            else:
                x = jnp.where(lane < HEAD_DIM, x, 0.0)
            qkv_ref[rows, head * LANES : (head + 1) * LANES] = x.astype(bf16)
    saved += started(sems, 4, (qkv_ref, qkv_hbm))
    scale = HEAD_DIM ** (-0.5)
    for head in range(q_heads):
        k_at = (q_heads + head // group) * LANES
        v_at = k_at + kv_heads * LANES
        for start in range(0, seq, block):
            end = start + block
            q = qkv_ref[start:end, head * LANES : (head + 1) * LANES]
            scores = times_transposed(q, qkv_ref[:end, k_at : k_at + LANES]) * scale
            row = start + lax.broadcasted_iota(jnp.int32, (block, end), 0)
            col = lax.broadcasted_iota(jnp.int32, (block, end), 1)
            scores = jnp.where((col <= row) & (col < length), scores, masked_value)
            row_max = jnp.max(scores, axis=1, keepdims=True)
            weights = jnp.exp(scores - row_max)
            row_sum = jnp.sum(weights, axis=1, keepdims=True)
            probs = (weights * (1.0 / row_sum)).astype(bf16)
            att_ref[start:end, head * LANES : (head + 1) * LANES] = times(
                probs, qkv_ref[:end, v_at : v_at + LANES]
            )
            lse_ref[start:end, head : head + 1] = row_max + jnp.log(row_sum)
    saved += started(sems, 5, (att_ref, att_hbm), (lse_ref, lse_hbm))
    for i in range(C):
        rows = pl.ds(pl.multiple_of((me ^ i) * tokens, tokens), tokens)
        x = att_ref[rows, :]
        low = packed([x[:, h * LANES : (h + 1) * LANES] for h in range(q_heads)])
        at = (i % 2) * tokens
        block_refs[i // 2][at : at + tokens, :] = low[:, :width_low].astype(bf16)
    for copy in saved:
        copy.wait()


def attention_forward(blocks, w_parts, tables, me, length, line, q_heads, kv_heads):
    C, Z = len(blocks), len(w_parts)
    tokens, width = blocks[0].shape
    seq = C * tokens
    heads = q_heads + 2 * kv_heads
    cols = w_parts[0].shape[1]
    saved = [
        ((seq, width), bf16),
        ((width, cols), bf16),
        ((seq, heads * LANES), bf16),
        ((seq, q_heads * LANES), f32),
        ((seq, LANES), f32),
    ]
    part = jax.ShapeDtypeStruct((2 * tokens, q_heads * HEAD_DIM), bf16)
    result = pl.pallas_call(
        functools.partial(attention_forward_kernel, C, Z, tokens, q_heads, kv_heads, 2 * tokens),
        out_shape=[pltpu.HBM(*x) for x in saved] + [part] * (C // 2),
        in_specs=[SMEM] + [VMEM] * C + [HBM] * (Z + 2),
        out_specs=[HBM] * len(saved) + [VMEM] * (C // 2),
        scratch_shapes=[pltpu.VMEM(*saved[0]), pltpu.VMEM(*saved[1]), pltpu.VMEM((seq, cols), f32)]
        + [pltpu.VMEM(*x) for x in saved[2:]]
        + [pltpu.VMEM((seq, LANES), f32)] * 2
        + [pltpu.SemaphoreType.DMA((7 + Z,))],
        compiler_params=pltpu.CompilerParams(vmem_limit_bytes=22 * MIB),
        cost_estimate=cost(seq * width * cols + 2 * seq * seq * heads * LANES, 3 * seq * width),
        name="attention_forward",
    )(jnp.stack([me, length, line]).astype(jnp.int32), *blocks, *in_hbm(*w_parts, *tables))
    return result[: len(saved)], result[len(saved) :]


def attention_backward_kernel(C, tokens, q_heads, kv_heads, block, info_ref, *refs):
    R = C // 2
    mine_refs, other_refs = refs[:R], refs[R:C]
    hbm_refs = refs[C : C + 7]
    dqkv_ref, gain_ref = refs[C + 7 : C + 9]
    keep_refs = refs[C + 9 : C + 9 + R]
    give_refs = refs[C + 9 + R : C + 9 + C]
    refs = refs[C + 9 + C :]
    qkv_ref, att_ref, lse_ref, cos_ref, sin_ref, w_ref, n_all_ref = refs[:7]
    wide_ref, grad_ref, dq_ref, dkv_ref, sems = refs[7:]
    copies = started(sems, 0, *zip(hbm_refs, refs[:7], strict=True))
    me, length = info_ref[0], info_ref[1]
    core = me % 2
    seq = C * tokens
    group = q_heads // kv_heads
    width_low = q_heads * HEAD_DIM
    lane = lax.broadcasted_iota(jnp.int32, (tokens, LANES), 1)
    wide_ref[...] = jnp.zeros_like(wide_ref)
    for i in range(C):
        rows = pl.ds(pl.multiple_of((me ^ i) * tokens, tokens), tokens)
        wide_ref[:, : 2 * width_low] = (other_refs if i % 2 else mine_refs)[i // 2][...].astype(f32)
        wide = wide_ref[...]
        wide = jnp.where(core == 0, wide, pltpu.roll(wide, wide.shape[1] - width_low, 1))
        for head in range(q_heads):
            x = jnp.where(lane < HEAD_DIM, head_of(wide, head), 0.0)
            grad_ref[rows, head * LANES : (head + 1) * LANES] = x.astype(bf16)
    dkv_ref[...] = jnp.zeros_like(dkv_ref)
    scale = HEAD_DIM ** (-0.5)
    for copy in copies[:5]:
        copy.wait()
    for start in range(0, seq, block):
        end = start + block
        lane_b = lax.broadcasted_iota(jnp.int32, (block, LANES), 1)
        delta = jnp.zeros((block, LANES), f32)
        for head in range(q_heads):
            at = slice(head * LANES, (head + 1) * LANES)
            one = jnp.sum(
                grad_ref[start:end, at].astype(f32) * att_ref[start:end, at], axis=1, keepdims=True
            )
            delta = jnp.where(lane_b == head, one, delta)
        delta_t = delta.T
        lse_t = lse_ref[start:end, :].T
        key = lax.broadcasted_iota(jnp.int32, (end, block), 0)
        query = start + lax.broadcasted_iota(jnp.int32, (end, block), 1)
        allowed = (key <= query) & (key < length)
        for head in range(q_heads):
            at = slice(head * LANES, (head + 1) * LANES)
            kv = head // group
            k_at = slice((q_heads + kv) * LANES, (q_heads + kv + 1) * LANES)
            v_at = slice((q_heads + kv_heads + kv) * LANES, (q_heads + kv_heads + kv + 1) * LANES)
            q, grad = qkv_ref[start:end, at], grad_ref[start:end, at]
            k, v = qkv_ref[:end, k_at], qkv_ref[:end, v_at]
            scores = times_transposed(k, q) * scale
            probs = jnp.where(allowed, jnp.exp(scores - lse_t[head : head + 1, :]), 0.0)
            grad_probs = times_transposed(v, grad)
            grad_scores = (probs * (grad_probs - delta_t[head : head + 1, :])).astype(bf16)
            dq_ref[start:end, at] = transposed_times(grad_scores, k) * scale
            dk_at = slice(kv * LANES, (kv + 1) * LANES)
            dv_at = slice((kv_heads + kv) * LANES, (kv_heads + kv + 1) * LANES)
            dkv_ref[:end, dk_at] += times(grad_scores, q) * scale
            dkv_ref[:end, dv_at] += times(probs.astype(bf16), grad)
    for i in range(C):
        rows = pl.ds(pl.multiple_of((me ^ i) * tokens, tokens), tokens)
        cosines, sines = cos_ref[rows, :], sin_ref[rows, :]
        heads = []
        for head in range(q_heads + 2 * kv_heads):
            if head < q_heads:
                x = dq_ref[rows, head * LANES : (head + 1) * LANES]
            else:
                x = dkv_ref[rows, (head - q_heads) * LANES : (head - q_heads + 1) * LANES]
            if head < q_heads + kv_heads:
                x = x * cosines - turned(x) * sines
            heads.append(x)
        dqkv_ref[i * tokens : (i + 1) * tokens, :] = packed(heads).astype(bf16)
    for copy in copies[5:]:
        copy.wait()

    def rows_of(at):
        part = times_transposed(dqkv_ref[...], w_ref[at, :])
        gain = jnp.sum(part * n_all_ref[:, at].astype(f32), axis=0, keepdims=True)
        gain_ref[:, at] = jnp.broadcast_to(gain, (gain_ref.shape[0], gain.shape[1]))
        return part

    parts_of(rows_of, keep_refs, give_refs)


def attention_backward(mine, other, saved, tables, me, length, q_heads, kv_heads):
    C = 2 * len(mine)
    tokens, pair = mine[0].shape
    normed_all, w_qkv, qkv, attended, lse = saved
    width, cols = w_qkv.shape
    loaded = (qkv, attended, lse, *tables, w_qkv, normed_all)
    seq = C * tokens
    heads = q_heads + 2 * kv_heads
    part = jax.ShapeDtypeStruct((tokens, width), bf16)
    result = pl.pallas_call(
        functools.partial(attention_backward_kernel, C, tokens, q_heads, kv_heads, 2 * tokens),
        out_shape=[
            jax.ShapeDtypeStruct((seq, cols), bf16),
            jax.ShapeDtypeStruct((8, width), f32),
        ]
        + [part] * C,
        in_specs=[SMEM] + [VMEM] * C + [HBM] * 7,
        out_specs=[VMEM] * (C + 2),
        scratch_shapes=[pltpu.VMEM(x.shape, x.dtype) for x in loaded]
        + [
            pltpu.VMEM((tokens, -(-pair // LANES) * LANES), f32),
            pltpu.VMEM((seq, q_heads * LANES), bf16),
            pltpu.VMEM((seq, q_heads * LANES), f32),
            pltpu.VMEM((seq, 2 * kv_heads * LANES), f32),
            pltpu.SemaphoreType.DMA((7,)),
        ],
        compiler_params=pltpu.CompilerParams(vmem_limit_bytes=26 * MIB),
        cost_estimate=cost(seq * width * cols + 4 * seq * seq * heads * LANES, 3 * seq * width),
        name="attention_backward",
    )(jnp.stack([me, length]).astype(jnp.int32), *mine, *other, *in_hbm(*loaded))
    return result[0], result[1], result[2 : 2 + C // 2], result[2 + C // 2 :]


def gather_rows(block_refs, all_ref):
    tokens = block_refs[0].shape[0]

    @pl.loop(0, tokens // 16)
    def _(n):
        for i, ref in enumerate(block_refs):
            at = pl.ds(pl.multiple_of(n * 16, 16), 16)
            to = pl.ds(pl.multiple_of(i * tokens + n * 16, 16), 16)
            all_ref[to, :] = ref[at, :]


def parts_of(rows_of, keep_refs, give_refs):
    tokens, width = keep_refs[0].shape
    strip = 4 * LANES

    @pl.loop(0, width // strip)
    def _(n):
        at = pl.ds(pl.multiple_of(n * strip, strip), strip)
        part = rows_of(at)
        for i in range(2 * len(keep_refs)):
            ref = (give_refs if i % 2 else keep_refs)[i // 2]
            ref[:, at] = part[i * tokens : (i + 1) * tokens, :].astype(bf16)


def ffn_forward_kernel(C, cuts, *refs):
    n_refs = refs[:C]
    gu_hbm, down_hbm, n_hbm, act_hbm, coef_hbm = refs[C : C + 5]
    keep_refs = refs[C + 5 : C + 5 + C // 2]
    give_refs = refs[C + 5 + C // 2 : 2 * C + 5]
    gu_ref, down_ref, n_all_ref, act_ref, coef_ref, sems = refs[2 * C + 5 :]
    tokens = n_refs[0].shape[0]
    pairs = [(n_refs[i], n_all_ref.at[i * tokens : (i + 1) * tokens, :]) for i in range(C)]
    weights = started(sems, 3, (gu_hbm, gu_ref), (down_hbm, down_ref), *pairs)
    w = down_ref.shape[0] // cuts
    for copy in weights[2:]:
        copy.wait()
    saved = started(sems, 0, (n_all_ref, n_hbm))
    weights[0].wait()

    @pl.loop(0, cuts)
    def _(j):
        at = pl.ds(pl.multiple_of(j * 2 * w, 2 * w), 2 * w)
        both = times(n_all_ref[...], gu_ref[:, at])
        gate, up = both[:, :w], both[:, w:]
        sigmoid = jax.nn.sigmoid(gate)
        silu = gate * sigmoid
        act_ref[:, pl.ds(pl.multiple_of(j * w, w), w)] = (silu * up).astype(bf16)
        slope = up * (sigmoid * (1.0 + gate * (1.0 - sigmoid)))
        coef_ref[:, at] = jnp.concatenate([slope, silu], axis=1).astype(bf16)

    saved += started(sems, 1, (act_ref, act_hbm), (coef_ref, coef_hbm))
    weights[1].wait()
    parts_of(lambda at: times(act_ref[...], down_ref[:, at]), keep_refs, give_refs)
    for copy in saved:
        copy.wait()


def ffn_forward(blocks, gate_up, down, cuts):
    C = len(blocks)
    tokens, width = blocks[0].shape
    seq, own = C * tokens, down.shape[0]
    saved = [((seq, width), bf16), ((seq, own), bf16), ((seq, 2 * own), bf16)]
    part = jax.ShapeDtypeStruct((tokens, width), bf16)
    result = pl.pallas_call(
        functools.partial(ffn_forward_kernel, C, cuts),
        out_shape=[pltpu.HBM(*x) for x in saved] + [part] * C,
        in_specs=[HBM] * (C + 2),
        out_specs=[HBM] * 3 + [VMEM] * C,
        scratch_shapes=[
            pltpu.VMEM((width, 2 * own), bf16),
            pltpu.VMEM((own, width), bf16),
            *[pltpu.VMEM(*x) for x in saved],
            pltpu.SemaphoreType.DMA((5 + C,)),
        ],
        compiler_params=pltpu.CompilerParams(vmem_limit_bytes=24 * MIB),
        cost_estimate=cost(3 * seq * width * own, 3 * seq * width),
        name="ffn_forward",
    )(*in_hbm(*blocks, gate_up, down))
    return result[:3], result[3 : 3 + C // 2], result[3 + C // 2 :]


def ffn_backward_kernel(C, cuts, *refs):
    g_refs = refs[:C]
    gu_hbm, down_hbm, coef_hbm, g_all_ref, dgu_ref = refs[C : C + 5]
    keep_refs = refs[C + 5 : C + 5 + C // 2]
    give_refs = refs[C + 5 + C // 2 : 2 * C + 5]
    gu_ref, down_ref, coef_ref, sems = refs[2 * C + 5 :]
    copies = started(sems, 0, (down_hbm, down_ref), (coef_hbm, coef_ref), (gu_hbm, gu_ref))
    gather_rows(g_refs, g_all_ref)
    for copy in copies[:2]:
        copy.wait()
    w = down_ref.shape[0] // cuts
    many = 2 if cuts % 2 == 0 else 1

    @pl.loop(0, cuts // many)
    def _(j):
        rows = pl.ds(pl.multiple_of(j * many * w, many * w), many * w)
        grad_act = times_transposed(g_all_ref[...], down_ref[rows, :])
        at = pl.ds(pl.multiple_of(j * many * 2 * w, many * 2 * w), many * 2 * w)
        parts = [grad_act[:, (n // 2) * w : (n // 2 + 1) * w] for n in range(2 * many)]
        both = jnp.concatenate(parts, axis=1)
        dgu_ref[:, at] = (both * coef_ref[:, at].astype(f32)).astype(bf16)

    copies[2].wait()
    parts_of(lambda at: times_transposed(dgu_ref[...], gu_ref[at, :]), keep_refs, give_refs)


def ffn_backward(blocks, gate_up, down, coef, cuts):
    C = len(blocks)
    tokens, width = blocks[0].shape
    seq, own = C * tokens, coef.shape[1] // 2
    part = jax.ShapeDtypeStruct((tokens, width), bf16)
    result = pl.pallas_call(
        functools.partial(ffn_backward_kernel, C, cuts),
        out_shape=[
            jax.ShapeDtypeStruct((seq, width), bf16),
            jax.ShapeDtypeStruct((seq, 2 * own), bf16),
        ]
        + [part] * C,
        in_specs=[VMEM] * C + [HBM] * 3,
        out_specs=[VMEM] * (C + 2),
        scratch_shapes=[
            pltpu.VMEM((width, 2 * own), bf16),
            pltpu.VMEM((own, width), bf16),
            pltpu.VMEM(coef.shape, bf16),
            pltpu.SemaphoreType.DMA((3,)),
        ],
        compiler_params=pltpu.CompilerParams(vmem_limit_bytes=24 * MIB),
        cost_estimate=cost(3 * seq * width * own, 3 * seq * width),
        name="ffn_backward",
    )(*blocks, *in_hbm(gate_up, down, coef))
    return result[:2], result[2 : 2 + C // 2], result[2 + C // 2 :]


def ffn_slices_kernel(C, Z, piece, me_ref, gate_hbm, up_hbm, down_hbm, *refs):
    gu_hbm, rows_hbm, gu_ref, rows_ref, sems = refs
    me = me_ref[0]
    pairs = []
    for j in range(Z):
        for a, ref in enumerate((gate_hbm, up_hbm)):
            at = pl.multiple_of((j * C + me) * piece, piece)
            to = (2 * j + a) * piece
            pairs.append((ref.at[:, pl.ds(at, piece)], gu_ref.at[:, to : to + piece]))
    at = pl.multiple_of(me * piece, piece)
    pairs.append((down_hbm.at[pl.ds(at, piece), :], rows_ref))
    for copy in started(sems, 0, *pairs):
        copy.wait()
    for copy in started(sems, 0, (gu_ref, gu_hbm), (rows_ref, rows_hbm)):
        copy.wait()


def ffn_slices(w_gate, w_up, w_down, me, C, Z):
    rows, ff = w_gate.shape
    width = w_down.shape[1]
    piece = ff // (Z * C)
    shapes = (rows, 2 * Z * piece), (piece, width)
    return pl.pallas_call(
        functools.partial(ffn_slices_kernel, C, Z, piece),
        out_shape=[pltpu.HBM(x, bf16) for x in shapes],
        in_specs=[SMEM, HBM, HBM, HBM],
        out_specs=[HBM, HBM],
        scratch_shapes=[pltpu.VMEM(x, bf16) for x in shapes]
        + [pltpu.SemaphoreType.DMA((2 * Z + 1,))],
        compiler_params=pltpu.CompilerParams(vmem_limit_bytes=8 * MIB),
        cost_estimate=cost(0, 6 * rows * ff // C),
        name="ffn_slices",
    )(me.reshape(1), *in_hbm(w_gate, w_up, w_down))


def arrived(pieces, low_ref, sems):
    pairs = []
    for i, first, ref in pieces:
        pairs.append((ref, low_ref.at[i, pl.ds(first, ref.shape[0]), :]))
    copies = started(sems, 0, *pairs)
    return [[copy for copy, piece in zip(copies, pieces) if piece[0] == i] for i in range(low_ref.shape[0])]


def column_grads_kernel(C, Z, piece, places, me_ref, *refs):
    gate_hbm, up_hbm, low_ref, wide_ref, in_sems, sems = refs[len(places) :]
    me = me_ref[0]
    stride = gate_hbm.shape[1] // Z
    arriving = arrived([(*place, ref) for place, ref in zip(places, refs)], low_ref, in_sems)
    flying = [(), ()]
    for i in range(C):
        slot = i % 2
        for copy in (*flying[slot], *arriving[i]):
            copy.wait()

        @pl.loop(0, low_ref.shape[1] // 16)
        def _(n):
            at = pl.ds(pl.multiple_of(n * 16, 16), 16)
            wide_ref[slot, at, :] = low_ref[i, at, :].astype(f32)

        pairs = []
        for j in range(Z):
            at = pl.multiple_of(j * stride + (me ^ i) * piece, piece)
            for a, ref in enumerate((gate_hbm, up_hbm)):
                to = (2 * j + a) * piece
                pairs.append((wide_ref.at[slot, :, to : to + piece], ref.at[:, pl.ds(at, piece)]))
        flying[slot] = started(sems.at[slot], 0, *pairs)
    for copies in flying:
        for copy in copies:
            copy.wait()


def column_grads(pieces, me, C, Z):
    rows, cols = pieces[0][2].shape
    piece = cols // (2 * Z)
    ff = Z * C * piece
    return pl.pallas_call(
        functools.partial(column_grads_kernel, C, Z, piece, [x[:2] for x in pieces]),
        out_shape=[pltpu.HBM((rows, ff), f32)] * 2,
        in_specs=[SMEM] + [HBM] * len(pieces),
        out_specs=[HBM] * 2,
        scratch_shapes=[
            pltpu.VMEM((C, rows, cols), bf16),
            pltpu.VMEM((2, rows, cols), f32),
            pltpu.SemaphoreType.DMA((len(pieces),)),
            pltpu.SemaphoreType.DMA((2, 2 * Z)),
        ],
        compiler_params=pltpu.CompilerParams(vmem_limit_bytes=16 * MIB),
        cost_estimate=cost(0, 6 * rows * ff),
        name="column_grads",
    )(me.reshape(1), *in_hbm(*[x[2] for x in pieces]))


def row_grads_kernel(C, places, me_ref, *refs):
    out_hbm, low_ref, tall_ref, in_sems, sems = refs[len(places) :]
    me = me_ref[0]
    piece = low_ref.shape[1]
    arriving = arrived([(*place, ref) for place, ref in zip(places, refs)], low_ref, in_sems)
    flying = []
    for i in range(C):
        for copy in arriving[i]:
            copy.wait()

        @pl.loop(0, piece // 16)
        def _(n):
            at = pl.ds(pl.multiple_of(n * 16, 16), 16)
            tall_ref[i, at, :] = low_ref[i, at, :].astype(f32)

        at = pl.multiple_of((me ^ i) * piece, piece)
        flying += started(sems, i, (tall_ref.at[i], out_hbm.at[pl.ds(at, piece), :]))
    for copy in flying:
        copy.wait()


def row_grads(pieces, me, C):
    piece, width = pieces[0][2].shape
    return pl.pallas_call(
        functools.partial(row_grads_kernel, C, [x[:2] for x in pieces]),
        out_shape=pltpu.HBM((C * piece, width), f32),
        in_specs=[SMEM] + [HBM] * len(pieces),
        out_specs=HBM,
        scratch_shapes=[
            pltpu.VMEM((C, piece, width), bf16),
            pltpu.VMEM((C, piece, width), f32),
            pltpu.SemaphoreType.DMA((len(pieces),)),
            pltpu.SemaphoreType.DMA((C,)),
        ],
        compiler_params=pltpu.CompilerParams(vmem_limit_bytes=16 * MIB),
        cost_estimate=cost(0, 4 * C * piece * width),
        name="row_grads",
    )(me.reshape(1), *in_hbm(*[x[2] for x in pieces]))


def middle_forward_kernel(C, Z, piece, info_ref, *refs):
    R = C // 2
    mine_refs, other_refs, w_refs = refs[:R], refs[R:C], refs[C : 2 * C]
    own_hbm, hidden_ref, gain_ref = refs[2 * C : 2 * C + 3]
    middle_ref, normed_ref, att_ref, out_hbm = refs[2 * C + 3 : 2 * C + 7]
    out_ref, low_ref, high_ref, sems = refs[2 * C + 7 :]
    me, line = info_ref[0], info_ref[1]
    rows_z = C * piece
    own_at = pl.ds(pl.multiple_of(line * rows_z, rows_z), rows_z)
    here = started(sems, 1, (own_hbm, out_ref.at[own_at, :]))
    core = me % 2
    tokens, half = hidden_ref.shape[0], mine_refs[0].shape[1]
    cols = w_refs[0].shape[1]
    strips = out_ref.shape[1] // cols
    for i in range(C):
        for j in range(1, Z):
            at = pl.multiple_of((line ^ j) * rows_z + (me ^ i) * piece, piece)
            for c in range(strips):
                first = ((j - 1) * strips + c) * piece
                out_ref[pl.ds(at, piece), c * cols : (c + 1) * cols] = w_refs[i][first : first + piece, :]
    for copy in here:
        copy.wait()
    saved = started(sems, 0, (out_ref, out_hbm))
    low_ref[...] = jnp.zeros_like(low_ref)
    high_ref[...] = jnp.zeros_like(high_ref)
    for s in range(R):
        own = mine_refs[s][:tokens, :].astype(f32)
        other = other_refs[s][tokens:, :].astype(f32)
        low_ref[:, :half] = jnp.where(core == 0, own, other)
        high_ref[:, :half] = jnp.where(core == 0, other, own)
        pair = low_ref[...] + pltpu.roll(high_ref[...], half, 1)
        at = pl.multiple_of(((me // 2) ^ s) * 2 * half, 2 * half)
        att_ref[:, pl.ds(at, 2 * half)] = pair.astype(bf16)
    middle = hidden_ref[...] + times(att_ref[...], out_ref[...])
    middle_ref[...] = middle
    normed_ref[...] = (middle * norm_scale(middle) * gain_ref[...]).astype(bf16)
    for copy in saved:
        copy.wait()


def middle_forward(mine, other, w_blocks, w_own, hidden, gain, me, line, Z):
    C = len(w_blocks)
    tokens, width = hidden.shape
    half = mine[0].shape[1]
    cols = w_blocks[0].shape[1]
    strips = width // cols
    piece = w_own.shape[0] // C
    if piece % 16 or (2 * half) % LANES:
        rows = [x.reshape(Z - 1, strips, piece, cols).transpose(0, 2, 1, 3) for x in w_blocks]
        rows = jnp.stack(unsort([x.reshape(Z - 1, piece, width) for x in rows], me), axis=1)
        rows = jnp.concatenate([w_own[None], rows.reshape(Z - 1, C * piece, width)])
        out_all = jnp.concatenate([pick(rows, line ^ j) for j in range(Z)], axis=0)
        heads = []
        for a, b in zip(mine, other, strict=True):
            heads += [a[:tokens], b[tokens:]]
        attended = jnp.concatenate(unsort(heads, me), axis=1)
        middle = hidden + times(attended, out_all)
        return middle, (middle * norm_scale(middle) * gain).astype(bf16), attended, out_all
    return pl.pallas_call(
        functools.partial(middle_forward_kernel, C, Z, piece),
        out_shape=[
            jax.ShapeDtypeStruct((tokens, width), f32),
            jax.ShapeDtypeStruct((tokens, width), bf16),
            jax.ShapeDtypeStruct((tokens, width), bf16),
            pltpu.HBM((width, width), bf16),
        ],
        in_specs=[SMEM] + [VMEM] * 2 * C + [HBM] + [VMEM] * 2,
        out_specs=[VMEM] * 3 + [HBM],
        scratch_shapes=[
            pltpu.VMEM((width, width), bf16),
            pltpu.VMEM((tokens, 2 * half), f32),
            pltpu.VMEM((tokens, 2 * half), f32),
            pltpu.SemaphoreType.DMA((2,)),
        ],
        compiler_params=pltpu.CompilerParams(vmem_limit_bytes=16 * MIB),
        cost_estimate=cost(tokens * width * width, 3 * width * width),
        name="middle_forward",
    )(jnp.stack([me, line]), *mine, *other, *w_blocks, *in_hbm(w_own), hidden, gain.reshape(1, width))


def middle_backward_kernel(R, info_ref, *refs):
    own_ref, got_refs = refs[0], refs[1:R]
    middle_ref, gain_ref, grad_out_ref, out_hbm = refs[R : R + 4]
    grad_ref, low_ref, gain_grad_ref = refs[R + 4 : R + 7]
    pair_refs, (att_ref, out_ref, sems) = refs[R + 7 : 2 * R + 7], refs[2 * R + 7 :]
    copies = started(sems, 0, (out_hbm, out_ref))
    upstream = own_ref[...]
    for ref in got_refs:
        upstream = upstream + ref[...].astype(f32)
    middle = middle_ref[...]
    back, gain_grad = norm_back(upstream, middle, norm_scale(middle), gain_ref[...])
    gain_grad_ref[...] = gain_grad.reshape(gain_grad_ref.shape)
    grad = grad_out_ref[...] + back
    grad_ref[...] = grad
    low = grad.astype(bf16)
    low_ref[...] = low
    for copy in copies:
        copy.wait()
    att_ref[...] = times_transposed(low, out_ref[...]).astype(bf16)
    pair_cols = pair_refs[0].shape[1]
    for s in range(R):
        at = pl.multiple_of(((info_ref[0] // 2) ^ s) * pair_cols, pair_cols)
        pair_refs[s][...] = att_ref[:, pl.ds(at, pair_cols)]


def middle_backward(own, got, middle, gain, grad_output, out_all, me):
    R = len(got) + 1
    tokens, width = middle.shape
    pair_cols = width // R
    if pair_cols % LANES:
        upstream = total(own, got)
        back, gain_grad = norm_back(upstream, middle, norm_scale(middle), gain)
        grad = grad_output + back
        low = grad.astype(bf16)
        cut = times_transposed(low, out_all).astype(bf16).reshape(tokens, R, pair_cols)
        return grad, low, gain_grad[None], *[pick(cut, (me // 2) ^ s, 1) for s in range(R)]
    result = pl.pallas_call(
        functools.partial(middle_backward_kernel, R),
        out_shape=[
            jax.ShapeDtypeStruct((tokens, width), f32),
            jax.ShapeDtypeStruct((tokens, width), bf16),
            jax.ShapeDtypeStruct((1, width), f32),
        ]
        + [pltpu.VMEM((tokens, pair_cols), bf16)] * R,
        in_specs=[SMEM] + [VMEM] * (R + 3) + [HBM],
        out_specs=[VMEM] * (3 + R),
        scratch_shapes=[
            pltpu.VMEM((tokens, width), bf16),
            pltpu.VMEM((width, width), bf16),
            pltpu.SemaphoreType.DMA((1,)),
        ],
        compiler_params=pltpu.CompilerParams(vmem_limit_bytes=16 * MIB),
        cost_estimate=cost(tokens * width * width, 3 * width * width),
        name="middle_backward",
    )(me.reshape(1), own, *got, middle, gain.reshape(1, width), grad_output, *in_hbm(out_all))
    return result


def out_grads_kernel(C, Z, piece, info_ref, att_ref, low_ref, *refs):
    keep_refs, give_refs, sum_ref = refs[: C // 2], refs[C // 2 : C], refs[C]
    me = info_ref[0]
    rows_z = C * piece
    sum_ref[...] = transposed_times(att_ref[...], low_ref[...])
    for i in range(C):
        ref = (give_refs if i % 2 else keep_refs)[i // 2]
        for j in range(Z):
            at = pl.multiple_of(j * rows_z + (me ^ i) * piece, piece)
            ref[j * piece : (j + 1) * piece, :] = sum_ref[pl.ds(at, piece), :].astype(bf16)


def out_grads(attended, low, me, C, Z):
    width = attended.shape[1]
    piece = width // (C * Z)
    if piece % 16:
        grad = transposed_times(attended, low).astype(bf16).reshape(Z, C, piece, width)
        grad = [pick(grad, me ^ i, 1).reshape(Z * piece, width) for i in range(C)]
        return grad[0::2], grad[1::2]
    result = pl.pallas_call(
        functools.partial(out_grads_kernel, C, Z, piece),
        out_shape=[pltpu.VMEM((Z * piece, width), bf16)] * C,
        in_specs=[SMEM, VMEM, VMEM],
        out_specs=[VMEM] * C,
        scratch_shapes=[pltpu.VMEM((width, width), f32)],
        compiler_params=pltpu.CompilerParams(vmem_limit_bytes=18 * MIB),
        cost_estimate=cost(2 * attended.shape[0] * width * width, 3 * width * width),
        name="out_grads",
    )(me.reshape(1), attended, low)
    return result[: C // 2], result[C // 2 :]


EXTRA = 16


def attention_packs_kernel(Z, C, info_ref, *refs):
    R = C // 2
    n_hbm, dqkv_ref, out_refs = refs[0], refs[1], refs[2 : R + 2]
    gain_one_ref, gain_two_ref, error_ref, pack_hbm = refs[R + 2 : R + 6]
    n_ref, sum_ref, tall_ref, sems = refs[R + 6 :]
    arriving = started(sems, 0, (n_hbm, n_ref))
    width, cols = n_ref.shape[1], tall_ref.shape[1]
    rows, tall = width // Z, tall_ref.shape[0] // Z
    piece = sum_ref.shape[0] // Z
    out = out_refs[0][...]
    for ref in out_refs[1:]:
        out = out + ref[...].astype(f32)
    sum_ref[...] = out.astype(bf16)
    line = info_ref[0]
    row = lax.broadcasted_iota(jnp.int32, (EXTRA, cols), 0)
    lane = lax.broadcasted_iota(jnp.int32, (EXTRA, cols), 1)
    error = error_ref[0, 0]
    high = error.astype(bf16).astype(f32)
    error = jnp.where(lane == 2 * line, high, jnp.where(lane == 2 * line + 1, error - high, 0.0))
    for j in range(Z):
        under = j * tall + rows
        for n in range(width // cols):
            at = slice(n * cols, (n + 1) * cols)
            tall_ref[under + n * piece : under + (n + 1) * piece, :] = sum_ref[
                j * piece : (j + 1) * piece, at
            ]
        at = slice(j * rows, (j + 1) * rows)
        extra = jnp.where(row == 0, gain_one_ref[0:1, at], jnp.where(row == 1, gain_two_ref[0:1, at], 0.0))
        extra = jnp.where(row == 2, error, extra)
        tall_ref[(j + 1) * tall - EXTRA : (j + 1) * tall, :] = extra.astype(bf16)
    for copy in arriving:
        copy.wait()

    @pl.loop(0, Z)
    def _(j):
        at = pl.ds(pl.multiple_of(j * rows, LANES), rows)
        to = pl.ds(pl.multiple_of(j * tall, 16), rows)
        tall_ref[to, :] = transposed_times(n_ref[:, at], dqkv_ref[...]).astype(bf16)

    for copy in started(sems, 0, (tall_ref, pack_hbm)):
        copy.wait()


def attention_packs(normed_all, grad_qkv, out_parts, gain_one, gain_two, error, line, Z, C):
    width = normed_all.shape[1]
    cols = grad_qkv.shape[1]
    rows = width // Z
    tall, parts = out_parts[0].shape[0], C // 2
    piece = tall // Z
    if rows != cols or piece % 16:
        grad = transposed_times(normed_all, grad_qkv).astype(bf16)
        grad_out = total(out_parts[0], out_parts[1:]).astype(bf16)
        lane = jnp.arange(cols, dtype=jnp.int32)
        high = error.astype(bf16)
        low = (error - high.astype(f32)).astype(bf16)
        zero = jnp.zeros((), bf16)
        error_row = jnp.where(lane == 2 * line, high, jnp.where(lane == 2 * line + 1, low, zero))
        packs = []
        for j in range(Z):
            at = slice(j * rows, (j + 1) * rows)
            out = grad_out[j * piece : (j + 1) * piece]
            gains = [jnp.pad(x[at].astype(bf16), (0, cols - rows)) for x in (gain_one[0], gain_two[0])]
            extra = jnp.pad(jnp.stack([*gains, error_row]), ((0, EXTRA - 3), (0, 0)))
            packs += [grad[at], *[out[:, c : c + cols] for c in range(0, width, cols)], extra]
        return jnp.concatenate(packs, axis=0)
    shape = (Z * (rows + piece * width // cols + EXTRA), cols)
    return pl.pallas_call(
        functools.partial(attention_packs_kernel, Z, C),
        out_shape=pltpu.HBM(shape, bf16),
        in_specs=[SMEM, HBM] + [VMEM] * (parts + 4),
        out_specs=HBM,
        scratch_shapes=[
            pltpu.VMEM(normed_all.shape, bf16),
            pltpu.VMEM((tall, width), bf16),
            pltpu.VMEM(shape, bf16),
            pltpu.SemaphoreType.DMA((1,)),
        ],
        compiler_params=pltpu.CompilerParams(vmem_limit_bytes=16 * MIB),
        cost_estimate=cost(normed_all.shape[0] * width * cols, 3 * width * width),
        name="attention_packs",
    )(line.reshape(1), *in_hbm(normed_all), grad_qkv, *out_parts, gain_one, gain_two, error.reshape(1, 1))


def attention_grads_kernel(C, rows, q_cols, kv_cols, places, me_ref, *refs):
    count = len(places)
    gain_ref, valid_ref = refs[count : count + 2]
    query_ref, key_ref, value_ref, out_ref, gains_ref, loss_ref = refs[count + 2 : count + 8]
    low_ref, sort_ref, extra_ref, in_sems = refs[count + 8 :]
    me = me_ref[0]
    cols = sort_ref.shape[2]
    strips = out_ref.shape[1] // cols
    piece = (low_ref.shape[1] - rows - EXTRA) // strips
    arriving = arrived([(*place, ref) for place, ref in zip(places, refs)], low_ref, in_sems)
    for i in range(C):
        for copy in arriving[i]:
            copy.wait()

        @pl.loop(0, rows // 16)
        def _(n):
            rows_n = pl.ds(pl.multiple_of(n * 16, 16), 16)
            sort_ref[me ^ i, rows_n, :] = low_ref[i, rows_n, :].astype(f32)

        at = pl.ds(pl.multiple_of((me ^ i) * piece, piece), piece)
        for c in range(strips):
            strip = low_ref[i, rows + c * piece : rows + (c + 1) * piece, :]
            out_ref[at, c * cols : (c + 1) * cols] = strip.astype(f32)
        extra_ref[me ^ i] = low_ref[i, low_ref.shape[1] - EXTRA :, :].astype(f32)
    extra = extra_ref[0]
    for b in range(1, C):
        extra = extra + extra_ref[b]
    row = lax.broadcasted_iota(jnp.int32, gains_ref.shape, 0)
    gains_ref[...] = extra[:8, :] / jnp.where(row == 0, gain_ref[...], 1.0)
    loss_ref[...] = jnp.sum(extra[2:3, :], axis=1, keepdims=True) / valid_ref[0, 0]
    lane = lax.broadcasted_iota(jnp.int32, sort_ref.shape[1:], 1)
    for ref, first, size in (
        (query_ref, 0, q_cols),
        (key_ref, q_cols, kv_cols),
        (value_ref, q_cols + kv_cols, kv_cols),
    ):
        many = cols // size
        for group in range(C // many):
            whole = None
            for j in range(many):
                x = sort_ref[group * many + j]
                shift = (j * size - first) % cols
                x = pltpu.roll(x, shift, 1) if shift else x
                whole = x if whole is None else jnp.where(lane < j * size, whole, x)
            ref[:, group * cols : (group + 1) * cols] = whole


def attention_grads(pieces, me, gain, valid_count, C, rows, width, q_cols, kv_cols, kv_copies):
    tall, cols = pieces[0][2].shape
    strips = width // cols
    piece = (tall - rows - EXTRA) // strips
    many = C // kv_copies
    if kv_copies > 1 or cols % q_cols or cols % kv_cols or q_cols + 2 * kv_cols != cols or rows != cols or piece % 16:
        parts = unsort([x[2] for x in pieces], me)

        def kv_final(start):
            own = [part[:rows, start : start + kv_cols].astype(f32) for part in parts]
            own = [sum(own[n : n + kv_copies]) for n in range(0, C, kv_copies)]
            return jnp.concatenate(own, axis=1)

        query = jnp.concatenate([part[:rows, :q_cols] for part in parts], axis=1).astype(f32)
        outs = [part[rows : tall - EXTRA].reshape(strips, piece, cols).transpose(1, 0, 2) for part in parts]
        out = jnp.concatenate([x.reshape(piece, width) for x in outs], axis=0).astype(f32)
        extra = sum([part[tall - EXTRA :].astype(f32) for part in parts])
        gains = extra[0, :rows] / gain, extra[1, :rows]
        loss = jnp.sum(extra[2]) / valid_count
        return query, kv_final(q_cols), kv_final(q_cols + kv_cols), out, *gains, loss
    *grads, gains, loss = pl.pallas_call(
        functools.partial(
            attention_grads_kernel, C, rows, q_cols, kv_cols, [x[:2] for x in pieces]
        ),
        out_shape=[
            jax.ShapeDtypeStruct((rows, C * q_cols), f32),
            jax.ShapeDtypeStruct((rows, many * kv_cols), f32),
            jax.ShapeDtypeStruct((rows, many * kv_cols), f32),
            jax.ShapeDtypeStruct((C * piece, width), f32),
            jax.ShapeDtypeStruct((8, cols), f32),
            jax.ShapeDtypeStruct((1, 1), f32),
        ],
        in_specs=[SMEM] + [HBM] * len(pieces) + [VMEM] * 2,
        out_specs=[VMEM] * 6,
        scratch_shapes=[
            pltpu.VMEM((C, tall, cols), bf16),
            pltpu.VMEM((C, rows, cols), f32),
            pltpu.VMEM((C, EXTRA, cols), f32),
            pltpu.SemaphoreType.DMA((len(pieces),)),
        ],
        compiler_params=pltpu.CompilerParams(vmem_limit_bytes=24 * MIB),
        cost_estimate=cost(0, 8 * rows * C * cols),
        name="attention_grads",
    )(
        me.reshape(1),
        *in_hbm(*[x[2] for x in pieces]),
        gain.reshape(1, rows),
        valid_count.reshape(1, 1),
    )
    return *grads, gains[0], gains[1], loss[0, 0]


def local(
    inputs,
    teacher,
    lengths,
    w_query,
    w_key,
    w_value,
    w_out,
    w_gate,
    w_up,
    w_down,
    gain_attn,
    gain_ffn,
):
    hidden_in = inputs[0]
    target = teacher[0]
    seq_length = lengths[0]
    tokens, width = hidden_in.shape
    C = lax.axis_size("ctx")
    Z = lax.axis_size("fsdp")
    R = C // 2
    p = lax.axis_index("ctx")
    z = lax.axis_index("fsdp")
    core = p % 2
    rows_z = width // Z
    seq = C * tokens
    q_heads = HEADS // C
    kv_heads = max(1, KV_HEADS // C)
    kv_copies = max(1, C // KV_HEADS)
    q_cols = q_heads * HEAD_DIM
    kv_cols = kv_heads * HEAD_DIM
    qkv_cols = q_cols + 2 * kv_cols
    positions = p * tokens + jnp.arange(tokens, dtype=jnp.int32)

    small = jnp.concatenate(
        [gain_attn.astype(f32), gain_ffn.astype(f32), jnp.full((LANES,), seq_length).astype(f32)]
    )
    small = jnp.stack(unsort(line_blocks(small.reshape(1, -1)), z)).reshape(Z, -1)
    gain_one = small[:, :rows_z].reshape(width)
    gain_two = small[:, rows_z : 2 * rows_z].reshape(width)
    valid_count = jnp.sum(small[:, 2 * rows_z])
    ff = w_gate.shape[1]
    ff_piece, own = ff // (Z * C), ff // C
    packed_ffn = ff_piece % LANES == 0
    if packed_ffn:
        cuts = Z
        gate_up_own, down_own = ffn_slices(w_gate, w_up, w_down, p, C, Z)
    else:
        cuts = 1
        gate_up_own = jnp.concatenate(
            [pick(w.reshape(rows_z, Z, C, ff_piece), p, 2).reshape(rows_z, own) for w in (w_gate, w_up)],
            axis=1,
        )
        down_own = lax.dynamic_slice_in_dim(w_down, p * ff_piece, ff_piece, 0)
    kv_start = (p * KV_HEADS // C) * HEAD_DIM
    out_piece = rows_z // C
    qkv_own = jnp.concatenate(
        [
            lax.dynamic_slice_in_dim(w_query, p * q_cols, q_cols, 1),
            lax.dynamic_slice_in_dim(w_key, kv_start, kv_cols, 1),
            lax.dynamic_slice_in_dim(w_value, kv_start, kv_cols, 1),
            jnp.zeros((rows_z, -qkv_cols % LANES), bf16),
        ],
        axis=1,
    )
    out_own = lax.dynamic_slice_in_dim(w_out, p * out_piece, out_piece, 0)
    cols = qkv_own.shape[1]
    out_own = jnp.concatenate([out_own[:, c : c + cols] for c in range(0, width, cols)], axis=0)

    scale_one = norm_scale(hidden_in)
    normed_one = (hidden_in * scale_one * gain_one).astype(bf16)
    weights_own = jnp.concatenate([qkv_own, out_own], axis=0)
    tables = rope_tables(seq)
    normed_got, weights, tables = lax.optimization_barrier(
        (plane_sends(normed_one), line_sends(weights_own), tables)
    )
    normed_blocks = together(core_blocks([normed_one] + normed_got))
    gate_up_own, down_own = after((gate_up_own, down_own), weights)
    gate_up = lax.all_gather(gate_up_own, "fsdp", axis=0, tiled=True)
    down_rows = lax.all_gather(down_own, "fsdp", axis=0, tiled=True)
    out_line = jnp.concatenate([x[rows_z:] for x in weights], axis=0)
    out_got = plane_sends(out_line)
    (normed_all, *saved), mine = attention_forward(
        normed_blocks, [weights_own] + weights, tables, p, seq_length, z, q_heads, kv_heads
    )

    out_blocks = together(core_blocks([out_line] + after(out_got, normed_all)))
    mine = after(mine, out_blocks)
    mine = [mine[0]] + together([partner(mine[s], "ctx", 2 * s) for s in range(1, R)])
    other = [partner(x, "ctx", 1) for x in mine]
    middle, normed_two_own, attended_tokens, out_all = middle_forward(
        mine, other, out_blocks, w_out, hidden_in, gain_two, p, z, Z
    )

    normed_two_blocks = plane_blocks(normed_two_own)
    (normed_two, activated, coef), keep, give = ffn_forward(
        normed_two_blocks, gate_up, down_rows, cuts
    )
    output = middle + plane_reduce(keep, give)

    valid_rows = (positions < seq_length).astype(f32)
    residual_error = output - target
    squares = jnp.sum(valid_rows[:, None] * residual_error * residual_error)
    grad_output = valid_rows[:, None] * (2.0 * residual_error) / valid_count

    (grad_low, grad_gu), keep, give = ffn_backward(
        plane_blocks(grad_output.astype(bf16)), gate_up, down_rows, coef, cuts
    )
    chips = chip_sums(keep, give)
    grad_gate_up = transposed_times(normed_two, after(grad_gu, chips)).astype(bf16)
    grad_down = transposed_times(activated, after(grad_low, grad_gate_up)).astype(bf16)
    shard_gate_up = lax.psum_scatter(grad_gate_up, "fsdp", scatter_dimension=0, tiled=True)
    shard_down = lax.psum_scatter(grad_down, "fsdp", scatter_dimension=0, tiled=True)
    grad_middle, m_low, grad_gain_two, *pairs = middle_backward(
        chips[0], after(chip_sends(chips), grad_down), middle, gain_two, grad_output, out_all, p
    )

    out_keep, out_give = out_grads(attended_tokens, after(m_low, pairs), p, C, Z)
    mine = [pairs[0]] + together([partner(pairs[s], "ctx", 2 * s) for s in range(1, R)])
    other = [partner(x, "ctx", 1) for x in mine]
    out_chips = chip_sums(out_keep, out_give)
    mine = after(mine, out_chips)
    grad_qkv, gain_part, keep, give = attention_backward(
        mine, other, (normed_all, *saved), tables, p, seq_length, q_heads, kv_heads
    )
    chips = chip_sums(keep, give)
    square = packed_ffn and C == 8
    out_got, grad_qkv = lax.optimization_barrier((chip_sends(out_chips), grad_qkv))
    packs = attention_packs(
        normed_all, grad_qkv, [out_chips[0]] + out_got, gain_part, grad_gain_two, squares, z, Z, C
    )
    shard_packs = lax.psum_scatter(packs, "fsdp", scatter_dimension=0, tiled=True)
    normed_got = [partner(x, "ctx", 2 * (s + 1)) for s, x in enumerate(after(chips[1:], out_got))]
    near = near_sends(after(shard_gate_up, out_got)) if square else []
    normed_got, near = lax.optimization_barrier((normed_got, near))
    grad_normed_one = total(chips[0], normed_got)
    back_one, _ = norm_back(grad_normed_one, hidden_in, scale_one, gain_one)
    grad_hidden = grad_middle + back_one


    if square:
        down_sent = after(shard_down, normed_got)
        far, down_got = lax.optimization_barrier((far_sends(near), plane_sends(down_sent)))
        pieces = square_pieces(shard_gate_up, near, far)
        down_blocks = together(core_blocks([shard_down] + down_got))
        pack_got = plane_sends(after(shard_packs, down_blocks))
        final_gate, final_up = column_grads(pieces, p, C, Z)
        final_down = row_grads([(i, 0, x) for i, x in enumerate(down_blocks)], p, C)
        pack_got, final_gate, final_down = lax.optimization_barrier((pack_got, final_gate, final_down))
        pack_blocks = together(core_blocks([shard_packs] + pack_got))
    else:
        pack_blocks = plane_blocks(shard_packs)
        gate_up, down = [
            jnp.stack(unsort(plane_blocks(x), p)).astype(f32) for x in (shard_gate_up, shard_down)
        ]
        gate_up = gate_up.reshape(C, rows_z, 2, Z, ff_piece).transpose(2, 1, 3, 0, 4)
        final_gate, final_up = gate_up.reshape(2, rows_z, ff)
        final_down = down.reshape(C * ff_piece, width)
    pieces = [(i, 0, block) for i, block in enumerate(pack_blocks)]
    final_query, final_key, final_value, final_out, *final_gains, loss_value = attention_grads(
        pieces,
        p,
        gain_attn.astype(f32),
        valid_count,
        C,
        rows_z,
        width,
        q_cols,
        kv_cols,
        kv_copies,
    )

    return (
        output[None],
        loss_value,
        grad_hidden[None],
        final_query,
        final_key,
        final_value,
        final_out,
        final_gate,
        final_up,
        final_down,
        *final_gains,
    )


def solution(mesh):
    return jax.shard_map(
        local,
        mesh=mesh,
        in_specs=(
            P("fsdp", "ctx", None),
            P("fsdp", "ctx", None),
            P("fsdp"),
            P("fsdp", None),
            P("fsdp", None),
            P("fsdp", None),
            P("fsdp", None),
            P("fsdp", None),
            P("fsdp", None),
            P("fsdp", None),
            P("fsdp"),
            P("fsdp"),
        ),
        out_specs=(
            P("fsdp", "ctx", None),
            P(),
            P("fsdp", "ctx", None),
            P("fsdp", None),
            P("fsdp", None),
            P("fsdp", None),
            P("fsdp", None),
            P("fsdp", None),
            P("fsdp", None),
            P("fsdp", None),
            P("fsdp"),
            P("fsdp"),
        ),
        check_vma=False,
    )
```

```python
import functools

import jax
import jax.numpy as jnp
from jax import lax
from jax.experimental import pallas as pl
from jax.experimental.pallas import tpu as pltpu
from jax.sharding import PartitionSpec as P

HEADS = 16
KV_HEADS = 8
HEAD_DIM = 96
LANES = 128

eps_norm = 1e-05
rope_base = 100000.0
masked_value = -1e30

f32 = jnp.float32
bf16 = jnp.bfloat16

VMEM = pl.BlockSpec(memory_space=pltpu.VMEM)
SMEM = pl.BlockSpec(memory_space=pltpu.SMEM)
HBM = pl.BlockSpec(memory_space=pltpu.HBM)
MIB = 1024 * 1024


def cost(multiply_adds, values):
    return pl.CostEstimate(flops=1, bytes_accessed=1, transcendentals=0)


def in_hbm(*xs):
    return [pltpu.with_memory_space_constraint(x, pltpu.HBM) for x in xs]


def started(sems, first, *pairs):
    copies = [pltpu.make_async_copy(a, b, sems.at[first + n]) for n, (a, b) in enumerate(pairs)]
    for copy in copies:
        copy.start()
    return copies


def times(left, right):
    return jnp.dot(left, right, preferred_element_type=f32)


def times_transposed(left, right):
    return lax.dot_general(left, right, (((1,), (1,)), ((), ())), preferred_element_type=f32)


def transposed_times(left, right):
    return lax.dot_general(left, right, (((0,), (0,)), ((), ())), preferred_element_type=f32)


def norm_scale(features):
    return lax.rsqrt(jnp.mean(features * features, axis=-1, keepdims=True) + eps_norm)


def norm_back(upstream, features, row_scale, gain_vector):
    weighted = upstream * gain_vector
    inner_mean = jnp.mean(weighted * features, axis=-1, keepdims=True)
    grad_rows = row_scale * weighted - features * (row_scale * row_scale * row_scale) * inner_mean
    return (grad_rows, jnp.sum(upstream * (features * row_scale), axis=0))


def partner(x, axis, mask):
    return lax.ppermute(x, axis, [(i, i ^ mask) for i in range(lax.axis_size(axis))])


def plane_sends(x):
    return [partner(x, "ctx", 2 * s) for s in range(1, lax.axis_size("ctx") // 2)]


def core_blocks(mine):
    blocks = []
    for x in mine:
        blocks += [x, partner(x, "ctx", 1)]
    return blocks


def plane_blocks(x):
    return core_blocks([x] + plane_sends(x))


def near_sends(x):
    return [partner(x, "ctx", 2), partner(x, "ctx", 4)]


def far_sends(near):
    half = near[0].shape[0] // 32 * 16
    return [partner(near[0][:half], "ctx", 4), partner(near[1][half:], "ctx", 2)]


def square_pieces(x, near, far):
    half = x.shape[0] // 32 * 16
    mine = [(0, 0, x), (1, 0, near[0]), (2, 0, near[1]), (3, 0, far[0]), (3, half, far[1])]
    other = together([partner(block, "ctx", 1) for _, _, block in mine])
    pieces = []
    for (s, first, block), swapped in zip(mine, other, strict=True):
        pieces += [(2 * s, first, block), (2 * s + 1, first, swapped)]
    return pieces


def line_sends(x):
    return [partner(x, "fsdp", s) for s in range(1, lax.axis_size("fsdp"))]


def plane_reduce(keep, give):
    chips = chip_sums(keep, give)
    return total(chips[0], chip_sends(chips))


def chip_sums(keep, give):
    got = [partner(x, "ctx", 1) for x in give[::-1]][::-1]
    own = keep[0].astype(f32) + got[0].astype(f32)
    return [own] + [
        (a.astype(f32) + b.astype(f32)).astype(bf16) for a, b in zip(keep[1:], got[1:], strict=True)
    ]


def chip_sends(chips):
    return together([partner(chips[s], "ctx", 2 * s) for s in range(len(chips) - 1, 0, -1)])


def total(own, got):
    for x in got:
        own = own + x.astype(f32)
    return own


def tree_sum(x, axis):
    mask = 1
    while mask < lax.axis_size(axis):
        x = x + partner(x, axis, mask)
        mask *= 2
    return x


def line_blocks(x):
    return [x] + together(line_sends(x))


def line_reduce(parts):
    got = together([partner(parts[s], "fsdp", s) for s in range(1, len(parts))])
    return total(parts[0].astype(f32), got)


def together(xs):
    return list(lax.optimization_barrier(tuple(xs)))


def after(x, *done):
    return lax.optimization_barrier((x, done))[0]


def pick(x, index, axis=0):
    return lax.dynamic_index_in_dim(x, index, axis, False)


def unsort(blocks, me):
    stacked = jnp.stack(blocks)
    return [pick(stacked, me ^ b) for b in range(len(blocks))]


def rope_tables(count):
    half_dim = HEAD_DIM // 2
    frequencies = rope_base ** (-(jnp.arange(half_dim, dtype=f32) * 2.0) / HEAD_DIM)
    angles = jnp.arange(count, dtype=f32)[:, None] * frequencies[None, :]
    cosines, sines = jnp.cos(angles), jnp.sin(angles)
    pad = jnp.zeros((count, LANES - HEAD_DIM), f32)
    return (
        jnp.concatenate([cosines, cosines, pad], axis=1),
        jnp.concatenate([-sines, sines, pad], axis=1),
    )


def turned(x):
    lane = lax.broadcasted_iota(jnp.int32, x.shape, 1)
    half_dim = HEAD_DIM // 2
    return jnp.where(
        lane < half_dim, pltpu.roll(x, LANES - half_dim, 1), pltpu.roll(x, half_dim, 1)
    )


def head_of(x, head):
    if head:
        x = pltpu.roll(x, x.shape[1] - head * HEAD_DIM, 1)
    return x[:, :LANES]


def packed(heads):
    wide = -(-len(heads) * HEAD_DIM // LANES) * LANES
    total = None
    for index, head in enumerate(heads):
        if wide > LANES:
            head = jnp.concatenate([head, jnp.zeros((head.shape[0], wide - LANES), f32)], axis=1)
        if index:
            head = pltpu.roll(head, index * HEAD_DIM, 1)
        total = head if total is None else total + head
    return total


def attention_forward_kernel(C, Z, tokens, q_heads, kv_heads, block, info_ref, *refs):
    R = C // 2
    n_refs, w_parts = refs[:C], refs[C : C + Z]
    cos_hbm, sin_hbm = refs[C + Z : C + Z + 2]
    n_hbm, w_hbm, qkv_hbm, att_hbm, lse_hbm = refs[C + Z + 2 : C + Z + 7]
    block_refs = refs[C + Z + 7 : C + Z + 7 + R]
    n_all_ref, w_ref, lin_ref, qkv_ref, att_ref, lse_ref, cos_ref, sin_ref, sems = refs[C + Z + 7 + R :]
    me, length = info_ref[0], info_ref[1]
    seq = C * tokens
    group = q_heads // kv_heads
    width_low = q_heads * HEAD_DIM
    rows_z = w_ref.shape[0] // Z
    pairs = []
    for j in range(Z):
        at = pl.multiple_of((info_ref[2] ^ j) * rows_z, rows_z)
        pairs.append((w_parts[j].at[:rows_z, :], w_ref.at[pl.ds(at, rows_z), :]))
    tables = started(sems, 0, (cos_hbm, cos_ref), (sin_hbm, sin_ref), *pairs)
    for i in range(C):
        n_all_ref[i * tokens : (i + 1) * tokens, :] = n_refs[i][...]
    for copy in tables[2:]:
        copy.wait()
    saved = started(sems, 2, (n_all_ref, n_hbm), (w_ref, w_hbm))
    step = 4 * tokens
    for start in range(0, seq, step):
        lin_ref[start : start + step, :] = times(n_all_ref[start : start + step, :], w_ref[...])
    for copy in tables[:2]:
        copy.wait()
    lane = lax.broadcasted_iota(jnp.int32, (tokens, LANES), 1)
    for i in range(C):
        rows = pl.ds(pl.multiple_of((me ^ i) * tokens, tokens), tokens)
        lin = lin_ref[i * tokens : (i + 1) * tokens, :]
        cosines, sines = cos_ref[rows, :], sin_ref[rows, :]
        for head in range(q_heads + 2 * kv_heads):
            x = head_of(lin, head)
            if head < q_heads + kv_heads:
                x = x * cosines + turned(x) * sines
            else:
                x = jnp.where(lane < HEAD_DIM, x, 0.0)
            qkv_ref[rows, head * LANES : (head + 1) * LANES] = x.astype(bf16)
    saved += started(sems, 4, (qkv_ref, qkv_hbm))
    scale = HEAD_DIM ** (-0.5)
    for head in range(q_heads):
        k_at = (q_heads + head // group) * LANES
        v_at = k_at + kv_heads * LANES
        for start in range(0, seq, block):
            end = start + block
            q = qkv_ref[start:end, head * LANES : (head + 1) * LANES]
            scores = times_transposed(q, qkv_ref[:end, k_at : k_at + LANES]) * scale
            row = start + lax.broadcasted_iota(jnp.int32, (block, end), 0)
            col = lax.broadcasted_iota(jnp.int32, (block, end), 1)
            scores = jnp.where((col <= row) & (col < length), scores, masked_value)
            row_max = jnp.max(scores, axis=1, keepdims=True)
            weights = jnp.exp(scores - row_max)
            row_sum = jnp.sum(weights, axis=1, keepdims=True)
            probs = (weights * (1.0 / row_sum)).astype(bf16)
            att_ref[start:end, head * LANES : (head + 1) * LANES] = times(
                probs, qkv_ref[:end, v_at : v_at + LANES]
            )
            lse_ref[start:end, head : head + 1] = row_max + jnp.log(row_sum)
    saved += started(sems, 5, (att_ref, att_hbm), (lse_ref, lse_hbm))
    for i in range(C):
        rows = pl.ds(pl.multiple_of((me ^ i) * tokens, tokens), tokens)
        x = att_ref[rows, :]
        low = packed([x[:, h * LANES : (h + 1) * LANES] for h in range(q_heads)])
        at = (i % 2) * tokens
        block_refs[i // 2][at : at + tokens, :] = low[:, :width_low].astype(bf16)
    for copy in saved:
        copy.wait()


def attention_forward(blocks, w_parts, tables, me, length, line, q_heads, kv_heads):
    C, Z = len(blocks), len(w_parts)
    tokens, width = blocks[0].shape
    seq = C * tokens
    heads = q_heads + 2 * kv_heads
    cols = w_parts[0].shape[1]
    saved = [
        ((seq, width), bf16),
        ((width, cols), bf16),
        ((seq, heads * LANES), bf16),
        ((seq, q_heads * LANES), f32),
        ((seq, LANES), f32),
    ]
    part = jax.ShapeDtypeStruct((2 * tokens, q_heads * HEAD_DIM), bf16)
    result = pl.pallas_call(
        functools.partial(attention_forward_kernel, C, Z, tokens, q_heads, kv_heads, 2 * tokens),
        out_shape=[pltpu.HBM(*x) for x in saved] + [part] * (C // 2),
        in_specs=[SMEM] + [VMEM] * C + [HBM] * (Z + 2),
        out_specs=[HBM] * len(saved) + [VMEM] * (C // 2),
        scratch_shapes=[pltpu.VMEM(*saved[0]), pltpu.VMEM(*saved[1]), pltpu.VMEM((seq, cols), f32)]
        + [pltpu.VMEM(*x) for x in saved[2:]]
        + [pltpu.VMEM((seq, LANES), f32)] * 2
        + [pltpu.SemaphoreType.DMA((7 + Z,))],
        compiler_params=pltpu.CompilerParams(vmem_limit_bytes=22 * MIB),
        cost_estimate=cost(seq * width * cols + 2 * seq * seq * heads * LANES, 3 * seq * width),
        name="attention_forward",
    )(jnp.stack([me, length, line]).astype(jnp.int32), *blocks, *in_hbm(*w_parts, *tables))
    return result[: len(saved)], result[len(saved) :]


def attention_backward_kernel(C, tokens, q_heads, kv_heads, block, info_ref, *refs):
    R = C // 2
    mine_refs, other_refs = refs[:R], refs[R:C]
    hbm_refs = refs[C : C + 7]
    grad_w_ref, gain_ref = refs[C + 7 : C + 9]
    keep_refs = refs[C + 9 : C + 9 + R]
    give_refs = refs[C + 9 + R : C + 9 + C]
    refs = refs[C + 9 + C :]
    qkv_ref, att_ref, lse_ref, cos_ref, sin_ref, w_ref, n_all_ref = refs[:7]
    wide_ref, grad_ref, dq_ref, dkv_ref, dqkv_ref, sems = refs[7:]
    copies = started(sems, 0, *zip(hbm_refs, refs[:7], strict=True))
    me, length = info_ref[0], info_ref[1]
    core = me % 2
    seq = C * tokens
    group = q_heads // kv_heads
    width_low = q_heads * HEAD_DIM
    lane = lax.broadcasted_iota(jnp.int32, (tokens, LANES), 1)
    wide_ref[...] = jnp.zeros_like(wide_ref)
    for i in range(C):
        rows = pl.ds(pl.multiple_of((me ^ i) * tokens, tokens), tokens)
        wide_ref[:, : 2 * width_low] = (other_refs if i % 2 else mine_refs)[i // 2][...].astype(f32)
        wide = wide_ref[...]
        wide = jnp.where(core == 0, wide, pltpu.roll(wide, wide.shape[1] - width_low, 1))
        for head in range(q_heads):
            x = jnp.where(lane < HEAD_DIM, head_of(wide, head), 0.0)
            grad_ref[rows, head * LANES : (head + 1) * LANES] = x.astype(bf16)
    dkv_ref[...] = jnp.zeros_like(dkv_ref)
    scale = HEAD_DIM ** (-0.5)
    for copy in copies[:5]:
        copy.wait()
    for start in range(0, seq, block):
        end = start + block
        lane_b = lax.broadcasted_iota(jnp.int32, (block, LANES), 1)
        delta = jnp.zeros((block, LANES), f32)
        for head in range(q_heads):
            at = slice(head * LANES, (head + 1) * LANES)
            one = jnp.sum(
                grad_ref[start:end, at].astype(f32) * att_ref[start:end, at], axis=1, keepdims=True
            )
            delta = jnp.where(lane_b == head, one, delta)
        delta_t = delta.T
        lse_t = lse_ref[start:end, :].T
        key = lax.broadcasted_iota(jnp.int32, (end, block), 0)
        query = start + lax.broadcasted_iota(jnp.int32, (end, block), 1)
        allowed = (key <= query) & (key < length)
        for head in range(q_heads):
            at = slice(head * LANES, (head + 1) * LANES)
            kv = head // group
            k_at = slice((q_heads + kv) * LANES, (q_heads + kv + 1) * LANES)
            v_at = slice((q_heads + kv_heads + kv) * LANES, (q_heads + kv_heads + kv + 1) * LANES)
            q, grad = qkv_ref[start:end, at], grad_ref[start:end, at]
            k, v = qkv_ref[:end, k_at], qkv_ref[:end, v_at]
            scores = times_transposed(k, q) * scale
            probs = jnp.where(allowed, jnp.exp(scores - lse_t[head : head + 1, :]), 0.0)
            grad_probs = times_transposed(v, grad)
            grad_scores = (probs * (grad_probs - delta_t[head : head + 1, :])).astype(bf16)
            dq_ref[start:end, at] = transposed_times(grad_scores, k) * scale
            dk_at = slice(kv * LANES, (kv + 1) * LANES)
            dv_at = slice((kv_heads + kv) * LANES, (kv_heads + kv + 1) * LANES)
            dkv_ref[:end, dk_at] += times(grad_scores, q) * scale
            dkv_ref[:end, dv_at] += times(probs.astype(bf16), grad)
    for i in range(C):
        rows = pl.ds(pl.multiple_of((me ^ i) * tokens, tokens), tokens)
        cosines, sines = cos_ref[rows, :], sin_ref[rows, :]
        heads = []
        for head in range(q_heads + 2 * kv_heads):
            if head < q_heads:
                x = dq_ref[rows, head * LANES : (head + 1) * LANES]
            else:
                x = dkv_ref[rows, (head - q_heads) * LANES : (head - q_heads + 1) * LANES]
            if head < q_heads + kv_heads:
                x = x * cosines - turned(x) * sines
            heads.append(x)
        dqkv_ref[i * tokens : (i + 1) * tokens, :] = packed(heads).astype(bf16)
    for copy in copies[5:]:
        copy.wait()

    def rows_of(at):
        part = times_transposed(dqkv_ref[...], w_ref[at, :])
        gain = jnp.sum(part * n_all_ref[:, at].astype(f32), axis=0, keepdims=True)
        gain_ref[:, at] = jnp.broadcast_to(gain, (gain_ref.shape[0], gain.shape[1]))
        return part

    parts_of(rows_of, keep_refs, give_refs)
    step = 3 * LANES

    @pl.loop(0, grad_w_ref.shape[0] // step)
    def _(n):
        at = pl.ds(pl.multiple_of(n * step, step), step)
        grad_w_ref[at, :] = transposed_times(n_all_ref[:, at], dqkv_ref[...]).astype(bf16)


def attention_backward(mine, other, saved, tables, me, length, q_heads, kv_heads):
    C = 2 * len(mine)
    tokens, pair = mine[0].shape
    normed_all, w_qkv, qkv, attended, lse = saved
    width, cols = w_qkv.shape
    loaded = (qkv, attended, lse, *tables, w_qkv, normed_all)
    seq = C * tokens
    heads = q_heads + 2 * kv_heads
    part = jax.ShapeDtypeStruct((tokens, width), bf16)
    result = pl.pallas_call(
        functools.partial(attention_backward_kernel, C, tokens, q_heads, kv_heads, 2 * tokens),
        out_shape=[
            jax.ShapeDtypeStruct((width, cols), bf16),
            jax.ShapeDtypeStruct((8, width), f32),
        ]
        + [part] * C,
        in_specs=[SMEM] + [VMEM] * C + [HBM] * 7,
        out_specs=[VMEM] * (C + 2),
        scratch_shapes=[pltpu.VMEM(x.shape, x.dtype) for x in loaded]
        + [
            pltpu.VMEM((tokens, -(-pair // LANES) * LANES), f32),
            pltpu.VMEM((seq, q_heads * LANES), bf16),
            pltpu.VMEM((seq, q_heads * LANES), f32),
            pltpu.VMEM((seq, 2 * kv_heads * LANES), f32),
            pltpu.VMEM((seq, cols), bf16),
            pltpu.SemaphoreType.DMA((7,)),
        ],
        compiler_params=pltpu.CompilerParams(vmem_limit_bytes=28 * MIB),
        cost_estimate=cost(seq * width * cols + 4 * seq * seq * heads * LANES, 3 * seq * width),
        name="attention_backward",
    )(jnp.stack([me, length]).astype(jnp.int32), *mine, *other, *in_hbm(*loaded))
    return result[0], result[1], result[2 : 2 + C // 2], result[2 + C // 2 :]


def gather_rows(block_refs, all_ref):
    tokens = block_refs[0].shape[0]

    @pl.loop(0, tokens // 16)
    def _(n):
        for i, ref in enumerate(block_refs):
            at = pl.ds(pl.multiple_of(n * 16, 16), 16)
            to = pl.ds(pl.multiple_of(i * tokens + n * 16, 16), 16)
            all_ref[to, :] = ref[at, :]


def parts_of(rows_of, keep_refs, give_refs):
    tokens, width = keep_refs[0].shape
    strip = 4 * LANES

    @pl.loop(0, width // strip)
    def _(n):
        at = pl.ds(pl.multiple_of(n * strip, strip), strip)
        part = rows_of(at)
        for i in range(2 * len(keep_refs)):
            ref = (give_refs if i % 2 else keep_refs)[i // 2]
            ref[:, at] = part[i * tokens : (i + 1) * tokens, :].astype(bf16)


def ffn_forward_kernel(C, cuts, *refs):
    n_refs = refs[:C]
    gu_hbm, down_hbm, n_hbm, act_hbm, coef_hbm = refs[C : C + 5]
    keep_refs = refs[C + 5 : C + 5 + C // 2]
    give_refs = refs[C + 5 + C // 2 : 2 * C + 5]
    gu_ref, down_ref, n_all_ref, act_ref, coef_ref, sems = refs[2 * C + 5 :]
    tokens = n_refs[0].shape[0]
    pairs = [(n_refs[i], n_all_ref.at[i * tokens : (i + 1) * tokens, :]) for i in range(C)]
    weights = started(sems, 3, (gu_hbm, gu_ref), (down_hbm, down_ref), *pairs)
    w = down_ref.shape[0] // cuts
    for copy in weights[2:]:
        copy.wait()
    saved = started(sems, 0, (n_all_ref, n_hbm))
    weights[0].wait()

    @pl.loop(0, cuts)
    def _(j):
        at = pl.ds(pl.multiple_of(j * 2 * w, 2 * w), 2 * w)
        both = times(n_all_ref[...], gu_ref[:, at])
        gate, up = both[:, :w], both[:, w:]
        sigmoid = jax.nn.sigmoid(gate)
        silu = gate * sigmoid
        act_ref[:, pl.ds(pl.multiple_of(j * w, w), w)] = (silu * up).astype(bf16)
        slope = up * (sigmoid * (1.0 + gate * (1.0 - sigmoid)))
        coef_ref[:, at] = jnp.concatenate([slope, silu], axis=1).astype(bf16)

    saved += started(sems, 1, (act_ref, act_hbm), (coef_ref, coef_hbm))
    weights[1].wait()
    parts_of(lambda at: times(act_ref[...], down_ref[:, at]), keep_refs, give_refs)
    for copy in saved:
        copy.wait()


def ffn_forward(blocks, gate_up, down, cuts):
    C = len(blocks)
    tokens, width = blocks[0].shape
    seq, own = C * tokens, down.shape[0]
    saved = [((seq, width), bf16), ((seq, own), bf16), ((seq, 2 * own), bf16)]
    part = jax.ShapeDtypeStruct((tokens, width), bf16)
    result = pl.pallas_call(
        functools.partial(ffn_forward_kernel, C, cuts),
        out_shape=[pltpu.HBM(*x) for x in saved] + [part] * C,
        in_specs=[HBM] * (C + 2),
        out_specs=[HBM] * 3 + [VMEM] * C,
        scratch_shapes=[
            pltpu.VMEM((width, 2 * own), bf16),
            pltpu.VMEM((own, width), bf16),
            *[pltpu.VMEM(*x) for x in saved],
            pltpu.SemaphoreType.DMA((5 + C,)),
        ],
        compiler_params=pltpu.CompilerParams(vmem_limit_bytes=24 * MIB),
        cost_estimate=cost(3 * seq * width * own, 3 * seq * width),
        name="ffn_forward",
    )(*in_hbm(*blocks, gate_up, down))
    return result[:3], result[3 : 3 + C // 2], result[3 + C // 2 :]


def ffn_backward_kernel(C, cuts, *refs):
    g_refs = refs[:C]
    gu_hbm, down_hbm, coef_hbm, g_all_ref, dgu_ref = refs[C : C + 5]
    keep_refs = refs[C + 5 : C + 5 + C // 2]
    give_refs = refs[C + 5 + C // 2 : 2 * C + 5]
    gu_ref, down_ref, coef_ref, sems = refs[2 * C + 5 :]
    copies = started(sems, 0, (down_hbm, down_ref), (coef_hbm, coef_ref), (gu_hbm, gu_ref))
    gather_rows(g_refs, g_all_ref)
    for copy in copies[:2]:
        copy.wait()
    w = down_ref.shape[0] // cuts
    many = 2 if cuts % 2 == 0 else 1

    @pl.loop(0, cuts // many)
    def _(j):
        rows = pl.ds(pl.multiple_of(j * many * w, many * w), many * w)
        grad_act = times_transposed(g_all_ref[...], down_ref[rows, :])
        at = pl.ds(pl.multiple_of(j * many * 2 * w, many * 2 * w), many * 2 * w)
        parts = [grad_act[:, (n // 2) * w : (n // 2 + 1) * w] for n in range(2 * many)]
        both = jnp.concatenate(parts, axis=1)
        dgu_ref[:, at] = (both * coef_ref[:, at].astype(f32)).astype(bf16)

    copies[2].wait()
    parts_of(lambda at: times_transposed(dgu_ref[...], gu_ref[at, :]), keep_refs, give_refs)


def ffn_backward(blocks, gate_up, down, coef, cuts):
    C = len(blocks)
    tokens, width = blocks[0].shape
    seq, own = C * tokens, coef.shape[1] // 2
    part = jax.ShapeDtypeStruct((tokens, width), bf16)
    result = pl.pallas_call(
        functools.partial(ffn_backward_kernel, C, cuts),
        out_shape=[
            jax.ShapeDtypeStruct((seq, width), bf16),
            jax.ShapeDtypeStruct((seq, 2 * own), bf16),
        ]
        + [part] * C,
        in_specs=[VMEM] * C + [HBM] * 3,
        out_specs=[VMEM] * (C + 2),
        scratch_shapes=[
            pltpu.VMEM((width, 2 * own), bf16),
            pltpu.VMEM((own, width), bf16),
            pltpu.VMEM(coef.shape, bf16),
            pltpu.SemaphoreType.DMA((3,)),
        ],
        compiler_params=pltpu.CompilerParams(vmem_limit_bytes=24 * MIB),
        cost_estimate=cost(3 * seq * width * own, 3 * seq * width),
        name="ffn_backward",
    )(*blocks, *in_hbm(gate_up, down, coef))
    return result[:2], result[2 : 2 + C // 2], result[2 + C // 2 :]


def ffn_slices_kernel(C, Z, piece, me_ref, gate_hbm, up_hbm, down_hbm, *refs):
    gu_hbm, rows_hbm, gu_ref, rows_ref, sems = refs
    me = me_ref[0]
    pairs = []
    for j in range(Z):
        for a, ref in enumerate((gate_hbm, up_hbm)):
            at = pl.multiple_of((j * C + me) * piece, piece)
            to = (2 * j + a) * piece
            pairs.append((ref.at[:, pl.ds(at, piece)], gu_ref.at[:, to : to + piece]))
    at = pl.multiple_of(me * piece, piece)
    pairs.append((down_hbm.at[pl.ds(at, piece), :], rows_ref))
    for copy in started(sems, 0, *pairs):
        copy.wait()
    for copy in started(sems, 0, (gu_ref, gu_hbm), (rows_ref, rows_hbm)):
        copy.wait()


def ffn_slices(w_gate, w_up, w_down, me, C, Z):
    rows, ff = w_gate.shape
    width = w_down.shape[1]
    piece = ff // (Z * C)
    shapes = (rows, 2 * Z * piece), (piece, width)
    return pl.pallas_call(
        functools.partial(ffn_slices_kernel, C, Z, piece),
        out_shape=[pltpu.HBM(x, bf16) for x in shapes],
        in_specs=[SMEM, HBM, HBM, HBM],
        out_specs=[HBM, HBM],
        scratch_shapes=[pltpu.VMEM(x, bf16) for x in shapes]
        + [pltpu.SemaphoreType.DMA((2 * Z + 1,))],
        compiler_params=pltpu.CompilerParams(vmem_limit_bytes=8 * MIB),
        cost_estimate=cost(0, 6 * rows * ff // C),
        name="ffn_slices",
    )(me.reshape(1), *in_hbm(w_gate, w_up, w_down))


def arrived(pieces, low_ref, sems):
    pairs = []
    for i, first, ref in pieces:
        pairs.append((ref, low_ref.at[i, pl.ds(first, ref.shape[0]), :]))
    copies = started(sems, 0, *pairs)
    return [[copy for copy, piece in zip(copies, pieces) if piece[0] == i] for i in range(low_ref.shape[0])]


def column_grads_kernel(C, Z, piece, places, me_ref, *refs):
    gate_hbm, up_hbm, low_ref, wide_ref, in_sems, sems = refs[len(places) :]
    me = me_ref[0]
    stride = gate_hbm.shape[1] // Z
    arriving = arrived([(*place, ref) for place, ref in zip(places, refs)], low_ref, in_sems)
    flying = [(), ()]
    for i in range(C):
        slot = i % 2
        for copy in (*flying[slot], *arriving[i]):
            copy.wait()

        @pl.loop(0, low_ref.shape[1] // 16)
        def _(n):
            at = pl.ds(pl.multiple_of(n * 16, 16), 16)
            wide_ref[slot, at, :] = low_ref[i, at, :].astype(f32)

        pairs = []
        for j in range(Z):
            at = pl.multiple_of(j * stride + (me ^ i) * piece, piece)
            for a, ref in enumerate((gate_hbm, up_hbm)):
                to = (2 * j + a) * piece
                pairs.append((wide_ref.at[slot, :, to : to + piece], ref.at[:, pl.ds(at, piece)]))
        flying[slot] = started(sems.at[slot], 0, *pairs)
    for copies in flying:
        for copy in copies:
            copy.wait()


def column_grads(pieces, me, C, Z):
    rows, cols = pieces[0][2].shape
    piece = cols // (2 * Z)
    ff = Z * C * piece
    return pl.pallas_call(
        functools.partial(column_grads_kernel, C, Z, piece, [x[:2] for x in pieces]),
        out_shape=[pltpu.HBM((rows, ff), f32)] * 2,
        in_specs=[SMEM] + [HBM] * len(pieces),
        out_specs=[HBM] * 2,
        scratch_shapes=[
            pltpu.VMEM((C, rows, cols), bf16),
            pltpu.VMEM((2, rows, cols), f32),
            pltpu.SemaphoreType.DMA((len(pieces),)),
            pltpu.SemaphoreType.DMA((2, 2 * Z)),
        ],
        compiler_params=pltpu.CompilerParams(vmem_limit_bytes=16 * MIB),
        cost_estimate=cost(0, 6 * rows * ff),
        name="column_grads",
    )(me.reshape(1), *in_hbm(*[x[2] for x in pieces]))


def row_grads_kernel(C, places, me_ref, *refs):
    out_hbm, low_ref, tall_ref, in_sems, sems = refs[len(places) :]
    me = me_ref[0]
    piece = low_ref.shape[1]
    arriving = arrived([(*place, ref) for place, ref in zip(places, refs)], low_ref, in_sems)
    flying = []
    for i in range(C):
        for copy in arriving[i]:
            copy.wait()

        @pl.loop(0, piece // 16)
        def _(n):
            at = pl.ds(pl.multiple_of(n * 16, 16), 16)
            tall_ref[i, at, :] = low_ref[i, at, :].astype(f32)

        at = pl.multiple_of((me ^ i) * piece, piece)
        flying += started(sems, i, (tall_ref.at[i], out_hbm.at[pl.ds(at, piece), :]))
    for copy in flying:
        copy.wait()


def row_grads(pieces, me, C):
    piece, width = pieces[0][2].shape
    return pl.pallas_call(
        functools.partial(row_grads_kernel, C, [x[:2] for x in pieces]),
        out_shape=pltpu.HBM((C * piece, width), f32),
        in_specs=[SMEM] + [HBM] * len(pieces),
        out_specs=HBM,
        scratch_shapes=[
            pltpu.VMEM((C, piece, width), bf16),
            pltpu.VMEM((C, piece, width), f32),
            pltpu.SemaphoreType.DMA((len(pieces),)),
            pltpu.SemaphoreType.DMA((C,)),
        ],
        compiler_params=pltpu.CompilerParams(vmem_limit_bytes=16 * MIB),
        cost_estimate=cost(0, 4 * C * piece * width),
        name="row_grads",
    )(me.reshape(1), *in_hbm(*[x[2] for x in pieces]))


def middle_forward_kernel(C, Z, piece, info_ref, *refs):
    R = C // 2
    mine_refs, other_refs, w_refs = refs[:R], refs[R:C], refs[C : 2 * C]
    own_hbm, hidden_ref, gain_ref = refs[2 * C : 2 * C + 3]
    middle_ref, normed_ref, att_ref, out_hbm = refs[2 * C + 3 : 2 * C + 7]
    out_ref, low_ref, high_ref, sems = refs[2 * C + 7 :]
    me, line = info_ref[0], info_ref[1]
    rows_z = C * piece
    own_at = pl.ds(pl.multiple_of(line * rows_z, rows_z), rows_z)
    here = started(sems, 1, (own_hbm, out_ref.at[own_at, :]))
    core = me % 2
    tokens, half = hidden_ref.shape[0], mine_refs[0].shape[1]
    for i in range(C):
        for j in range(1, Z):
            at = pl.multiple_of((line ^ j) * rows_z + (me ^ i) * piece, piece)
            out_ref[pl.ds(at, piece), :] = w_refs[i][(j - 1) * piece : j * piece, :]
    for copy in here:
        copy.wait()
    saved = started(sems, 0, (out_ref, out_hbm))
    low_ref[...] = jnp.zeros_like(low_ref)
    high_ref[...] = jnp.zeros_like(high_ref)
    for s in range(R):
        own = mine_refs[s][:tokens, :].astype(f32)
        other = other_refs[s][tokens:, :].astype(f32)
        low_ref[:, :half] = jnp.where(core == 0, own, other)
        high_ref[:, :half] = jnp.where(core == 0, other, own)
        pair = low_ref[...] + pltpu.roll(high_ref[...], half, 1)
        at = pl.multiple_of(((me // 2) ^ s) * 2 * half, 2 * half)
        att_ref[:, pl.ds(at, 2 * half)] = pair.astype(bf16)
    middle = hidden_ref[...] + times(att_ref[...], out_ref[...])
    middle_ref[...] = middle
    normed_ref[...] = (middle * norm_scale(middle) * gain_ref[...]).astype(bf16)
    for copy in saved:
        copy.wait()


def middle_forward(mine, other, w_blocks, w_own, hidden, gain, me, line, Z):
    C = len(w_blocks)
    tokens, width = hidden.shape
    half = mine[0].shape[1]
    piece = w_own.shape[0] // C
    if piece % 16 or (2 * half) % LANES:
        rows = jnp.stack(unsort([x.reshape(Z - 1, piece, width) for x in w_blocks], me), axis=1)
        rows = jnp.concatenate([w_own[None], rows.reshape(Z - 1, C * piece, width)])
        out_all = jnp.concatenate([pick(rows, line ^ j) for j in range(Z)], axis=0)
        heads = []
        for a, b in zip(mine, other, strict=True):
            heads += [a[:tokens], b[tokens:]]
        attended = jnp.concatenate(unsort(heads, me), axis=1)
        middle = hidden + times(attended, out_all)
        return middle, (middle * norm_scale(middle) * gain).astype(bf16), attended, out_all
    return pl.pallas_call(
        functools.partial(middle_forward_kernel, C, Z, piece),
        out_shape=[
            jax.ShapeDtypeStruct((tokens, width), f32),
            jax.ShapeDtypeStruct((tokens, width), bf16),
            jax.ShapeDtypeStruct((tokens, width), bf16),
            pltpu.HBM((width, width), bf16),
        ],
        in_specs=[SMEM] + [VMEM] * 2 * C + [HBM] + [VMEM] * 2,
        out_specs=[VMEM] * 3 + [HBM],
        scratch_shapes=[
            pltpu.VMEM((width, width), bf16),
            pltpu.VMEM((tokens, 2 * half), f32),
            pltpu.VMEM((tokens, 2 * half), f32),
            pltpu.SemaphoreType.DMA((2,)),
        ],
        compiler_params=pltpu.CompilerParams(vmem_limit_bytes=16 * MIB),
        cost_estimate=cost(tokens * width * width, 3 * width * width),
        name="middle_forward",
    )(jnp.stack([me, line]), *mine, *other, *w_blocks, *in_hbm(w_own), hidden, gain.reshape(1, width))


def middle_backward_kernel(R, info_ref, *refs):
    own_ref, got_refs = refs[0], refs[1:R]
    middle_ref, gain_ref, grad_out_ref, out_hbm = refs[R : R + 4]
    grad_ref, low_ref, gain_grad_ref = refs[R + 4 : R + 7]
    pair_refs, (att_ref, out_ref, sems) = refs[R + 7 : 2 * R + 7], refs[2 * R + 7 :]
    copies = started(sems, 0, (out_hbm, out_ref))
    upstream = own_ref[...]
    for ref in got_refs:
        upstream = upstream + ref[...].astype(f32)
    middle = middle_ref[...]
    back, gain_grad = norm_back(upstream, middle, norm_scale(middle), gain_ref[...])
    gain_grad_ref[...] = gain_grad.reshape(gain_grad_ref.shape)
    grad = grad_out_ref[...] + back
    grad_ref[...] = grad
    low = grad.astype(bf16)
    low_ref[...] = low
    for copy in copies:
        copy.wait()
    att_ref[...] = times_transposed(low, out_ref[...]).astype(bf16)
    pair_cols = pair_refs[0].shape[1]
    for s in range(R):
        at = pl.multiple_of(((info_ref[0] // 2) ^ s) * pair_cols, pair_cols)
        pair_refs[s][...] = att_ref[:, pl.ds(at, pair_cols)]


def middle_backward(own, got, middle, gain, grad_output, out_all, me):
    R = len(got) + 1
    tokens, width = middle.shape
    pair_cols = width // R
    if pair_cols % LANES:
        upstream = total(own, got)
        back, gain_grad = norm_back(upstream, middle, norm_scale(middle), gain)
        grad = grad_output + back
        low = grad.astype(bf16)
        cut = times_transposed(low, out_all).astype(bf16).reshape(tokens, R, pair_cols)
        return grad, low, gain_grad[None], *[pick(cut, (me // 2) ^ s, 1) for s in range(R)]
    result = pl.pallas_call(
        functools.partial(middle_backward_kernel, R),
        out_shape=[
            jax.ShapeDtypeStruct((tokens, width), f32),
            jax.ShapeDtypeStruct((tokens, width), bf16),
            jax.ShapeDtypeStruct((1, width), f32),
        ]
        + [pltpu.VMEM((tokens, pair_cols), bf16)] * R,
        in_specs=[SMEM] + [VMEM] * (R + 3) + [HBM],
        out_specs=[VMEM] * (3 + R),
        scratch_shapes=[
            pltpu.VMEM((tokens, width), bf16),
            pltpu.VMEM((width, width), bf16),
            pltpu.SemaphoreType.DMA((1,)),
        ],
        compiler_params=pltpu.CompilerParams(vmem_limit_bytes=16 * MIB),
        cost_estimate=cost(tokens * width * width, 3 * width * width),
        name="middle_backward",
    )(me.reshape(1), own, *got, middle, gain.reshape(1, width), grad_output, *in_hbm(out_all))
    return result


def out_grads_kernel(C, Z, piece, info_ref, att_ref, low_ref, *refs):
    keep_refs, give_refs, sum_ref = refs[: C // 2], refs[C // 2 : C], refs[C]
    me = info_ref[0]
    rows_z = C * piece
    sum_ref[...] = transposed_times(att_ref[...], low_ref[...])
    for i in range(C):
        ref = (give_refs if i % 2 else keep_refs)[i // 2]
        for j in range(Z):
            at = pl.multiple_of(j * rows_z + (me ^ i) * piece, piece)
            ref[j * piece : (j + 1) * piece, :] = sum_ref[pl.ds(at, piece), :].astype(bf16)


def out_grads(attended, low, me, C, Z):
    width = attended.shape[1]
    piece = width // (C * Z)
    if piece % 16:
        grad = transposed_times(attended, low).astype(bf16).reshape(Z, C, piece, width)
        grad = [pick(grad, me ^ i, 1).reshape(Z * piece, width) for i in range(C)]
        return grad[0::2], grad[1::2]
    result = pl.pallas_call(
        functools.partial(out_grads_kernel, C, Z, piece),
        out_shape=[pltpu.VMEM((Z * piece, width), bf16)] * C,
        in_specs=[SMEM, VMEM, VMEM],
        out_specs=[VMEM] * C,
        scratch_shapes=[pltpu.VMEM((width, width), f32)],
        compiler_params=pltpu.CompilerParams(vmem_limit_bytes=18 * MIB),
        cost_estimate=cost(2 * attended.shape[0] * width * width, 3 * width * width),
        name="out_grads",
    )(me.reshape(1), attended, low)
    return result[: C // 2], result[C // 2 :]


EXTRA = 16


def attention_packs_kernel(Z, C, info_ref, *refs):
    R = C // 2
    grad_ref, out_refs = refs[0], refs[1 : R + 1]
    gain_one_ref, gain_two_ref, error_ref, pack_hbm, token_ref = refs[R + 1 : R + 6]
    sum_ref, tall_ref, sems = refs[R + 6 :]
    token_ref[...] = jnp.zeros_like(token_ref)
    width, cols = grad_ref.shape
    rows, tall = width // Z, tall_ref.shape[0] // Z
    piece = sum_ref.shape[0] // Z
    out = out_refs[0][...]
    for ref in out_refs[1:]:
        out = out + ref[...].astype(f32)
    sum_ref[...] = out.astype(bf16)
    line = info_ref[0]
    row = lax.broadcasted_iota(jnp.int32, (EXTRA, cols), 0)
    lane = lax.broadcasted_iota(jnp.int32, (EXTRA, cols), 1)
    error = error_ref[0, 0]
    high = error.astype(bf16).astype(f32)
    error = jnp.where(lane == 2 * line, high, jnp.where(lane == 2 * line + 1, error - high, 0.0))
    for j in range(Z):
        under = j * tall + rows
        for n in range(width // cols):
            at = slice(n * cols, (n + 1) * cols)
            tall_ref[under + n * piece : under + (n + 1) * piece, :] = sum_ref[
                j * piece : (j + 1) * piece, at
            ]
        at = slice(j * rows, (j + 1) * rows)
        extra = jnp.where(row == 0, gain_one_ref[0:1, at], jnp.where(row == 1, gain_two_ref[0:1, at], 0.0))
        extra = jnp.where(row == 2, error, extra)
        tall_ref[(j + 1) * tall - EXTRA : (j + 1) * tall, :] = extra.astype(bf16)

    @pl.loop(0, rows // 16)
    def _(n):
        for j in range(Z):
            at = pl.ds(pl.multiple_of(j * rows + n * 16, 16), 16)
            to = pl.ds(pl.multiple_of(j * tall + n * 16, 16), 16)
            tall_ref[to, :] = grad_ref[at, :]

    for copy in started(sems, 0, (tall_ref, pack_hbm)):
        copy.wait()


def attention_packs(grad, out_parts, gain_one, gain_two, error, line, Z, C):
    width, cols = grad.shape
    rows = width // Z
    tall, parts = out_parts[0].shape[0], C // 2
    piece = tall // Z
    if rows != cols or piece % 16:
        grad_out = total(out_parts[0], out_parts[1:]).astype(bf16)
        lane = jnp.arange(cols, dtype=jnp.int32)
        high = error.astype(bf16)
        low = (error - high.astype(f32)).astype(bf16)
        zero = jnp.zeros((), bf16)
        error_row = jnp.where(lane == 2 * line, high, jnp.where(lane == 2 * line + 1, low, zero))
        packs = []
        for j in range(Z):
            at = slice(j * rows, (j + 1) * rows)
            out = grad_out[j * piece : (j + 1) * piece]
            gains = [jnp.pad(x[at].astype(bf16), (0, cols - rows)) for x in (gain_one[0], gain_two[0])]
            extra = jnp.pad(jnp.stack([*gains, error_row]), ((0, EXTRA - 3), (0, 0)))
            packs += [grad[at], *[out[:, c : c + cols] for c in range(0, width, cols)], extra]
        return jnp.concatenate(packs, axis=0), jnp.zeros((8, LANES), f32)
    shape = (Z * (rows + piece * width // cols + EXTRA), cols)
    return pl.pallas_call(
        functools.partial(attention_packs_kernel, Z, C),
        out_shape=[pltpu.HBM(shape, bf16), jax.ShapeDtypeStruct((8, LANES), f32)],
        in_specs=[SMEM] + [VMEM] * (parts + 4),
        out_specs=[HBM, VMEM],
        scratch_shapes=[
            pltpu.VMEM((tall, width), bf16),
            pltpu.VMEM(shape, bf16),
            pltpu.SemaphoreType.DMA((1,)),
        ],
        compiler_params=pltpu.CompilerParams(vmem_limit_bytes=16 * MIB),
        cost_estimate=cost(0, 3 * width * width),
        name="attention_packs",
    )(line.reshape(1), grad, *out_parts, gain_one, gain_two, error.reshape(1, 1))


def attention_grads_kernel(C, rows, q_cols, kv_cols, places, me_ref, *refs):
    count = len(places)
    gain_ref, valid_ref = refs[count : count + 2]
    *grads_hbm, gains_ref, loss_ref = refs[count + 2 : count + 8]
    low_ref, extra_ref, query_ref, key_ref, value_ref, out_ref, in_sems, out_sems = refs[count + 8 :]
    me = me_ref[0]
    cols = low_ref.shape[2]
    strips = out_ref.shape[1] // cols
    piece = (low_ref.shape[1] - rows - EXTRA) // strips
    arriving = arrived([(*place, ref) for place, ref in zip(places, refs)], low_ref, in_sems)
    for i in range(C):
        for copy in arriving[i]:
            copy.wait()
        at = pl.ds(pl.multiple_of((me ^ i) * piece, piece), piece)
        for c in range(strips):
            strip = low_ref[i, rows + c * piece : rows + (c + 1) * piece, :]
            out_ref[at, c * cols : (c + 1) * cols] = strip.astype(f32)
        extra_ref[me ^ i] = low_ref[i, low_ref.shape[1] - EXTRA :, :].astype(f32)
    leaving = started(out_sems, 3, (out_ref, grads_hbm[3]))
    extra = extra_ref[0]
    for b in range(1, C):
        extra = extra + extra_ref[b]
    row = lax.broadcasted_iota(jnp.int32, gains_ref.shape, 0)
    gains_ref[...] = extra[:8, :] / jnp.where(row == 0, gain_ref[...], 1.0)
    loss_ref[...] = jnp.sum(extra[2:3, :], axis=1, keepdims=True) / valid_ref[0, 0]
    lane = lax.broadcasted_iota(jnp.int32, (rows, cols), 1)
    for n, (ref, first, size) in enumerate(
        (
            (query_ref, 0, q_cols),
            (key_ref, q_cols, kv_cols),
            (value_ref, q_cols + kv_cols, kv_cols),
        )
    ):
        many = cols // size
        for group in range(C // many):
            whole = None
            for j in range(many):
                x = low_ref[me ^ (group * many + j), :rows, :].astype(f32)
                shift = (j * size - first) % cols
                x = pltpu.roll(x, shift, 1) if shift else x
                whole = x if whole is None else jnp.where(lane < j * size, whole, x)
            ref[:, group * cols : (group + 1) * cols] = whole
        leaving += started(out_sems, n, (ref, grads_hbm[n]))
    for copy in leaving:
        copy.wait()


def attention_grads(pieces, me, gain, valid_count, C, rows, width, q_cols, kv_cols, kv_copies):
    tall, cols = pieces[0][2].shape
    strips = width // cols
    piece = (tall - rows - EXTRA) // strips
    many = C // kv_copies
    if kv_copies > 1 or cols % q_cols or cols % kv_cols or q_cols + 2 * kv_cols != cols or rows != cols or piece % 16:
        parts = unsort([x[2] for x in pieces], me)

        def kv_final(start):
            own = [part[:rows, start : start + kv_cols].astype(f32) for part in parts]
            own = [sum(own[n : n + kv_copies]) for n in range(0, C, kv_copies)]
            return jnp.concatenate(own, axis=1)

        query = jnp.concatenate([part[:rows, :q_cols] for part in parts], axis=1).astype(f32)
        outs = [part[rows : tall - EXTRA].reshape(strips, piece, cols).transpose(1, 0, 2) for part in parts]
        out = jnp.concatenate([x.reshape(piece, width) for x in outs], axis=0).astype(f32)
        extra = sum([part[tall - EXTRA :].astype(f32) for part in parts])
        gains = extra[0, :rows] / gain, extra[1, :rows]
        loss = jnp.sum(extra[2]) / valid_count
        return query, kv_final(q_cols), kv_final(q_cols + kv_cols), out, *gains, loss
    shapes = [(rows, C * q_cols), (rows, many * kv_cols), (rows, many * kv_cols), (C * piece, width)]
    *grads, gains, loss = pl.pallas_call(
        functools.partial(
            attention_grads_kernel, C, rows, q_cols, kv_cols, [x[:2] for x in pieces]
        ),
        out_shape=[
            *[pltpu.HBM(x, f32) for x in shapes],
            jax.ShapeDtypeStruct((8, cols), f32),
            jax.ShapeDtypeStruct((1, 1), f32),
        ],
        in_specs=[SMEM] + [HBM] * len(pieces) + [VMEM] * 2,
        out_specs=[HBM] * 4 + [VMEM] * 2,
        scratch_shapes=[
            pltpu.VMEM((C, tall, cols), bf16),
            pltpu.VMEM((C, EXTRA, cols), f32),
            *[pltpu.VMEM(x, f32) for x in shapes],
            pltpu.SemaphoreType.DMA((len(pieces),)),
            pltpu.SemaphoreType.DMA((4,)),
        ],
        compiler_params=pltpu.CompilerParams(vmem_limit_bytes=24 * MIB),
        cost_estimate=cost(0, 8 * rows * C * cols),
        name="attention_grads",
    )(
        me.reshape(1),
        *in_hbm(*[x[2] for x in pieces]),
        gain.reshape(1, rows),
        valid_count.reshape(1, 1),
    )
    return *grads, gains[0], gains[1], loss[0, 0]


def local(
    inputs,
    teacher,
    lengths,
    w_query,
    w_key,
    w_value,
    w_out,
    w_gate,
    w_up,
    w_down,
    gain_attn,
    gain_ffn,
):
    hidden_in = inputs[0]
    target = teacher[0]
    seq_length = lengths[0]
    tokens, width = hidden_in.shape
    C = lax.axis_size("ctx")
    Z = lax.axis_size("fsdp")
    R = C // 2
    p = lax.axis_index("ctx")
    z = lax.axis_index("fsdp")
    core = p % 2
    rows_z = width // Z
    seq = C * tokens
    q_heads = HEADS // C
    kv_heads = max(1, KV_HEADS // C)
    kv_copies = max(1, C // KV_HEADS)
    q_cols = q_heads * HEAD_DIM
    kv_cols = kv_heads * HEAD_DIM
    qkv_cols = q_cols + 2 * kv_cols
    positions = p * tokens + jnp.arange(tokens, dtype=jnp.int32)

    small = jnp.concatenate(
        [gain_attn.astype(f32), gain_ffn.astype(f32), jnp.full((LANES,), seq_length).astype(f32)]
    )
    small = jnp.stack(unsort(line_blocks(small.reshape(1, -1)), z)).reshape(Z, -1)
    gain_one = small[:, :rows_z].reshape(width)
    gain_two = small[:, rows_z : 2 * rows_z].reshape(width)
    valid_count = jnp.sum(small[:, 2 * rows_z])
    ff = w_gate.shape[1]
    ff_piece, own = ff // (Z * C), ff // C
    packed_ffn = ff_piece % LANES == 0
    if packed_ffn:
        cuts = Z
        gate_up_own, down_own = ffn_slices(w_gate, w_up, w_down, p, C, Z)
    else:
        cuts = 1
        gate_up_own = jnp.concatenate(
            [pick(w.reshape(rows_z, Z, C, ff_piece), p, 2).reshape(rows_z, own) for w in (w_gate, w_up)],
            axis=1,
        )
        down_own = lax.dynamic_slice_in_dim(w_down, p * ff_piece, ff_piece, 0)
    kv_start = (p * KV_HEADS // C) * HEAD_DIM
    out_piece = rows_z // C
    qkv_own = jnp.concatenate(
        [
            lax.dynamic_slice_in_dim(w_query, p * q_cols, q_cols, 1),
            lax.dynamic_slice_in_dim(w_key, kv_start, kv_cols, 1),
            lax.dynamic_slice_in_dim(w_value, kv_start, kv_cols, 1),
            jnp.zeros((rows_z, -qkv_cols % LANES), bf16),
        ],
        axis=1,
    )
    out_own = lax.dynamic_slice_in_dim(w_out, p * out_piece, out_piece, 0)

    scale_one = norm_scale(hidden_in)
    normed_one = (hidden_in * scale_one * gain_one).astype(bf16)
    tables = rope_tables(seq)
    normed_got, weights, tables = lax.optimization_barrier(
        (plane_sends(normed_one), line_sends(qkv_own), tables)
    )
    normed_blocks = together(core_blocks([normed_one] + normed_got))
    gate_up_own, down_own = after((gate_up_own, down_own), weights)
    gate_up = lax.all_gather(gate_up_own, "fsdp", axis=0, tiled=True)
    down_rows = lax.all_gather(down_own, "fsdp", axis=0, tiled=True)
    out_line = line_sends(after(out_own, weights))
    (normed_all, *saved), mine = attention_forward(
        normed_blocks, [qkv_own] + weights, tables, p, seq_length, z, q_heads, kv_heads
    )

    out_line, normed_all = lax.optimization_barrier((out_line, normed_all))
    out_line = jnp.concatenate(out_line, axis=0)
    out_blocks = together(core_blocks([out_line] + together(plane_sends(out_line))))
    mine = after(mine, out_blocks)
    mine = [mine[0]] + together([partner(mine[s], "ctx", 2 * s) for s in range(1, R)])
    other = [partner(x, "ctx", 1) for x in mine]
    middle, normed_two_own, attended_tokens, out_all = middle_forward(
        mine, other, out_blocks, w_out, hidden_in, gain_two, p, z, Z
    )

    normed_two_blocks = plane_blocks(normed_two_own)
    (normed_two, activated, coef), keep, give = ffn_forward(
        normed_two_blocks, gate_up, down_rows, cuts
    )
    output = middle + plane_reduce(keep, give)

    valid_rows = (positions < seq_length).astype(f32)
    residual_error = output - target
    squares = jnp.sum(valid_rows[:, None] * residual_error * residual_error)
    grad_output = valid_rows[:, None] * (2.0 * residual_error) / valid_count

    (grad_low, grad_gu), keep, give = ffn_backward(
        plane_blocks(grad_output.astype(bf16)), gate_up, down_rows, coef, cuts
    )
    chips = chip_sums(keep, give)
    grad_gate_up = transposed_times(normed_two, after(grad_gu, chips)).astype(bf16)
    grad_down = transposed_times(activated, after(grad_low, grad_gate_up)).astype(bf16)
    shard_gate_up = lax.psum_scatter(grad_gate_up, "fsdp", scatter_dimension=0, tiled=True)
    shard_down = lax.psum_scatter(grad_down, "fsdp", scatter_dimension=0, tiled=True)
    grad_middle, m_low, grad_gain_two, *pairs = middle_backward(
        chips[0], after(chip_sends(chips), grad_down), middle, gain_two, grad_output, out_all, p
    )

    out_keep, out_give = out_grads(attended_tokens, after(m_low, pairs), p, C, Z)
    mine = [pairs[0]] + together([partner(pairs[s], "ctx", 2 * s) for s in range(1, R)])
    other = [partner(x, "ctx", 1) for x in mine]
    out_chips = chip_sums(out_keep, out_give)
    mine = after(mine, out_chips)
    grad_qkv, gain_part, keep, give = attention_backward(
        mine, other, (normed_all, *saved), tables, p, seq_length, q_heads, kv_heads
    )
    chips = chip_sums(keep, give)
    square = packed_ffn and C == 8
    out_got, grad_qkv = lax.optimization_barrier((chip_sends(out_chips), grad_qkv))
    packs, token = attention_packs(
        grad_qkv, [out_chips[0]] + out_got, gain_part, grad_gain_two, squares, z, Z, C
    )
    shard_packs = lax.psum_scatter(packs, "fsdp", scatter_dimension=0, tiled=True)
    normed_got = [partner(x, "ctx", 2 * (s + 1)) for s, x in enumerate(after(chips[1:], out_got))]
    near = near_sends(after(shard_gate_up, out_got)) if square else []
    normed_got, near, token = lax.optimization_barrier((normed_got, near, token))
    grad_normed_one = total(chips[0], normed_got)
    back_one, _ = norm_back(grad_normed_one, hidden_in, scale_one, gain_one)
    grad_hidden = grad_middle + back_one


    if square:
        down_near = near_sends(after(shard_down, normed_got))
        far, down_near = lax.optimization_barrier((far_sends(near), down_near))
        pieces = square_pieces(shard_gate_up, near, far)
        final_gate, final_up = column_grads(pieces, p, C, Z)
        pack_near = near_sends(after(shard_packs, far))
        down_far, pack_near, final_gate = lax.optimization_barrier(
            (far_sends(down_near), pack_near, final_gate)
        )
        final_down = row_grads(square_pieces(shard_down, down_near, down_far), p, C)
        pack_far, final_down, grad_hidden = lax.optimization_barrier(
            (far_sends(pack_near), final_down, grad_hidden)
        )
        pieces = square_pieces(shard_packs, pack_near, pack_far)
    else:
        pieces = [(i, 0, block) for i, block in enumerate(plane_blocks(shard_packs))]
        gate_up, down = [
            jnp.stack(unsort(plane_blocks(x), p)).astype(f32) for x in (shard_gate_up, shard_down)
        ]
        gate_up = gate_up.reshape(C, rows_z, 2, Z, ff_piece).transpose(2, 1, 3, 0, 4)
        final_gate, final_up = gate_up.reshape(2, rows_z, ff)
        final_down = down.reshape(C * ff_piece, width)
    final_query, final_key, final_value, final_out, *final_gains, loss_value = attention_grads(
        pieces,
        p,
        gain_attn.astype(f32),
        valid_count,
        C,
        rows_z,
        width,
        q_cols,
        kv_cols,
        kv_copies,
    )

    return (
        output[None],
        loss_value,
        grad_hidden[None],
        final_query,
        final_key,
        final_value,
        final_out,
        final_gate,
        final_up,
        final_down,
        *final_gains,
    )


def solution(mesh):
    return jax.shard_map(
        local,
        mesh=mesh,
        in_specs=(
            P("fsdp", "ctx", None),
            P("fsdp", "ctx", None),
            P("fsdp"),
            P("fsdp", None),
            P("fsdp", None),
            P("fsdp", None),
            P("fsdp", None),
            P("fsdp", None),
            P("fsdp", None),
            P("fsdp", None),
            P("fsdp"),
            P("fsdp"),
        ),
        out_specs=(
            P("fsdp", "ctx", None),
            P(),
            P("fsdp", "ctx", None),
            P("fsdp", None),
            P("fsdp", None),
            P("fsdp", None),
            P("fsdp", None),
            P("fsdp", None),
            P("fsdp", None),
            P("fsdp", None),
            P("fsdp"),
            P("fsdp"),
        ),
        check_vma=False,
    )
```

```python
import functools

import jax
import jax.numpy as jnp
from jax import lax
from jax.experimental import pallas as pl
from jax.experimental.pallas import tpu as pltpu
from jax.sharding import PartitionSpec as P

HEADS = 16
KV_HEADS = 8
HEAD_DIM = 96
LANES = 128

eps_norm = 1e-05
rope_base = 100000.0
masked_value = -1e30

f32 = jnp.float32
bf16 = jnp.bfloat16

VMEM = pl.BlockSpec(memory_space=pltpu.VMEM)
SMEM = pl.BlockSpec(memory_space=pltpu.SMEM)
HBM = pl.BlockSpec(memory_space=pltpu.HBM)
MIB = 1024 * 1024


def cost(multiply_adds, values):
    return pl.CostEstimate(flops=1, bytes_accessed=1, transcendentals=0)


def in_hbm(*xs):
    return [pltpu.with_memory_space_constraint(x, pltpu.HBM) for x in xs]


def started(sems, first, *pairs):
    copies = [pltpu.make_async_copy(a, b, sems.at[first + n]) for n, (a, b) in enumerate(pairs)]
    for copy in copies:
        copy.start()
    return copies


def times(left, right):
    return jnp.dot(left, right, preferred_element_type=f32)


def times_transposed(left, right):
    return lax.dot_general(left, right, (((1,), (1,)), ((), ())), preferred_element_type=f32)


def transposed_times(left, right):
    return lax.dot_general(left, right, (((0,), (0,)), ((), ())), preferred_element_type=f32)


def norm_scale(features):
    return lax.rsqrt(jnp.mean(features * features, axis=-1, keepdims=True) + eps_norm)


def norm_back(upstream, features, row_scale, gain_vector):
    weighted = upstream * gain_vector
    inner_mean = jnp.mean(weighted * features, axis=-1, keepdims=True)
    grad_rows = row_scale * weighted - features * (row_scale * row_scale * row_scale) * inner_mean
    return (grad_rows, jnp.sum(upstream * (features * row_scale), axis=0))


def partner(x, axis, mask):
    return lax.ppermute(x, axis, [(i, i ^ mask) for i in range(lax.axis_size(axis))])


def plane_sends(x):
    return [partner(x, "ctx", 2 * s) for s in range(1, lax.axis_size("ctx") // 2)]


def core_blocks(mine):
    blocks = []
    for x in mine:
        blocks += [x, partner(x, "ctx", 1)]
    return blocks


def plane_blocks(x):
    return core_blocks([x] + plane_sends(x))


def near_sends(x):
    return [partner(x, "ctx", 2), partner(x, "ctx", 4)]


def far_sends(near):
    half = near[0].shape[0] // 32 * 16
    return [partner(near[0][:half], "ctx", 4), partner(near[1][half:], "ctx", 2)]


def square_pieces(x, near, far):
    half = x.shape[0] // 32 * 16
    mine = [(0, 0, x), (1, 0, near[0]), (2, 0, near[1]), (3, 0, far[0]), (3, half, far[1])]
    other = together([partner(block, "ctx", 1) for _, _, block in mine])
    pieces = []
    for (s, first, block), swapped in zip(mine, other, strict=True):
        pieces += [(2 * s, first, block), (2 * s + 1, first, swapped)]
    return pieces


def line_sends(x):
    return [partner(x, "fsdp", s) for s in range(1, lax.axis_size("fsdp"))]


def plane_reduce(keep, give):
    chips = chip_sums(keep, give)
    return total(chips[0], chip_sends(chips))


def chip_sums(keep, give):
    got = [partner(x, "ctx", 1) for x in give[::-1]][::-1]
    own = keep[0].astype(f32) + got[0].astype(f32)
    return [own] + [
        (a.astype(f32) + b.astype(f32)).astype(bf16) for a, b in zip(keep[1:], got[1:], strict=True)
    ]


def chip_sends(chips):
    return together([partner(chips[s], "ctx", 2 * s) for s in range(len(chips) - 1, 0, -1)])


def total(own, got):
    for x in got:
        own = own + x.astype(f32)
    return own


def tree_sum(x, axis):
    mask = 1
    while mask < lax.axis_size(axis):
        x = x + partner(x, axis, mask)
        mask *= 2
    return x


def line_blocks(x):
    return [x] + together(line_sends(x))


def line_reduce(parts):
    got = together([partner(parts[s], "fsdp", s) for s in range(1, len(parts))])
    return total(parts[0].astype(f32), got)


def together(xs):
    return list(lax.optimization_barrier(tuple(xs)))


def after(x, *done):
    return lax.optimization_barrier((x, done))[0]


def pick(x, index, axis=0):
    return lax.dynamic_index_in_dim(x, index, axis, False)


def unsort(blocks, me):
    stacked = jnp.stack(blocks)
    return [pick(stacked, me ^ b) for b in range(len(blocks))]


def rope_tables(count):
    half_dim = HEAD_DIM // 2
    frequencies = rope_base ** (-(jnp.arange(half_dim, dtype=f32) * 2.0) / HEAD_DIM)
    angles = jnp.arange(count, dtype=f32)[:, None] * frequencies[None, :]
    cosines, sines = jnp.cos(angles), jnp.sin(angles)
    pad = jnp.zeros((count, LANES - HEAD_DIM), f32)
    return (
        jnp.concatenate([cosines, cosines, pad], axis=1),
        jnp.concatenate([-sines, sines, pad], axis=1),
    )


def turned(x):
    lane = lax.broadcasted_iota(jnp.int32, x.shape, 1)
    half_dim = HEAD_DIM // 2
    return jnp.where(
        lane < half_dim, pltpu.roll(x, LANES - half_dim, 1), pltpu.roll(x, half_dim, 1)
    )


def head_of(x, head):
    if head:
        x = pltpu.roll(x, x.shape[1] - head * HEAD_DIM, 1)
    return x[:, :LANES]


def packed(heads):
    wide = -(-len(heads) * HEAD_DIM // LANES) * LANES
    total = None
    for index, head in enumerate(heads):
        if wide > LANES:
            head = jnp.concatenate([head, jnp.zeros((head.shape[0], wide - LANES), f32)], axis=1)
        if index:
            head = pltpu.roll(head, index * HEAD_DIM, 1)
        total = head if total is None else total + head
    return total


def attention_forward_kernel(C, Z, tokens, q_heads, kv_heads, block, info_ref, *refs):
    R = C // 2
    n_refs, w_parts = refs[:C], refs[C : C + Z]
    cos_hbm, sin_hbm = refs[C + Z : C + Z + 2]
    n_hbm, w_hbm, qkv_hbm, att_hbm, lse_hbm = refs[C + Z + 2 : C + Z + 7]
    block_refs = refs[C + Z + 7 : C + Z + 7 + R]
    n_all_ref, w_ref, lin_ref, qkv_ref, att_ref, lse_ref, cos_ref, sin_ref, sems = refs[C + Z + 7 + R :]
    me, length = info_ref[0], info_ref[1]
    seq = C * tokens
    group = q_heads // kv_heads
    width_low = q_heads * HEAD_DIM
    rows_z = w_ref.shape[0] // Z
    pairs = []
    for j in range(Z):
        at = pl.multiple_of((info_ref[2] ^ j) * rows_z, rows_z)
        pairs.append((w_parts[j].at[:rows_z, :], w_ref.at[pl.ds(at, rows_z), :]))
    tables = started(sems, 0, (cos_hbm, cos_ref), (sin_hbm, sin_ref), *pairs)
    for i in range(C):
        n_all_ref[i * tokens : (i + 1) * tokens, :] = n_refs[i][...]
    for copy in tables[2:]:
        copy.wait()
    saved = started(sems, 2, (n_all_ref, n_hbm), (w_ref, w_hbm))
    step = 4 * tokens
    for start in range(0, seq, step):
        lin_ref[start : start + step, :] = times(n_all_ref[start : start + step, :], w_ref[...])
    for copy in tables[:2]:
        copy.wait()
    lane = lax.broadcasted_iota(jnp.int32, (tokens, LANES), 1)
    for i in range(C):
        rows = pl.ds(pl.multiple_of((me ^ i) * tokens, tokens), tokens)
        lin = lin_ref[i * tokens : (i + 1) * tokens, :]
        cosines, sines = cos_ref[rows, :], sin_ref[rows, :]
        for head in range(q_heads + 2 * kv_heads):
            x = head_of(lin, head)
            if head < q_heads + kv_heads:
                x = x * cosines + turned(x) * sines
            else:
                x = jnp.where(lane < HEAD_DIM, x, 0.0)
            qkv_ref[rows, head * LANES : (head + 1) * LANES] = x.astype(bf16)
    saved += started(sems, 4, (qkv_ref, qkv_hbm))
    scale = HEAD_DIM ** (-0.5)
    for head in range(q_heads):
        k_at = (q_heads + head // group) * LANES
        v_at = k_at + kv_heads * LANES
        for start in range(0, seq, block):
            end = start + block
            q = qkv_ref[start:end, head * LANES : (head + 1) * LANES]
            scores = times_transposed(q, qkv_ref[:end, k_at : k_at + LANES]) * scale
            row = start + lax.broadcasted_iota(jnp.int32, (block, end), 0)
            col = lax.broadcasted_iota(jnp.int32, (block, end), 1)
            scores = jnp.where((col <= row) & (col < length), scores, masked_value)
            row_max = jnp.max(scores, axis=1, keepdims=True)
            weights = jnp.exp(scores - row_max)
            row_sum = jnp.sum(weights, axis=1, keepdims=True)
            probs = (weights * (1.0 / row_sum)).astype(bf16)
            att_ref[start:end, head * LANES : (head + 1) * LANES] = times(
                probs, qkv_ref[:end, v_at : v_at + LANES]
            )
            lse_ref[start:end, head : head + 1] = row_max + jnp.log(row_sum)
    saved += started(sems, 5, (att_ref, att_hbm), (lse_ref, lse_hbm))
    for i in range(C):
        rows = pl.ds(pl.multiple_of((me ^ i) * tokens, tokens), tokens)
        x = att_ref[rows, :]
        low = packed([x[:, h * LANES : (h + 1) * LANES] for h in range(q_heads)])
        at = (i % 2) * tokens
        block_refs[i // 2][at : at + tokens, :] = low[:, :width_low].astype(bf16)
    for copy in saved:
        copy.wait()


def attention_forward(blocks, w_parts, tables, me, length, line, q_heads, kv_heads):
    C, Z = len(blocks), len(w_parts)
    tokens, width = blocks[0].shape
    seq = C * tokens
    heads = q_heads + 2 * kv_heads
    cols = w_parts[0].shape[1]
    saved = [
        ((seq, width), bf16),
        ((width, cols), bf16),
        ((seq, heads * LANES), bf16),
        ((seq, q_heads * LANES), f32),
        ((seq, LANES), f32),
    ]
    part = jax.ShapeDtypeStruct((2 * tokens, q_heads * HEAD_DIM), bf16)
    result = pl.pallas_call(
        functools.partial(attention_forward_kernel, C, Z, tokens, q_heads, kv_heads, 2 * tokens),
        out_shape=[pltpu.HBM(*x) for x in saved] + [part] * (C // 2),
        in_specs=[SMEM] + [VMEM] * C + [HBM] * (Z + 2),
        out_specs=[HBM] * len(saved) + [VMEM] * (C // 2),
        scratch_shapes=[pltpu.VMEM(*saved[0]), pltpu.VMEM(*saved[1]), pltpu.VMEM((seq, cols), f32)]
        + [pltpu.VMEM(*x) for x in saved[2:]]
        + [pltpu.VMEM((seq, LANES), f32)] * 2
        + [pltpu.SemaphoreType.DMA((7 + Z,))],
        compiler_params=pltpu.CompilerParams(vmem_limit_bytes=22 * MIB),
        cost_estimate=cost(seq * width * cols + 2 * seq * seq * heads * LANES, 3 * seq * width),
        name="attention_forward",
    )(jnp.stack([me, length, line]).astype(jnp.int32), *blocks, *in_hbm(*w_parts, *tables))
    return result[: len(saved)], result[len(saved) :]


def attention_backward_kernel(C, tokens, q_heads, kv_heads, block, info_ref, *refs):
    R = C // 2
    mine_refs, other_refs = refs[:R], refs[R:C]
    hbm_refs = refs[C : C + 7]
    grad_w_ref, gain_ref = refs[C + 7 : C + 9]
    keep_refs = refs[C + 9 : C + 9 + R]
    give_refs = refs[C + 9 + R : C + 9 + C]
    refs = refs[C + 9 + C :]
    qkv_ref, att_ref, lse_ref, cos_ref, sin_ref, w_ref, n_all_ref = refs[:7]
    wide_ref, grad_ref, dq_ref, dkv_ref, dqkv_ref, sems = refs[7:]
    copies = started(sems, 0, *zip(hbm_refs, refs[:7], strict=True))
    me, length = info_ref[0], info_ref[1]
    core = me % 2
    seq = C * tokens
    group = q_heads // kv_heads
    width_low = q_heads * HEAD_DIM
    lane = lax.broadcasted_iota(jnp.int32, (tokens, LANES), 1)
    wide_ref[...] = jnp.zeros_like(wide_ref)
    for i in range(C):
        rows = pl.ds(pl.multiple_of((me ^ i) * tokens, tokens), tokens)
        wide_ref[:, : 2 * width_low] = (other_refs if i % 2 else mine_refs)[i // 2][...].astype(f32)
        wide = wide_ref[...]
        wide = jnp.where(core == 0, wide, pltpu.roll(wide, wide.shape[1] - width_low, 1))
        for head in range(q_heads):
            x = jnp.where(lane < HEAD_DIM, head_of(wide, head), 0.0)
            grad_ref[rows, head * LANES : (head + 1) * LANES] = x.astype(bf16)
    dkv_ref[...] = jnp.zeros_like(dkv_ref)
    scale = HEAD_DIM ** (-0.5)
    for copy in copies[:5]:
        copy.wait()
    for start in range(0, seq, block):
        end = start + block
        lane_b = lax.broadcasted_iota(jnp.int32, (block, LANES), 1)
        delta = jnp.zeros((block, LANES), f32)
        for head in range(q_heads):
            at = slice(head * LANES, (head + 1) * LANES)
            one = jnp.sum(
                grad_ref[start:end, at].astype(f32) * att_ref[start:end, at], axis=1, keepdims=True
            )
            delta = jnp.where(lane_b == head, one, delta)
        delta_t = delta.T
        lse_t = lse_ref[start:end, :].T
        key = lax.broadcasted_iota(jnp.int32, (end, block), 0)
        query = start + lax.broadcasted_iota(jnp.int32, (end, block), 1)
        allowed = (key <= query) & (key < length)
        for head in range(q_heads):
            at = slice(head * LANES, (head + 1) * LANES)
            kv = head // group
            k_at = slice((q_heads + kv) * LANES, (q_heads + kv + 1) * LANES)
            v_at = slice((q_heads + kv_heads + kv) * LANES, (q_heads + kv_heads + kv + 1) * LANES)
            q, grad = qkv_ref[start:end, at], grad_ref[start:end, at]
            k, v = qkv_ref[:end, k_at], qkv_ref[:end, v_at]
            scores = times_transposed(k, q) * scale
            probs = jnp.where(allowed, jnp.exp(scores - lse_t[head : head + 1, :]), 0.0)
            grad_probs = times_transposed(v, grad)
            grad_scores = (probs * (grad_probs - delta_t[head : head + 1, :])).astype(bf16)
            dq_ref[start:end, at] = transposed_times(grad_scores, k) * scale
            dk_at = slice(kv * LANES, (kv + 1) * LANES)
            dv_at = slice((kv_heads + kv) * LANES, (kv_heads + kv + 1) * LANES)
            dkv_ref[:end, dk_at] += times(grad_scores, q) * scale
            dkv_ref[:end, dv_at] += times(probs.astype(bf16), grad)
    for i in range(C):
        rows = pl.ds(pl.multiple_of((me ^ i) * tokens, tokens), tokens)
        cosines, sines = cos_ref[rows, :], sin_ref[rows, :]
        heads = []
        for head in range(q_heads + 2 * kv_heads):
            if head < q_heads:
                x = dq_ref[rows, head * LANES : (head + 1) * LANES]
            else:
                x = dkv_ref[rows, (head - q_heads) * LANES : (head - q_heads + 1) * LANES]
            if head < q_heads + kv_heads:
                x = x * cosines - turned(x) * sines
            heads.append(x)
        dqkv_ref[i * tokens : (i + 1) * tokens, :] = packed(heads).astype(bf16)
    for copy in copies[5:]:
        copy.wait()

    def rows_of(at):
        part = times_transposed(dqkv_ref[...], w_ref[at, :])
        gain = jnp.sum(part * n_all_ref[:, at].astype(f32), axis=0, keepdims=True)
        gain_ref[:, at] = jnp.broadcast_to(gain, (gain_ref.shape[0], gain.shape[1]))
        return part

    parts_of(rows_of, keep_refs, give_refs)
    step = 3 * LANES

    @pl.loop(0, grad_w_ref.shape[0] // step)
    def _(n):
        at = pl.ds(pl.multiple_of(n * step, step), step)
        grad_w_ref[at, :] = transposed_times(n_all_ref[:, at], dqkv_ref[...]).astype(bf16)


def attention_backward(mine, other, saved, tables, me, length, q_heads, kv_heads):
    C = 2 * len(mine)
    tokens, pair = mine[0].shape
    normed_all, w_qkv, qkv, attended, lse = saved
    width, cols = w_qkv.shape
    loaded = (qkv, attended, lse, *tables, w_qkv, normed_all)
    seq = C * tokens
    heads = q_heads + 2 * kv_heads
    part = jax.ShapeDtypeStruct((tokens, width), bf16)
    result = pl.pallas_call(
        functools.partial(attention_backward_kernel, C, tokens, q_heads, kv_heads, 2 * tokens),
        out_shape=[
            jax.ShapeDtypeStruct((width, cols), bf16),
            jax.ShapeDtypeStruct((8, width), f32),
        ]
        + [part] * C,
        in_specs=[SMEM] + [VMEM] * C + [HBM] * 7,
        out_specs=[VMEM] * (C + 2),
        scratch_shapes=[pltpu.VMEM(x.shape, x.dtype) for x in loaded]
        + [
            pltpu.VMEM((tokens, -(-pair // LANES) * LANES), f32),
            pltpu.VMEM((seq, q_heads * LANES), bf16),
            pltpu.VMEM((seq, q_heads * LANES), f32),
            pltpu.VMEM((seq, 2 * kv_heads * LANES), f32),
            pltpu.VMEM((seq, cols), bf16),
            pltpu.SemaphoreType.DMA((7,)),
        ],
        compiler_params=pltpu.CompilerParams(vmem_limit_bytes=28 * MIB),
        cost_estimate=cost(seq * width * cols + 4 * seq * seq * heads * LANES, 3 * seq * width),
        name="attention_backward",
    )(jnp.stack([me, length]).astype(jnp.int32), *mine, *other, *in_hbm(*loaded))
    return result[0], result[1], result[2 : 2 + C // 2], result[2 + C // 2 :]


def gather_rows(block_refs, all_ref):
    tokens = block_refs[0].shape[0]

    @pl.loop(0, tokens // 16)
    def _(n):
        for i, ref in enumerate(block_refs):
            at = pl.ds(pl.multiple_of(n * 16, 16), 16)
            to = pl.ds(pl.multiple_of(i * tokens + n * 16, 16), 16)
            all_ref[to, :] = ref[at, :]


def parts_of(rows_of, keep_refs, give_refs):
    tokens, width = keep_refs[0].shape
    strip = 4 * LANES

    @pl.loop(0, width // strip)
    def _(n):
        at = pl.ds(pl.multiple_of(n * strip, strip), strip)
        part = rows_of(at)
        for i in range(2 * len(keep_refs)):
            ref = (give_refs if i % 2 else keep_refs)[i // 2]
            ref[:, at] = part[i * tokens : (i + 1) * tokens, :].astype(bf16)


def ffn_units_kernel(C, cuts, *refs):
    n_refs = refs[:C]
    gu_hbm, n_hbm, coef_hbm, act_ref = refs[C : C + 4]
    gu_ref, n_all_ref, coef_ref, sems = refs[C + 4 :]
    tokens = n_refs[0].shape[0]
    pairs = [(n_refs[i], n_all_ref.at[i * tokens : (i + 1) * tokens, :]) for i in range(C)]
    for copy in started(sems, 0, (gu_hbm, gu_ref), *pairs):
        copy.wait()
    saved = started(sems, 0, (n_all_ref, n_hbm))
    w = act_ref.shape[1] // cuts

    @pl.loop(0, cuts)
    def _(j):
        at = pl.ds(pl.multiple_of(j * 2 * w, 2 * w), 2 * w)
        both = times(n_all_ref[...], gu_ref[:, at])
        gate, up = both[:, :w], both[:, w:]
        sigmoid = jax.nn.sigmoid(gate)
        silu = gate * sigmoid
        act_ref[:, pl.ds(pl.multiple_of(j * w, w), w)] = (silu * up).astype(bf16)
        slope = up * (sigmoid * (1.0 + gate * (1.0 - sigmoid)))
        coef_ref[:, at] = jnp.concatenate([slope, silu], axis=1).astype(bf16)

    saved += started(sems, 1, (coef_ref, coef_hbm))
    for copy in saved:
        copy.wait()


def ffn_units(blocks, gate_up, cuts):
    C = len(blocks)
    tokens, width = blocks[0].shape
    seq, both = C * tokens, gate_up.shape[1]
    return pl.pallas_call(
        functools.partial(ffn_units_kernel, C, cuts),
        out_shape=[
            pltpu.HBM((seq, width), bf16),
            pltpu.HBM((seq, both), bf16),
            jax.ShapeDtypeStruct((seq, both // 2), bf16),
        ],
        in_specs=[HBM] * (C + 1),
        out_specs=[HBM, HBM, VMEM],
        scratch_shapes=[
            pltpu.VMEM(gate_up.shape, bf16),
            pltpu.VMEM((seq, width), bf16),
            pltpu.VMEM((seq, both), bf16),
            pltpu.SemaphoreType.DMA((C + 1,)),
        ],
        compiler_params=pltpu.CompilerParams(vmem_limit_bytes=20 * MIB),
        cost_estimate=cost(2 * seq * width * both, 3 * seq * width),
        name="ffn_units",
    )(*in_hbm(*blocks, gate_up))


def ffn_forward_kernel(C, act_ref, down_hbm, *refs):
    keep_refs, give_refs, (down_ref, sems) = refs[: C // 2], refs[C // 2 : C], refs[C:]
    for copy in started(sems, 0, (down_hbm, down_ref)):
        copy.wait()
    parts_of(lambda at: times(act_ref[...], down_ref[:, at]), keep_refs, give_refs)


def ffn_forward(activated, down, C):
    seq, own = activated.shape
    width = down.shape[1]
    result = pl.pallas_call(
        functools.partial(ffn_forward_kernel, C),
        out_shape=[jax.ShapeDtypeStruct((seq // C, width), bf16)] * C,
        in_specs=[VMEM, HBM],
        out_specs=[VMEM] * C,
        scratch_shapes=[pltpu.VMEM(down.shape, bf16), pltpu.SemaphoreType.DMA((1,))],
        compiler_params=pltpu.CompilerParams(vmem_limit_bytes=12 * MIB),
        cost_estimate=cost(seq * width * own, seq * width),
        name="ffn_forward",
    )(activated, *in_hbm(down))
    return result[: C // 2], result[C // 2 :]


def ffn_backward_kernel(C, cuts, *refs):
    g_refs = refs[:C]
    gu_hbm, down_hbm, coef_hbm, g_all_ref, dgu_ref = refs[C : C + 5]
    keep_refs = refs[C + 5 : C + 5 + C // 2]
    give_refs = refs[C + 5 + C // 2 : 2 * C + 5]
    gu_ref, down_ref, coef_ref, sems = refs[2 * C + 5 :]
    copies = started(sems, 0, (down_hbm, down_ref), (coef_hbm, coef_ref), (gu_hbm, gu_ref))
    gather_rows(g_refs, g_all_ref)
    for copy in copies[:2]:
        copy.wait()
    w = down_ref.shape[0] // cuts
    many = 2 if cuts % 2 == 0 else 1

    @pl.loop(0, cuts // many)
    def _(j):
        rows = pl.ds(pl.multiple_of(j * many * w, many * w), many * w)
        grad_act = times_transposed(g_all_ref[...], down_ref[rows, :])
        at = pl.ds(pl.multiple_of(j * many * 2 * w, many * 2 * w), many * 2 * w)
        parts = [grad_act[:, (n // 2) * w : (n // 2 + 1) * w] for n in range(2 * many)]
        both = jnp.concatenate(parts, axis=1)
        dgu_ref[:, at] = (both * coef_ref[:, at].astype(f32)).astype(bf16)

    copies[2].wait()
    parts_of(lambda at: times_transposed(dgu_ref[...], gu_ref[at, :]), keep_refs, give_refs)


def ffn_backward(blocks, gate_up, down, coef, cuts):
    C = len(blocks)
    tokens, width = blocks[0].shape
    seq, own = C * tokens, coef.shape[1] // 2
    part = jax.ShapeDtypeStruct((tokens, width), bf16)
    result = pl.pallas_call(
        functools.partial(ffn_backward_kernel, C, cuts),
        out_shape=[
            jax.ShapeDtypeStruct((seq, width), bf16),
            jax.ShapeDtypeStruct((seq, 2 * own), bf16),
        ]
        + [part] * C,
        in_specs=[VMEM] * C + [HBM] * 3,
        out_specs=[VMEM] * (C + 2),
        scratch_shapes=[
            pltpu.VMEM((width, 2 * own), bf16),
            pltpu.VMEM((own, width), bf16),
            pltpu.VMEM(coef.shape, bf16),
            pltpu.SemaphoreType.DMA((3,)),
        ],
        compiler_params=pltpu.CompilerParams(vmem_limit_bytes=24 * MIB),
        cost_estimate=cost(3 * seq * width * own, 3 * seq * width),
        name="ffn_backward",
    )(*blocks, *in_hbm(gate_up, down, coef))
    return result[:2], result[2 : 2 + C // 2], result[2 + C // 2 :]


def ffn_slices_kernel(C, Z, piece, me_ref, gate_hbm, up_hbm, down_hbm, *refs):
    gu_hbm, rows_hbm, gu_ref, rows_ref, sems = refs
    me = me_ref[0]
    pairs = []
    for j in range(Z):
        for a, ref in enumerate((gate_hbm, up_hbm)):
            at = pl.multiple_of((j * C + me) * piece, piece)
            to = (2 * j + a) * piece
            pairs.append((ref.at[:, pl.ds(at, piece)], gu_ref.at[:, to : to + piece]))
    at = pl.multiple_of(me * piece, piece)
    pairs.append((down_hbm.at[pl.ds(at, piece), :], rows_ref))
    for copy in started(sems, 0, *pairs):
        copy.wait()
    for copy in started(sems, 0, (gu_ref, gu_hbm), (rows_ref, rows_hbm)):
        copy.wait()


def ffn_slices(w_gate, w_up, w_down, me, C, Z):
    rows, ff = w_gate.shape
    width = w_down.shape[1]
    piece = ff // (Z * C)
    shapes = (rows, 2 * Z * piece), (piece, width)
    return pl.pallas_call(
        functools.partial(ffn_slices_kernel, C, Z, piece),
        out_shape=[pltpu.HBM(x, bf16) for x in shapes],
        in_specs=[SMEM, HBM, HBM, HBM],
        out_specs=[HBM, HBM],
        scratch_shapes=[pltpu.VMEM(x, bf16) for x in shapes]
        + [pltpu.SemaphoreType.DMA((2 * Z + 1,))],
        compiler_params=pltpu.CompilerParams(vmem_limit_bytes=8 * MIB),
        cost_estimate=cost(0, 6 * rows * ff // C),
        name="ffn_slices",
    )(me.reshape(1), *in_hbm(w_gate, w_up, w_down))


def arrived(pieces, low_ref, sems):
    pairs = []
    for i, first, ref in pieces:
        pairs.append((ref, low_ref.at[i, pl.ds(first, ref.shape[0]), :]))
    copies = started(sems, 0, *pairs)
    return [[copy for copy, piece in zip(copies, pieces) if piece[0] == i] for i in range(low_ref.shape[0])]


def column_grads_kernel(C, Z, piece, places, me_ref, *refs):
    gate_hbm, up_hbm, low_ref, wide_ref, in_sems, sems = refs[len(places) :]
    me = me_ref[0]
    stride = gate_hbm.shape[1] // Z
    arriving = arrived([(*place, ref) for place, ref in zip(places, refs)], low_ref, in_sems)
    flying = [(), ()]
    for i in range(C):
        slot = i % 2
        for copy in (*flying[slot], *arriving[i]):
            copy.wait()

        @pl.loop(0, low_ref.shape[1] // 16)
        def _(n):
            at = pl.ds(pl.multiple_of(n * 16, 16), 16)
            wide_ref[slot, at, :] = low_ref[i, at, :].astype(f32)

        pairs = []
        for j in range(Z):
            at = pl.multiple_of(j * stride + (me ^ i) * piece, piece)
            for a, ref in enumerate((gate_hbm, up_hbm)):
                to = (2 * j + a) * piece
                pairs.append((wide_ref.at[slot, :, to : to + piece], ref.at[:, pl.ds(at, piece)]))
        flying[slot] = started(sems.at[slot], 0, *pairs)
    for copies in flying:
        for copy in copies:
            copy.wait()


def column_grads(pieces, me, C, Z):
    rows, cols = pieces[0][2].shape
    piece = cols // (2 * Z)
    ff = Z * C * piece
    return pl.pallas_call(
        functools.partial(column_grads_kernel, C, Z, piece, [x[:2] for x in pieces]),
        out_shape=[pltpu.HBM((rows, ff), f32)] * 2,
        in_specs=[SMEM] + [HBM] * len(pieces),
        out_specs=[HBM] * 2,
        scratch_shapes=[
            pltpu.VMEM((C, rows, cols), bf16),
            pltpu.VMEM((2, rows, cols), f32),
            pltpu.SemaphoreType.DMA((len(pieces),)),
            pltpu.SemaphoreType.DMA((2, 2 * Z)),
        ],
        compiler_params=pltpu.CompilerParams(vmem_limit_bytes=16 * MIB),
        cost_estimate=cost(0, 6 * rows * ff),
        name="column_grads",
    )(me.reshape(1), *in_hbm(*[x[2] for x in pieces]))


def row_grads_kernel(C, places, me_ref, *refs):
    out_hbm, low_ref, tall_ref, in_sems, sems = refs[len(places) :]
    me = me_ref[0]
    piece = low_ref.shape[1]
    arriving = arrived([(*place, ref) for place, ref in zip(places, refs)], low_ref, in_sems)
    flying = []
    for i in range(C):
        for copy in arriving[i]:
            copy.wait()

        @pl.loop(0, piece // 16)
        def _(n):
            at = pl.ds(pl.multiple_of(n * 16, 16), 16)
            tall_ref[i, at, :] = low_ref[i, at, :].astype(f32)

        at = pl.multiple_of((me ^ i) * piece, piece)
        flying += started(sems, i, (tall_ref.at[i], out_hbm.at[pl.ds(at, piece), :]))
    for copy in flying:
        copy.wait()


def row_grads(pieces, me, C):
    piece, width = pieces[0][2].shape
    return pl.pallas_call(
        functools.partial(row_grads_kernel, C, [x[:2] for x in pieces]),
        out_shape=pltpu.HBM((C * piece, width), f32),
        in_specs=[SMEM] + [HBM] * len(pieces),
        out_specs=HBM,
        scratch_shapes=[
            pltpu.VMEM((C, piece, width), bf16),
            pltpu.VMEM((C, piece, width), f32),
            pltpu.SemaphoreType.DMA((len(pieces),)),
            pltpu.SemaphoreType.DMA((C,)),
        ],
        compiler_params=pltpu.CompilerParams(vmem_limit_bytes=16 * MIB),
        cost_estimate=cost(0, 4 * C * piece * width),
        name="row_grads",
    )(me.reshape(1), *in_hbm(*[x[2] for x in pieces]))


def middle_forward_kernel(C, Z, piece, info_ref, *refs):
    R = C // 2
    mine_refs, other_refs, w_refs = refs[:R], refs[R:C], refs[C : 2 * C]
    own_hbm, hidden_ref, gain_ref = refs[2 * C : 2 * C + 3]
    middle_ref, normed_ref, att_ref, out_hbm = refs[2 * C + 3 : 2 * C + 7]
    out_ref, low_ref, high_ref, sems = refs[2 * C + 7 :]
    me, line = info_ref[0], info_ref[1]
    rows_z = C * piece
    own_at = pl.ds(pl.multiple_of(line * rows_z, rows_z), rows_z)
    here = started(sems, 1, (own_hbm, out_ref.at[own_at, :]))
    core = me % 2
    tokens, half = hidden_ref.shape[0], mine_refs[0].shape[1]
    for i in range(C):
        for j in range(1, Z):
            at = pl.multiple_of((line ^ j) * rows_z + (me ^ i) * piece, piece)
            out_ref[pl.ds(at, piece), :] = w_refs[i][(j - 1) * piece : j * piece, :]
    for copy in here:
        copy.wait()
    saved = started(sems, 0, (out_ref, out_hbm))
    low_ref[...] = jnp.zeros_like(low_ref)
    high_ref[...] = jnp.zeros_like(high_ref)
    for s in range(R):
        own = mine_refs[s][:tokens, :].astype(f32)
        other = other_refs[s][tokens:, :].astype(f32)
        low_ref[:, :half] = jnp.where(core == 0, own, other)
        high_ref[:, :half] = jnp.where(core == 0, other, own)
        pair = low_ref[...] + pltpu.roll(high_ref[...], half, 1)
        at = pl.multiple_of(((me // 2) ^ s) * 2 * half, 2 * half)
        att_ref[:, pl.ds(at, 2 * half)] = pair.astype(bf16)
    middle = hidden_ref[...] + times(att_ref[...], out_ref[...])
    middle_ref[...] = middle
    normed_ref[...] = (middle * norm_scale(middle) * gain_ref[...]).astype(bf16)
    for copy in saved:
        copy.wait()


def middle_forward(mine, other, w_blocks, w_own, hidden, gain, me, line, Z):
    C = len(w_blocks)
    tokens, width = hidden.shape
    half = mine[0].shape[1]
    piece = w_own.shape[0] // C
    if piece % 16 or (2 * half) % LANES:
        rows = jnp.stack(unsort([x.reshape(Z - 1, piece, width) for x in w_blocks], me), axis=1)
        rows = jnp.concatenate([w_own[None], rows.reshape(Z - 1, C * piece, width)])
        out_all = jnp.concatenate([pick(rows, line ^ j) for j in range(Z)], axis=0)
        heads = []
        for a, b in zip(mine, other, strict=True):
            heads += [a[:tokens], b[tokens:]]
        attended = jnp.concatenate(unsort(heads, me), axis=1)
        middle = hidden + times(attended, out_all)
        return middle, (middle * norm_scale(middle) * gain).astype(bf16), attended, out_all
    return pl.pallas_call(
        functools.partial(middle_forward_kernel, C, Z, piece),
        out_shape=[
            jax.ShapeDtypeStruct((tokens, width), f32),
            jax.ShapeDtypeStruct((tokens, width), bf16),
            jax.ShapeDtypeStruct((tokens, width), bf16),
            pltpu.HBM((width, width), bf16),
        ],
        in_specs=[SMEM] + [VMEM] * 2 * C + [HBM] + [VMEM] * 2,
        out_specs=[VMEM] * 3 + [HBM],
        scratch_shapes=[
            pltpu.VMEM((width, width), bf16),
            pltpu.VMEM((tokens, 2 * half), f32),
            pltpu.VMEM((tokens, 2 * half), f32),
            pltpu.SemaphoreType.DMA((2,)),
        ],
        compiler_params=pltpu.CompilerParams(vmem_limit_bytes=16 * MIB),
        cost_estimate=cost(tokens * width * width, 3 * width * width),
        name="middle_forward",
    )(jnp.stack([me, line]), *mine, *other, *w_blocks, *in_hbm(w_own), hidden, gain.reshape(1, width))


def middle_backward_kernel(R, info_ref, *refs):
    own_ref, got_refs = refs[0], refs[1:R]
    middle_ref, gain_ref, grad_out_ref, out_hbm = refs[R : R + 4]
    grad_ref, low_ref, gain_grad_ref = refs[R + 4 : R + 7]
    pair_refs, (att_ref, out_ref, sems) = refs[R + 7 : 2 * R + 7], refs[2 * R + 7 :]
    copies = started(sems, 0, (out_hbm, out_ref))
    upstream = own_ref[...]
    for ref in got_refs:
        upstream = upstream + ref[...].astype(f32)
    middle = middle_ref[...]
    back, gain_grad = norm_back(upstream, middle, norm_scale(middle), gain_ref[...])
    gain_grad_ref[...] = gain_grad.reshape(gain_grad_ref.shape)
    grad = grad_out_ref[...] + back
    grad_ref[...] = grad
    low = grad.astype(bf16)
    low_ref[...] = low
    for copy in copies:
        copy.wait()
    att_ref[...] = times_transposed(low, out_ref[...]).astype(bf16)
    pair_cols = pair_refs[0].shape[1]
    for s in range(R):
        at = pl.multiple_of(((info_ref[0] // 2) ^ s) * pair_cols, pair_cols)
        pair_refs[s][...] = att_ref[:, pl.ds(at, pair_cols)]


def middle_backward(own, got, middle, gain, grad_output, out_all, me):
    R = len(got) + 1
    tokens, width = middle.shape
    pair_cols = width // R
    if pair_cols % LANES:
        upstream = total(own, got)
        back, gain_grad = norm_back(upstream, middle, norm_scale(middle), gain)
        grad = grad_output + back
        low = grad.astype(bf16)
        cut = times_transposed(low, out_all).astype(bf16).reshape(tokens, R, pair_cols)
        return grad, low, gain_grad[None], *[pick(cut, (me // 2) ^ s, 1) for s in range(R)]
    result = pl.pallas_call(
        functools.partial(middle_backward_kernel, R),
        out_shape=[
            jax.ShapeDtypeStruct((tokens, width), f32),
            jax.ShapeDtypeStruct((tokens, width), bf16),
            jax.ShapeDtypeStruct((1, width), f32),
        ]
        + [pltpu.VMEM((tokens, pair_cols), bf16)] * R,
        in_specs=[SMEM] + [VMEM] * (R + 3) + [HBM],
        out_specs=[VMEM] * (3 + R),
        scratch_shapes=[
            pltpu.VMEM((tokens, width), bf16),
            pltpu.VMEM((width, width), bf16),
            pltpu.SemaphoreType.DMA((1,)),
        ],
        compiler_params=pltpu.CompilerParams(vmem_limit_bytes=16 * MIB),
        cost_estimate=cost(tokens * width * width, 3 * width * width),
        name="middle_backward",
    )(me.reshape(1), own, *got, middle, gain.reshape(1, width), grad_output, *in_hbm(out_all))
    return result


def out_grads_kernel(C, Z, piece, info_ref, att_ref, low_ref, *refs):
    keep_refs, give_refs, sum_ref = refs[: C // 2], refs[C // 2 : C], refs[C]
    me = info_ref[0]
    rows_z = C * piece
    sum_ref[...] = transposed_times(att_ref[...], low_ref[...])
    for i in range(C):
        ref = (give_refs if i % 2 else keep_refs)[i // 2]
        for j in range(Z):
            at = pl.multiple_of(j * rows_z + (me ^ i) * piece, piece)
            ref[j * piece : (j + 1) * piece, :] = sum_ref[pl.ds(at, piece), :].astype(bf16)


def out_grads(attended, low, me, C, Z):
    width = attended.shape[1]
    piece = width // (C * Z)
    if piece % 16:
        grad = transposed_times(attended, low).astype(bf16).reshape(Z, C, piece, width)
        grad = [pick(grad, me ^ i, 1).reshape(Z * piece, width) for i in range(C)]
        return grad[0::2], grad[1::2]
    result = pl.pallas_call(
        functools.partial(out_grads_kernel, C, Z, piece),
        out_shape=[pltpu.VMEM((Z * piece, width), bf16)] * C,
        in_specs=[SMEM, VMEM, VMEM],
        out_specs=[VMEM] * C,
        scratch_shapes=[pltpu.VMEM((width, width), f32)],
        compiler_params=pltpu.CompilerParams(vmem_limit_bytes=18 * MIB),
        cost_estimate=cost(2 * attended.shape[0] * width * width, 3 * width * width),
        name="out_grads",
    )(me.reshape(1), attended, low)
    return result[: C // 2], result[C // 2 :]


EXTRA = 16


def attention_packs_kernel(Z, C, info_ref, *refs):
    R = C // 2
    grad_ref, out_refs = refs[0], refs[1 : R + 1]
    gain_one_ref, gain_two_ref, error_ref, pack_hbm, token_ref = refs[R + 1 : R + 6]
    sum_ref, tall_ref, sems = refs[R + 6 :]
    token_ref[...] = jnp.zeros_like(token_ref)
    width, cols = grad_ref.shape
    rows, tall = width // Z, tall_ref.shape[0] // Z
    piece = sum_ref.shape[0] // Z
    out = out_refs[0][...]
    for ref in out_refs[1:]:
        out = out + ref[...].astype(f32)
    sum_ref[...] = out.astype(bf16)
    line = info_ref[0]
    row = lax.broadcasted_iota(jnp.int32, (EXTRA, cols), 0)
    lane = lax.broadcasted_iota(jnp.int32, (EXTRA, cols), 1)
    error = error_ref[0, 0]
    high = error.astype(bf16).astype(f32)
    error = jnp.where(lane == 2 * line, high, jnp.where(lane == 2 * line + 1, error - high, 0.0))
    for j in range(Z):
        under = j * tall + rows
        for n in range(width // cols):
            at = slice(n * cols, (n + 1) * cols)
            tall_ref[under + n * piece : under + (n + 1) * piece, :] = sum_ref[
                j * piece : (j + 1) * piece, at
            ]
        at = slice(j * rows, (j + 1) * rows)
        extra = jnp.where(row == 0, gain_one_ref[0:1, at], jnp.where(row == 1, gain_two_ref[0:1, at], 0.0))
        extra = jnp.where(row == 2, error, extra)
        tall_ref[(j + 1) * tall - EXTRA : (j + 1) * tall, :] = extra.astype(bf16)

    @pl.loop(0, rows // 16)
    def _(n):
        for j in range(Z):
            at = pl.ds(pl.multiple_of(j * rows + n * 16, 16), 16)
            to = pl.ds(pl.multiple_of(j * tall + n * 16, 16), 16)
            tall_ref[to, :] = grad_ref[at, :]

    for copy in started(sems, 0, (tall_ref, pack_hbm)):
        copy.wait()


def attention_packs(grad, out_parts, gain_one, gain_two, error, line, Z, C):
    width, cols = grad.shape
    rows = width // Z
    tall, parts = out_parts[0].shape[0], C // 2
    piece = tall // Z
    if rows != cols or piece % 16:
        grad_out = total(out_parts[0], out_parts[1:]).astype(bf16)
        lane = jnp.arange(cols, dtype=jnp.int32)
        high = error.astype(bf16)
        low = (error - high.astype(f32)).astype(bf16)
        zero = jnp.zeros((), bf16)
        error_row = jnp.where(lane == 2 * line, high, jnp.where(lane == 2 * line + 1, low, zero))
        packs = []
        for j in range(Z):
            at = slice(j * rows, (j + 1) * rows)
            out = grad_out[j * piece : (j + 1) * piece]
            gains = [jnp.pad(x[at].astype(bf16), (0, cols - rows)) for x in (gain_one[0], gain_two[0])]
            extra = jnp.pad(jnp.stack([*gains, error_row]), ((0, EXTRA - 3), (0, 0)))
            packs += [grad[at], *[out[:, c : c + cols] for c in range(0, width, cols)], extra]
        return jnp.concatenate(packs, axis=0), jnp.zeros((8, LANES), f32)
    shape = (Z * (rows + piece * width // cols + EXTRA), cols)
    return pl.pallas_call(
        functools.partial(attention_packs_kernel, Z, C),
        out_shape=[pltpu.HBM(shape, bf16), jax.ShapeDtypeStruct((8, LANES), f32)],
        in_specs=[SMEM] + [VMEM] * (parts + 4),
        out_specs=[HBM, VMEM],
        scratch_shapes=[
            pltpu.VMEM((tall, width), bf16),
            pltpu.VMEM(shape, bf16),
            pltpu.SemaphoreType.DMA((1,)),
        ],
        compiler_params=pltpu.CompilerParams(vmem_limit_bytes=16 * MIB),
        cost_estimate=cost(0, 3 * width * width),
        name="attention_packs",
    )(line.reshape(1), grad, *out_parts, gain_one, gain_two, error.reshape(1, 1))


def attention_grads_kernel(C, rows, q_cols, kv_cols, places, me_ref, *refs):
    count = len(places)
    gain_ref, valid_ref = refs[count : count + 2]
    *grads_hbm, gains_ref, loss_ref = refs[count + 2 : count + 8]
    low_ref, extra_ref, query_ref, key_ref, value_ref, out_ref, in_sems, out_sems = refs[count + 8 :]
    me = me_ref[0]
    cols = low_ref.shape[2]
    strips = out_ref.shape[1] // cols
    piece = (low_ref.shape[1] - rows - EXTRA) // strips
    arriving = arrived([(*place, ref) for place, ref in zip(places, refs)], low_ref, in_sems)
    for i in range(C):
        for copy in arriving[i]:
            copy.wait()
        at = pl.ds(pl.multiple_of((me ^ i) * piece, piece), piece)
        for c in range(strips):
            strip = low_ref[i, rows + c * piece : rows + (c + 1) * piece, :]
            out_ref[at, c * cols : (c + 1) * cols] = strip.astype(f32)
        extra_ref[me ^ i] = low_ref[i, low_ref.shape[1] - EXTRA :, :].astype(f32)
    leaving = started(out_sems, 3, (out_ref, grads_hbm[3]))
    extra = extra_ref[0]
    for b in range(1, C):
        extra = extra + extra_ref[b]
    row = lax.broadcasted_iota(jnp.int32, gains_ref.shape, 0)
    gains_ref[...] = extra[:8, :] / jnp.where(row == 0, gain_ref[...], 1.0)
    loss_ref[...] = jnp.sum(extra[2:3, :], axis=1, keepdims=True) / valid_ref[0, 0]
    lane = lax.broadcasted_iota(jnp.int32, (rows, cols), 1)
    for n, (ref, first, size) in enumerate(
        (
            (query_ref, 0, q_cols),
            (key_ref, q_cols, kv_cols),
            (value_ref, q_cols + kv_cols, kv_cols),
        )
    ):
        many = cols // size
        for group in range(C // many):
            whole = None
            for j in range(many):
                x = low_ref[me ^ (group * many + j), :rows, :].astype(f32)
                shift = (j * size - first) % cols
                x = pltpu.roll(x, shift, 1) if shift else x
                whole = x if whole is None else jnp.where(lane < j * size, whole, x)
            ref[:, group * cols : (group + 1) * cols] = whole
        leaving += started(out_sems, n, (ref, grads_hbm[n]))
    for copy in leaving:
        copy.wait()


def attention_grads(pieces, me, gain, valid_count, C, rows, width, q_cols, kv_cols, kv_copies):
    tall, cols = pieces[0][2].shape
    strips = width // cols
    piece = (tall - rows - EXTRA) // strips
    many = C // kv_copies
    if kv_copies > 1 or cols % q_cols or cols % kv_cols or q_cols + 2 * kv_cols != cols or rows != cols or piece % 16:
        parts = unsort([x[2] for x in pieces], me)

        def kv_final(start):
            own = [part[:rows, start : start + kv_cols].astype(f32) for part in parts]
            own = [sum(own[n : n + kv_copies]) for n in range(0, C, kv_copies)]
            return jnp.concatenate(own, axis=1)

        query = jnp.concatenate([part[:rows, :q_cols] for part in parts], axis=1).astype(f32)
        outs = [part[rows : tall - EXTRA].reshape(strips, piece, cols).transpose(1, 0, 2) for part in parts]
        out = jnp.concatenate([x.reshape(piece, width) for x in outs], axis=0).astype(f32)
        extra = sum([part[tall - EXTRA :].astype(f32) for part in parts])
        gains = extra[0, :rows] / gain, extra[1, :rows]
        loss = jnp.sum(extra[2]) / valid_count
        return query, kv_final(q_cols), kv_final(q_cols + kv_cols), out, *gains, loss
    shapes = [(rows, C * q_cols), (rows, many * kv_cols), (rows, many * kv_cols), (C * piece, width)]
    *grads, gains, loss = pl.pallas_call(
        functools.partial(
            attention_grads_kernel, C, rows, q_cols, kv_cols, [x[:2] for x in pieces]
        ),
        out_shape=[
            *[pltpu.HBM(x, f32) for x in shapes],
            jax.ShapeDtypeStruct((8, cols), f32),
            jax.ShapeDtypeStruct((1, 1), f32),
        ],
        in_specs=[SMEM] + [HBM] * len(pieces) + [VMEM] * 2,
        out_specs=[HBM] * 4 + [VMEM] * 2,
        scratch_shapes=[
            pltpu.VMEM((C, tall, cols), bf16),
            pltpu.VMEM((C, EXTRA, cols), f32),
            *[pltpu.VMEM(x, f32) for x in shapes],
            pltpu.SemaphoreType.DMA((len(pieces),)),
            pltpu.SemaphoreType.DMA((4,)),
        ],
        compiler_params=pltpu.CompilerParams(vmem_limit_bytes=24 * MIB),
        cost_estimate=cost(0, 8 * rows * C * cols),
        name="attention_grads",
    )(
        me.reshape(1),
        *in_hbm(*[x[2] for x in pieces]),
        gain.reshape(1, rows),
        valid_count.reshape(1, 1),
    )
    return *grads, gains[0], gains[1], loss[0, 0]


def local(
    inputs,
    teacher,
    lengths,
    w_query,
    w_key,
    w_value,
    w_out,
    w_gate,
    w_up,
    w_down,
    gain_attn,
    gain_ffn,
):
    hidden_in = inputs[0]
    target = teacher[0]
    seq_length = lengths[0]
    tokens, width = hidden_in.shape
    C = lax.axis_size("ctx")
    Z = lax.axis_size("fsdp")
    R = C // 2
    p = lax.axis_index("ctx")
    z = lax.axis_index("fsdp")
    core = p % 2
    rows_z = width // Z
    seq = C * tokens
    q_heads = HEADS // C
    kv_heads = max(1, KV_HEADS // C)
    kv_copies = max(1, C // KV_HEADS)
    q_cols = q_heads * HEAD_DIM
    kv_cols = kv_heads * HEAD_DIM
    qkv_cols = q_cols + 2 * kv_cols
    positions = p * tokens + jnp.arange(tokens, dtype=jnp.int32)

    kv_start = (p * KV_HEADS // C) * HEAD_DIM
    out_piece = rows_z // C
    qkv_own = jnp.concatenate(
        [
            lax.dynamic_slice_in_dim(w_query, p * q_cols, q_cols, 1),
            lax.dynamic_slice_in_dim(w_key, kv_start, kv_cols, 1),
            lax.dynamic_slice_in_dim(w_value, kv_start, kv_cols, 1),
            jnp.zeros((rows_z, -qkv_cols % LANES), bf16),
        ],
        axis=1,
    )
    out_own = lax.dynamic_slice_in_dim(w_out, p * out_piece, out_piece, 0)

    small = jnp.concatenate(
        [gain_attn.astype(f32), gain_ffn.astype(f32), jnp.full((LANES,), seq_length).astype(f32)]
    )
    small = after(small.reshape(1, -1), qkv_own)
    small = jnp.stack(unsort(line_blocks(small), z)).reshape(Z, -1)
    gain_one = small[:, :rows_z].reshape(width)
    gain_two = small[:, rows_z : 2 * rows_z].reshape(width)
    valid_count = jnp.sum(small[:, 2 * rows_z])
    ff = w_gate.shape[1]
    ff_piece, own = ff // (Z * C), ff // C
    packed_ffn = ff_piece % LANES == 0
    if packed_ffn:
        cuts = Z
        gate_up_own, down_own = ffn_slices(w_gate, w_up, w_down, p, C, Z)
    else:
        cuts = 1
        gate_up_own = jnp.concatenate(
            [pick(w.reshape(rows_z, Z, C, ff_piece), p, 2).reshape(rows_z, own) for w in (w_gate, w_up)],
            axis=1,
        )
        down_own = lax.dynamic_slice_in_dim(w_down, p * ff_piece, ff_piece, 0)
    scale_one = norm_scale(hidden_in)
    normed_one = (hidden_in * scale_one * gain_one).astype(bf16)
    tables = rope_tables(seq)
    normed_got, weights, tables = lax.optimization_barrier(
        (plane_sends(normed_one), line_sends(qkv_own), tables)
    )
    normed_blocks = together(core_blocks([normed_one] + normed_got))
    gate_up_own, down_own = after((gate_up_own, down_own), weights)
    gate_up = lax.all_gather(gate_up_own, "fsdp", axis=0, tiled=True)
    down_rows = lax.all_gather(down_own, "fsdp", axis=0, tiled=True)
    out_line = line_sends(after(out_own, weights))
    (normed_all, *saved), mine = attention_forward(
        normed_blocks, [qkv_own] + weights, tables, p, seq_length, z, q_heads, kv_heads
    )

    out_line, normed_all = lax.optimization_barrier((out_line, normed_all))
    out_line = jnp.concatenate(out_line, axis=0)
    out_blocks = together(core_blocks([out_line] + together(plane_sends(out_line))))
    mine = after(mine, out_blocks)
    mine = [mine[0]] + together([partner(mine[s], "ctx", 2 * s) for s in range(1, R)])
    other = [partner(x, "ctx", 1) for x in mine]
    middle, normed_two_own, attended_tokens, out_all = middle_forward(
        mine, other, out_blocks, w_out, hidden_in, gain_two, p, z, Z
    )

    normed_two, coef, activated = ffn_units(plane_blocks(normed_two_own), gate_up, cuts)
    keep, give = ffn_forward(activated, after(down_rows, activated), C)
    output = middle + plane_reduce(keep, give)

    valid_rows = (positions < seq_length).astype(f32)
    residual_error = output - target
    squares = jnp.sum(valid_rows[:, None] * residual_error * residual_error)
    grad_output = valid_rows[:, None] * (2.0 * residual_error) / valid_count

    (grad_low, grad_gu), keep, give = ffn_backward(
        plane_blocks(grad_output.astype(bf16)), gate_up, down_rows, coef, cuts
    )
    chips = chip_sums(keep, give)
    grad_gate_up = transposed_times(normed_two, after(grad_gu, chips)).astype(bf16)
    grad_down = transposed_times(activated, after(grad_low, grad_gate_up)).astype(bf16)
    shard_gate_up = lax.psum_scatter(grad_gate_up, "fsdp", scatter_dimension=0, tiled=True)
    shard_down = lax.psum_scatter(grad_down, "fsdp", scatter_dimension=0, tiled=True)
    grad_middle, m_low, grad_gain_two, *pairs = middle_backward(
        chips[0], after(chip_sends(chips), grad_down), middle, gain_two, grad_output, out_all, p
    )

    out_keep, out_give = out_grads(attended_tokens, after(m_low, pairs), p, C, Z)
    out_chips = chip_sums(out_keep, out_give)
    mine = [partner(pairs[s], "ctx", 2 * s) for s in range(1, R)]
    mine = [pairs[0]] + list(after(mine, out_chips))
    other = [partner(x, "ctx", 1) for x in mine]
    grad_qkv, gain_part, keep, give = attention_backward(
        mine, other, (normed_all, *saved), tables, p, seq_length, q_heads, kv_heads
    )
    chips = chip_sums(keep, give)
    square = packed_ffn and C == 8
    out_got, grad_qkv = lax.optimization_barrier((chip_sends(out_chips), grad_qkv))
    packs, token = attention_packs(
        grad_qkv, [out_chips[0]] + out_got, gain_part, grad_gain_two, squares, z, Z, C
    )
    shard_packs = lax.psum_scatter(packs, "fsdp", scatter_dimension=0, tiled=True)
    normed_got = [partner(x, "ctx", 2 * (s + 1)) for s, x in enumerate(after(chips[1:], out_got))]
    near = near_sends(after(shard_gate_up, out_got)) if square else []
    normed_got, near, token = lax.optimization_barrier((normed_got, near, token))
    grad_normed_one = total(chips[0], normed_got)
    back_one, _ = norm_back(grad_normed_one, hidden_in, scale_one, gain_one)
    grad_hidden = grad_middle + back_one


    if square:
        down_near = near_sends(after(shard_down, normed_got))
        far, down_near = lax.optimization_barrier((far_sends(near), down_near))
        pieces = square_pieces(shard_gate_up, near, far)
        final_gate, final_up = column_grads(pieces, p, C, Z)
        pack_near = near_sends(after(shard_packs, far))
        down_far, pack_near, final_gate = lax.optimization_barrier(
            (far_sends(down_near), pack_near, final_gate)
        )
        final_down = row_grads(square_pieces(shard_down, down_near, down_far), p, C)
        pack_far, final_down, grad_hidden = lax.optimization_barrier(
            (far_sends(pack_near), final_down, grad_hidden)
        )
        pieces = square_pieces(shard_packs, pack_near, pack_far)
    else:
        pieces = [(i, 0, block) for i, block in enumerate(plane_blocks(shard_packs))]
        gate_up, down = [
            jnp.stack(unsort(plane_blocks(x), p)).astype(f32) for x in (shard_gate_up, shard_down)
        ]
        gate_up = gate_up.reshape(C, rows_z, 2, Z, ff_piece).transpose(2, 1, 3, 0, 4)
        final_gate, final_up = gate_up.reshape(2, rows_z, ff)
        final_down = down.reshape(C * ff_piece, width)
    final_query, final_key, final_value, final_out, *final_gains, loss_value = attention_grads(
        pieces,
        p,
        gain_attn.astype(f32),
        valid_count,
        C,
        rows_z,
        width,
        q_cols,
        kv_cols,
        kv_copies,
    )

    return (
        output[None],
        loss_value,
        grad_hidden[None],
        final_query,
        final_key,
        final_value,
        final_out,
        final_gate,
        final_up,
        final_down,
        *final_gains,
    )


def solution(mesh):
    return jax.shard_map(
        local,
        mesh=mesh,
        in_specs=(
            P("fsdp", "ctx", None),
            P("fsdp", "ctx", None),
            P("fsdp"),
            P("fsdp", None),
            P("fsdp", None),
            P("fsdp", None),
            P("fsdp", None),
            P("fsdp", None),
            P("fsdp", None),
            P("fsdp", None),
            P("fsdp"),
            P("fsdp"),
        ),
        out_specs=(
            P("fsdp", "ctx", None),
            P(),
            P("fsdp", "ctx", None),
            P("fsdp", None),
            P("fsdp", None),
            P("fsdp", None),
            P("fsdp", None),
            P("fsdp", None),
            P("fsdp", None),
            P("fsdp", None),
            P("fsdp"),
            P("fsdp"),
        ),
        check_vma=False,
    )
```

```python
import functools

import jax
import jax.numpy as jnp
from jax import lax
from jax.experimental import pallas as pl
from jax.experimental.pallas import tpu as pltpu
from jax.sharding import PartitionSpec as P

HEADS = 16
KV_HEADS = 8
HEAD_DIM = 96
LANES = 128

eps_norm = 1e-05
rope_base = 100000.0
masked_value = -1e30

f32 = jnp.float32
bf16 = jnp.bfloat16

VMEM = pl.BlockSpec(memory_space=pltpu.VMEM)
SMEM = pl.BlockSpec(memory_space=pltpu.SMEM)
HBM = pl.BlockSpec(memory_space=pltpu.HBM)
MIB = 1024 * 1024


def cost(multiply_adds, values):
    return pl.CostEstimate(flops=1, bytes_accessed=1, transcendentals=0)


def in_hbm(*xs):
    return [pltpu.with_memory_space_constraint(x, pltpu.HBM) for x in xs]


def started(sems, first, *pairs):
    copies = [pltpu.make_async_copy(a, b, sems.at[first + n]) for n, (a, b) in enumerate(pairs)]
    for copy in copies:
        copy.start()
    return copies


def times(left, right):
    return jnp.dot(left, right, preferred_element_type=f32)


def times_transposed(left, right):
    return lax.dot_general(left, right, (((1,), (1,)), ((), ())), preferred_element_type=f32)


def transposed_times(left, right):
    return lax.dot_general(left, right, (((0,), (0,)), ((), ())), preferred_element_type=f32)


def norm_scale(features):
    return lax.rsqrt(jnp.mean(features * features, axis=-1, keepdims=True) + eps_norm)


def norm_back(upstream, features, row_scale, gain_vector):
    weighted = upstream * gain_vector
    inner_mean = jnp.mean(weighted * features, axis=-1, keepdims=True)
    grad_rows = row_scale * weighted - features * (row_scale * row_scale * row_scale) * inner_mean
    return (grad_rows, jnp.sum(upstream * (features * row_scale), axis=0))


def partner(x, axis, mask):
    return lax.ppermute(x, axis, [(i, i ^ mask) for i in range(lax.axis_size(axis))])


def plane_sends(x):
    return [partner(x, "ctx", 2 * s) for s in range(1, lax.axis_size("ctx") // 2)]


def core_blocks(mine):
    blocks = []
    for x in mine:
        blocks += [x, partner(x, "ctx", 1)]
    return blocks


def plane_blocks(x):
    return core_blocks([x] + plane_sends(x))


def near_sends(x):
    return [partner(x, "ctx", 2), partner(x, "ctx", 4)]


def far_sends(near):
    half = near[0].shape[0] // 32 * 16
    return [partner(near[0][:half], "ctx", 4), partner(near[1][half:], "ctx", 2)]


def square_pieces(x, near, far):
    half = x.shape[0] // 32 * 16
    mine = [(0, 0, x), (1, 0, near[0]), (2, 0, near[1]), (3, 0, far[0]), (3, half, far[1])]
    other = together([partner(block, "ctx", 1) for _, _, block in mine])
    pieces = []
    for (s, first, block), swapped in zip(mine, other, strict=True):
        pieces += [(2 * s, first, block), (2 * s + 1, first, swapped)]
    return pieces


def line_sends(x):
    return [partner(x, "fsdp", s) for s in range(1, lax.axis_size("fsdp"))]


def plane_reduce(keep, give):
    chips = chip_sums(keep, give)
    return total(chips[0], chip_sends(chips))


def chip_sums(keep, give):
    got = [partner(x, "ctx", 1) for x in give[::-1]][::-1]
    own = keep[0].astype(f32) + got[0].astype(f32)
    return [own] + [
        (a.astype(f32) + b.astype(f32)).astype(bf16) for a, b in zip(keep[1:], got[1:], strict=True)
    ]


def chip_sends(chips):
    return together([partner(chips[s], "ctx", 2 * s) for s in range(len(chips) - 1, 0, -1)])


def total(own, got):
    for x in got:
        own = own + x.astype(f32)
    return own


def tree_sum(x, axis):
    mask = 1
    while mask < lax.axis_size(axis):
        x = x + partner(x, axis, mask)
        mask *= 2
    return x


def line_blocks(x):
    return [x] + together(line_sends(x))


def line_reduce(parts):
    got = together([partner(parts[s], "fsdp", s) for s in range(1, len(parts))])
    return total(parts[0].astype(f32), got)


def together(xs):
    return list(lax.optimization_barrier(tuple(xs)))


def after(x, *done):
    return lax.optimization_barrier((x, done))[0]


def pick(x, index, axis=0):
    return lax.dynamic_index_in_dim(x, index, axis, False)


def unsort(blocks, me):
    stacked = jnp.stack(blocks)
    return [pick(stacked, me ^ b) for b in range(len(blocks))]


def rope_tables(count):
    half_dim = HEAD_DIM // 2
    frequencies = rope_base ** (-(jnp.arange(half_dim, dtype=f32) * 2.0) / HEAD_DIM)
    angles = jnp.arange(count, dtype=f32)[:, None] * frequencies[None, :]
    cosines, sines = jnp.cos(angles), jnp.sin(angles)
    pad = jnp.zeros((count, LANES - HEAD_DIM), f32)
    return (
        jnp.concatenate([cosines, cosines, pad], axis=1),
        jnp.concatenate([-sines, sines, pad], axis=1),
    )


def turned(x):
    lane = lax.broadcasted_iota(jnp.int32, x.shape, 1)
    half_dim = HEAD_DIM // 2
    return jnp.where(
        lane < half_dim, pltpu.roll(x, LANES - half_dim, 1), pltpu.roll(x, half_dim, 1)
    )


def head_of(x, head):
    if head:
        x = pltpu.roll(x, x.shape[1] - head * HEAD_DIM, 1)
    return x[:, :LANES]


def packed(heads):
    wide = -(-len(heads) * HEAD_DIM // LANES) * LANES
    total = None
    for index, head in enumerate(heads):
        if wide > LANES:
            head = jnp.concatenate([head, jnp.zeros((head.shape[0], wide - LANES), f32)], axis=1)
        if index:
            head = pltpu.roll(head, index * HEAD_DIM, 1)
        total = head if total is None else total + head
    return total


def attention_forward_kernel(C, Z, tokens, q_heads, kv_heads, block, info_ref, *refs):
    R = C // 2
    n_refs, w_parts = refs[:C], refs[C : C + Z]
    cos_hbm, sin_hbm = refs[C + Z : C + Z + 2]
    n_hbm, w_hbm, qkv_hbm, att_hbm, lse_hbm = refs[C + Z + 2 : C + Z + 7]
    block_refs = refs[C + Z + 7 : C + Z + 7 + R]
    n_all_ref, w_ref, lin_ref, qkv_ref, att_ref, lse_ref, cos_ref, sin_ref, sems = refs[C + Z + 7 + R :]
    me, length = info_ref[0], info_ref[1]
    seq = C * tokens
    group = q_heads // kv_heads
    width_low = q_heads * HEAD_DIM
    rows_z = w_ref.shape[0] // Z
    pairs = []
    for j in range(Z):
        at = pl.multiple_of((info_ref[2] ^ j) * rows_z, rows_z)
        pairs.append((w_parts[j].at[:rows_z, :], w_ref.at[pl.ds(at, rows_z), :]))
    tables = started(sems, 0, (cos_hbm, cos_ref), (sin_hbm, sin_ref), *pairs)
    for i in range(C):
        n_all_ref[i * tokens : (i + 1) * tokens, :] = n_refs[i][...]
    for copy in tables[2:]:
        copy.wait()
    saved = started(sems, 2, (n_all_ref, n_hbm), (w_ref, w_hbm))
    step = 4 * tokens
    for start in range(0, seq, step):
        lin_ref[start : start + step, :] = times(n_all_ref[start : start + step, :], w_ref[...])
    for copy in tables[:2]:
        copy.wait()
    lane = lax.broadcasted_iota(jnp.int32, (tokens, LANES), 1)
    for i in range(C):
        rows = pl.ds(pl.multiple_of((me ^ i) * tokens, tokens), tokens)
        lin = lin_ref[i * tokens : (i + 1) * tokens, :]
        cosines, sines = cos_ref[rows, :], sin_ref[rows, :]
        for head in range(q_heads + 2 * kv_heads):
            x = head_of(lin, head)
            if head < q_heads + kv_heads:
                x = x * cosines + turned(x) * sines
            else:
                x = jnp.where(lane < HEAD_DIM, x, 0.0)
            qkv_ref[rows, head * LANES : (head + 1) * LANES] = x.astype(bf16)
    saved += started(sems, 4, (qkv_ref, qkv_hbm))
    scale = HEAD_DIM ** (-0.5)
    for head in range(q_heads):
        k_at = (q_heads + head // group) * LANES
        v_at = k_at + kv_heads * LANES
        for start in range(0, seq, block):
            end = start + block
            q = qkv_ref[start:end, head * LANES : (head + 1) * LANES]
            scores = times_transposed(q, qkv_ref[:end, k_at : k_at + LANES]) * scale
            row = start + lax.broadcasted_iota(jnp.int32, (block, end), 0)
            col = lax.broadcasted_iota(jnp.int32, (block, end), 1)
            scores = jnp.where((col <= row) & (col < length), scores, masked_value)
            row_max = jnp.max(scores, axis=1, keepdims=True)
            weights = jnp.exp(scores - row_max)
            row_sum = jnp.sum(weights, axis=1, keepdims=True)
            probs = (weights * (1.0 / row_sum)).astype(bf16)
            att_ref[start:end, head * LANES : (head + 1) * LANES] = times(
                probs, qkv_ref[:end, v_at : v_at + LANES]
            )
            lse_ref[start:end, head : head + 1] = row_max + jnp.log(row_sum)
    saved += started(sems, 5, (att_ref, att_hbm), (lse_ref, lse_hbm))
    for i in range(C):
        rows = pl.ds(pl.multiple_of((me ^ i) * tokens, tokens), tokens)
        x = att_ref[rows, :]
        low = packed([x[:, h * LANES : (h + 1) * LANES] for h in range(q_heads)])
        at = (i % 2) * tokens
        block_refs[i // 2][at : at + tokens, :] = low[:, :width_low].astype(bf16)
    for copy in saved:
        copy.wait()


def attention_forward(blocks, w_parts, tables, me, length, line, q_heads, kv_heads):
    C, Z = len(blocks), len(w_parts)
    tokens, width = blocks[0].shape
    seq = C * tokens
    heads = q_heads + 2 * kv_heads
    cols = w_parts[0].shape[1]
    saved = [
        ((seq, width), bf16),
        ((width, cols), bf16),
        ((seq, heads * LANES), bf16),
        ((seq, q_heads * LANES), f32),
        ((seq, LANES), f32),
    ]
    part = jax.ShapeDtypeStruct((2 * tokens, q_heads * HEAD_DIM), bf16)
    result = pl.pallas_call(
        functools.partial(attention_forward_kernel, C, Z, tokens, q_heads, kv_heads, 2 * tokens),
        out_shape=[pltpu.HBM(*x) for x in saved] + [part] * (C // 2),
        in_specs=[SMEM] + [VMEM] * C + [HBM] * (Z + 2),
        out_specs=[HBM] * len(saved) + [VMEM] * (C // 2),
        scratch_shapes=[pltpu.VMEM(*saved[0]), pltpu.VMEM(*saved[1]), pltpu.VMEM((seq, cols), f32)]
        + [pltpu.VMEM(*x) for x in saved[2:]]
        + [pltpu.VMEM((seq, LANES), f32)] * 2
        + [pltpu.SemaphoreType.DMA((7 + Z,))],
        compiler_params=pltpu.CompilerParams(vmem_limit_bytes=22 * MIB),
        cost_estimate=cost(seq * width * cols + 2 * seq * seq * heads * LANES, 3 * seq * width),
        name="attention_forward",
    )(jnp.stack([me, length, line]).astype(jnp.int32), *blocks, *in_hbm(*w_parts, *tables))
    return result[: len(saved)], result[len(saved) :]


def attention_backward_kernel(C, tokens, q_heads, kv_heads, block, info_ref, *refs):
    R = C // 2
    mine_refs, other_refs = refs[:R], refs[R:C]
    hbm_refs = refs[C : C + 7]
    grad_w_ref, gain_ref = refs[C + 7 : C + 9]
    keep_refs = refs[C + 9 : C + 9 + R]
    give_refs = refs[C + 9 + R : C + 9 + C]
    refs = refs[C + 9 + C :]
    qkv_ref, att_ref, lse_ref, cos_ref, sin_ref, w_ref, n_all_ref = refs[:7]
    wide_ref, grad_ref, dq_ref, dkv_ref, dqkv_ref, sems = refs[7:]
    copies = started(sems, 0, *zip(hbm_refs, refs[:7], strict=True))
    me, length = info_ref[0], info_ref[1]
    core = me % 2
    seq = C * tokens
    group = q_heads // kv_heads
    width_low = q_heads * HEAD_DIM
    lane = lax.broadcasted_iota(jnp.int32, (tokens, LANES), 1)
    wide_ref[...] = jnp.zeros_like(wide_ref)
    for i in range(C):
        rows = pl.ds(pl.multiple_of((me ^ i) * tokens, tokens), tokens)
        wide_ref[:, : 2 * width_low] = (other_refs if i % 2 else mine_refs)[i // 2][...].astype(f32)
        wide = wide_ref[...]
        wide = jnp.where(core == 0, wide, pltpu.roll(wide, wide.shape[1] - width_low, 1))
        for head in range(q_heads):
            x = jnp.where(lane < HEAD_DIM, head_of(wide, head), 0.0)
            grad_ref[rows, head * LANES : (head + 1) * LANES] = x.astype(bf16)
    dkv_ref[...] = jnp.zeros_like(dkv_ref)
    scale = HEAD_DIM ** (-0.5)
    for copy in copies[:5]:
        copy.wait()
    for start in range(0, seq, block):
        end = start + block
        lane_b = lax.broadcasted_iota(jnp.int32, (block, LANES), 1)
        delta = jnp.zeros((block, LANES), f32)
        for head in range(q_heads):
            at = slice(head * LANES, (head + 1) * LANES)
            one = jnp.sum(
                grad_ref[start:end, at].astype(f32) * att_ref[start:end, at], axis=1, keepdims=True
            )
            delta = jnp.where(lane_b == head, one, delta)
        delta_t = delta.T
        lse_t = lse_ref[start:end, :].T
        key = lax.broadcasted_iota(jnp.int32, (end, block), 0)
        query = start + lax.broadcasted_iota(jnp.int32, (end, block), 1)
        allowed = (key <= query) & (key < length)
        for head in range(q_heads):
            at = slice(head * LANES, (head + 1) * LANES)
            kv = head // group
            k_at = slice((q_heads + kv) * LANES, (q_heads + kv + 1) * LANES)
            v_at = slice((q_heads + kv_heads + kv) * LANES, (q_heads + kv_heads + kv + 1) * LANES)
            q, grad = qkv_ref[start:end, at], grad_ref[start:end, at]
            k, v = qkv_ref[:end, k_at], qkv_ref[:end, v_at]
            scores = times_transposed(k, q) * scale
            probs = jnp.where(allowed, jnp.exp(scores - lse_t[head : head + 1, :]), 0.0)
            grad_probs = times_transposed(v, grad)
            grad_scores = (probs * (grad_probs - delta_t[head : head + 1, :])).astype(bf16)
            dq_ref[start:end, at] = transposed_times(grad_scores, k) * scale
            dk_at = slice(kv * LANES, (kv + 1) * LANES)
            dv_at = slice((kv_heads + kv) * LANES, (kv_heads + kv + 1) * LANES)
            dkv_ref[:end, dk_at] += times(grad_scores, q) * scale
            dkv_ref[:end, dv_at] += times(probs.astype(bf16), grad)
    for i in range(C):
        rows = pl.ds(pl.multiple_of((me ^ i) * tokens, tokens), tokens)
        cosines, sines = cos_ref[rows, :], sin_ref[rows, :]
        heads = []
        for head in range(q_heads + 2 * kv_heads):
            if head < q_heads:
                x = dq_ref[rows, head * LANES : (head + 1) * LANES]
            else:
                x = dkv_ref[rows, (head - q_heads) * LANES : (head - q_heads + 1) * LANES]
            if head < q_heads + kv_heads:
                x = x * cosines - turned(x) * sines
            heads.append(x)
        dqkv_ref[i * tokens : (i + 1) * tokens, :] = packed(heads).astype(bf16)
    for copy in copies[5:]:
        copy.wait()

    def rows_of(at):
        part = times_transposed(dqkv_ref[...], w_ref[at, :])
        gain = jnp.sum(part * n_all_ref[:, at].astype(f32), axis=0, keepdims=True)
        gain_ref[:, at] = jnp.broadcast_to(gain, (gain_ref.shape[0], gain.shape[1]))
        return part

    parts_of(rows_of, keep_refs, give_refs)
    step = 3 * LANES

    @pl.loop(0, grad_w_ref.shape[0] // step)
    def _(n):
        at = pl.ds(pl.multiple_of(n * step, step), step)
        grad_w_ref[at, :] = transposed_times(n_all_ref[:, at], dqkv_ref[...]).astype(bf16)


def attention_backward(mine, other, saved, tables, me, length, q_heads, kv_heads):
    C = 2 * len(mine)
    tokens, pair = mine[0].shape
    normed_all, w_qkv, qkv, attended, lse = saved
    width, cols = w_qkv.shape
    loaded = (qkv, attended, lse, *tables, w_qkv, normed_all)
    seq = C * tokens
    heads = q_heads + 2 * kv_heads
    part = jax.ShapeDtypeStruct((tokens, width), bf16)
    result = pl.pallas_call(
        functools.partial(attention_backward_kernel, C, tokens, q_heads, kv_heads, 2 * tokens),
        out_shape=[
            jax.ShapeDtypeStruct((width, cols), bf16),
            jax.ShapeDtypeStruct((8, width), f32),
        ]
        + [part] * C,
        in_specs=[SMEM] + [VMEM] * C + [HBM] * 7,
        out_specs=[VMEM] * (C + 2),
        scratch_shapes=[pltpu.VMEM(x.shape, x.dtype) for x in loaded]
        + [
            pltpu.VMEM((tokens, -(-pair // LANES) * LANES), f32),
            pltpu.VMEM((seq, q_heads * LANES), bf16),
            pltpu.VMEM((seq, q_heads * LANES), f32),
            pltpu.VMEM((seq, 2 * kv_heads * LANES), f32),
            pltpu.VMEM((seq, cols), bf16),
            pltpu.SemaphoreType.DMA((7,)),
        ],
        compiler_params=pltpu.CompilerParams(vmem_limit_bytes=28 * MIB),
        cost_estimate=cost(seq * width * cols + 4 * seq * seq * heads * LANES, 3 * seq * width),
        name="attention_backward",
    )(jnp.stack([me, length]).astype(jnp.int32), *mine, *other, *in_hbm(*loaded))
    return result[0], result[1], result[2 : 2 + C // 2], result[2 + C // 2 :]


def gather_rows(block_refs, all_ref):
    tokens = block_refs[0].shape[0]

    @pl.loop(0, tokens // 16)
    def _(n):
        for i, ref in enumerate(block_refs):
            at = pl.ds(pl.multiple_of(n * 16, 16), 16)
            to = pl.ds(pl.multiple_of(i * tokens + n * 16, 16), 16)
            all_ref[to, :] = ref[at, :]


def parts_of(rows_of, keep_refs, give_refs):
    tokens, width = keep_refs[0].shape
    strip = 4 * LANES

    @pl.loop(0, width // strip)
    def _(n):
        at = pl.ds(pl.multiple_of(n * strip, strip), strip)
        part = rows_of(at)
        for i in range(2 * len(keep_refs)):
            ref = (give_refs if i % 2 else keep_refs)[i // 2]
            ref[:, at] = part[i * tokens : (i + 1) * tokens, :].astype(bf16)


def ffn_units_kernel(C, cuts, *refs):
    n_refs = refs[:C]
    gu_hbm, n_hbm, coef_hbm, act_ref = refs[C : C + 4]
    gu_ref, n_all_ref, coef_ref, sems = refs[C + 4 :]
    tokens = n_refs[0].shape[0]
    pairs = [(n_refs[i], n_all_ref.at[i * tokens : (i + 1) * tokens, :]) for i in range(C)]
    for copy in started(sems, 0, (gu_hbm, gu_ref), *pairs):
        copy.wait()
    saved = started(sems, 0, (n_all_ref, n_hbm))
    w = act_ref.shape[1] // cuts

    @pl.loop(0, cuts)
    def _(j):
        at = pl.ds(pl.multiple_of(j * 2 * w, 2 * w), 2 * w)
        both = times(n_all_ref[...], gu_ref[:, at])
        gate, up = both[:, :w], both[:, w:]
        sigmoid = jax.nn.sigmoid(gate)
        silu = gate * sigmoid
        act_ref[:, pl.ds(pl.multiple_of(j * w, w), w)] = (silu * up).astype(bf16)
        slope = up * (sigmoid * (1.0 + gate * (1.0 - sigmoid)))
        coef_ref[:, at] = jnp.concatenate([slope, silu], axis=1).astype(bf16)

    saved += started(sems, 1, (coef_ref, coef_hbm))
    for copy in saved:
        copy.wait()


def ffn_units(blocks, gate_up, cuts):
    C = len(blocks)
    tokens, width = blocks[0].shape
    seq, both = C * tokens, gate_up.shape[1]
    return pl.pallas_call(
        functools.partial(ffn_units_kernel, C, cuts),
        out_shape=[
            pltpu.HBM((seq, width), bf16),
            pltpu.HBM((seq, both), bf16),
            jax.ShapeDtypeStruct((seq, both // 2), bf16),
        ],
        in_specs=[HBM] * (C + 1),
        out_specs=[HBM, HBM, VMEM],
        scratch_shapes=[
            pltpu.VMEM(gate_up.shape, bf16),
            pltpu.VMEM((seq, width), bf16),
            pltpu.VMEM((seq, both), bf16),
            pltpu.SemaphoreType.DMA((C + 1,)),
        ],
        compiler_params=pltpu.CompilerParams(vmem_limit_bytes=20 * MIB),
        cost_estimate=cost(2 * seq * width * both, 3 * seq * width),
        name="ffn_units",
    )(*in_hbm(*blocks, gate_up))


def ffn_forward_kernel(C, act_ref, down_hbm, *refs):
    keep_refs, give_refs, (down_ref, sems) = refs[: C // 2], refs[C // 2 : C], refs[C:]
    for copy in started(sems, 0, (down_hbm, down_ref)):
        copy.wait()
    parts_of(lambda at: times(act_ref[...], down_ref[:, at]), keep_refs, give_refs)


def ffn_forward(activated, down, C):
    seq, own = activated.shape
    width = down.shape[1]
    result = pl.pallas_call(
        functools.partial(ffn_forward_kernel, C),
        out_shape=[jax.ShapeDtypeStruct((seq // C, width), bf16)] * C,
        in_specs=[VMEM, HBM],
        out_specs=[VMEM] * C,
        scratch_shapes=[pltpu.VMEM(down.shape, bf16), pltpu.SemaphoreType.DMA((1,))],
        compiler_params=pltpu.CompilerParams(vmem_limit_bytes=12 * MIB),
        cost_estimate=cost(seq * width * own, seq * width),
        name="ffn_forward",
    )(activated, *in_hbm(down))
    return result[: C // 2], result[C // 2 :]


def ffn_backward_kernel(C, cuts, *refs):
    g_refs = refs[:C]
    gu_hbm, down_hbm, coef_hbm, g_all_ref, dgu_ref = refs[C : C + 5]
    keep_refs = refs[C + 5 : C + 5 + C // 2]
    give_refs = refs[C + 5 + C // 2 : 2 * C + 5]
    gu_ref, down_ref, coef_ref, sems = refs[2 * C + 5 :]
    copies = started(sems, 0, (down_hbm, down_ref), (coef_hbm, coef_ref), (gu_hbm, gu_ref))
    gather_rows(g_refs, g_all_ref)
    for copy in copies[:2]:
        copy.wait()
    w = down_ref.shape[0] // cuts
    many = 2 if cuts % 2 == 0 else 1

    @pl.loop(0, cuts // many)
    def _(j):
        rows = pl.ds(pl.multiple_of(j * many * w, many * w), many * w)
        grad_act = times_transposed(g_all_ref[...], down_ref[rows, :])
        at = pl.ds(pl.multiple_of(j * many * 2 * w, many * 2 * w), many * 2 * w)
        parts = [grad_act[:, (n // 2) * w : (n // 2 + 1) * w] for n in range(2 * many)]
        both = jnp.concatenate(parts, axis=1)
        dgu_ref[:, at] = (both * coef_ref[:, at].astype(f32)).astype(bf16)

    copies[2].wait()
    parts_of(lambda at: times_transposed(dgu_ref[...], gu_ref[at, :]), keep_refs, give_refs)


def ffn_backward(blocks, gate_up, down, coef, cuts):
    C = len(blocks)
    tokens, width = blocks[0].shape
    seq, own = C * tokens, coef.shape[1] // 2
    part = jax.ShapeDtypeStruct((tokens, width), bf16)
    result = pl.pallas_call(
        functools.partial(ffn_backward_kernel, C, cuts),
        out_shape=[
            jax.ShapeDtypeStruct((seq, width), bf16),
            jax.ShapeDtypeStruct((seq, 2 * own), bf16),
        ]
        + [part] * C,
        in_specs=[VMEM] * C + [HBM] * 3,
        out_specs=[VMEM] * (C + 2),
        scratch_shapes=[
            pltpu.VMEM((width, 2 * own), bf16),
            pltpu.VMEM((own, width), bf16),
            pltpu.VMEM(coef.shape, bf16),
            pltpu.SemaphoreType.DMA((3,)),
        ],
        compiler_params=pltpu.CompilerParams(vmem_limit_bytes=24 * MIB),
        cost_estimate=cost(3 * seq * width * own, 3 * seq * width),
        name="ffn_backward",
    )(*blocks, *in_hbm(gate_up, down, coef))
    return result[:2], result[2 : 2 + C // 2], result[2 + C // 2 :]


def ffn_slices_kernel(C, Z, piece, me_ref, gate_hbm, up_hbm, down_hbm, *refs):
    gu_hbm, rows_hbm, gu_ref, rows_ref, sems = refs
    me = me_ref[0]
    pairs = []
    for j in range(Z):
        for a, ref in enumerate((gate_hbm, up_hbm)):
            at = pl.multiple_of((j * C + me) * piece, piece)
            to = (2 * j + a) * piece
            pairs.append((ref.at[:, pl.ds(at, piece)], gu_ref.at[:, to : to + piece]))
    at = pl.multiple_of(me * piece, piece)
    pairs.append((down_hbm.at[pl.ds(at, piece), :], rows_ref))
    for copy in started(sems, 0, *pairs):
        copy.wait()
    for copy in started(sems, 0, (gu_ref, gu_hbm), (rows_ref, rows_hbm)):
        copy.wait()


def ffn_slices(w_gate, w_up, w_down, me, C, Z):
    rows, ff = w_gate.shape
    width = w_down.shape[1]
    piece = ff // (Z * C)
    shapes = (rows, 2 * Z * piece), (piece, width)
    return pl.pallas_call(
        functools.partial(ffn_slices_kernel, C, Z, piece),
        out_shape=[pltpu.HBM(x, bf16) for x in shapes],
        in_specs=[SMEM, HBM, HBM, HBM],
        out_specs=[HBM, HBM],
        scratch_shapes=[pltpu.VMEM(x, bf16) for x in shapes]
        + [pltpu.SemaphoreType.DMA((2 * Z + 1,))],
        compiler_params=pltpu.CompilerParams(vmem_limit_bytes=8 * MIB),
        cost_estimate=cost(0, 6 * rows * ff // C),
        name="ffn_slices",
    )(me.reshape(1), *in_hbm(w_gate, w_up, w_down))


def arrived(pieces, low_ref, sems):
    pairs = []
    for i, first, ref in pieces:
        pairs.append((ref, low_ref.at[i, pl.ds(first, ref.shape[0]), :]))
    copies = started(sems, 0, *pairs)
    return [[copy for copy, piece in zip(copies, pieces) if piece[0] == i] for i in range(low_ref.shape[0])]


def column_grads_kernel(C, Z, piece, places, me_ref, *refs):
    gate_hbm, up_hbm, low_ref, wide_ref, in_sems, sems = refs[len(places) :]
    me = me_ref[0]
    stride = gate_hbm.shape[1] // Z
    arriving = arrived([(*place, ref) for place, ref in zip(places, refs)], low_ref, in_sems)
    flying = [(), ()]
    for i in range(C):
        slot = i % 2
        for copy in (*flying[slot], *arriving[i]):
            copy.wait()

        @pl.loop(0, low_ref.shape[1] // 16)
        def _(n):
            at = pl.ds(pl.multiple_of(n * 16, 16), 16)
            wide_ref[slot, at, :] = low_ref[i, at, :].astype(f32)

        pairs = []
        for j in range(Z):
            at = pl.multiple_of(j * stride + (me ^ i) * piece, piece)
            for a, ref in enumerate((gate_hbm, up_hbm)):
                to = (2 * j + a) * piece
                pairs.append((wide_ref.at[slot, :, to : to + piece], ref.at[:, pl.ds(at, piece)]))
        flying[slot] = started(sems.at[slot], 0, *pairs)
    for copies in flying:
        for copy in copies:
            copy.wait()


def column_grads(pieces, me, C, Z):
    rows, cols = pieces[0][2].shape
    piece = cols // (2 * Z)
    ff = Z * C * piece
    return pl.pallas_call(
        functools.partial(column_grads_kernel, C, Z, piece, [x[:2] for x in pieces]),
        out_shape=[pltpu.HBM((rows, ff), f32)] * 2,
        in_specs=[SMEM] + [HBM] * len(pieces),
        out_specs=[HBM] * 2,
        scratch_shapes=[
            pltpu.VMEM((C, rows, cols), bf16),
            pltpu.VMEM((2, rows, cols), f32),
            pltpu.SemaphoreType.DMA((len(pieces),)),
            pltpu.SemaphoreType.DMA((2, 2 * Z)),
        ],
        compiler_params=pltpu.CompilerParams(vmem_limit_bytes=16 * MIB),
        cost_estimate=cost(0, 6 * rows * ff),
        name="column_grads",
    )(me.reshape(1), *in_hbm(*[x[2] for x in pieces]))


def row_grads_kernel(C, places, me_ref, *refs):
    out_hbm, low_ref, tall_ref, in_sems, sems = refs[len(places) :]
    me = me_ref[0]
    piece = low_ref.shape[1]
    arriving = arrived([(*place, ref) for place, ref in zip(places, refs)], low_ref, in_sems)
    flying = []
    for i in range(C):
        for copy in arriving[i]:
            copy.wait()

        @pl.loop(0, piece // 16)
        def _(n):
            at = pl.ds(pl.multiple_of(n * 16, 16), 16)
            tall_ref[i, at, :] = low_ref[i, at, :].astype(f32)

        at = pl.multiple_of((me ^ i) * piece, piece)
        flying += started(sems, i, (tall_ref.at[i], out_hbm.at[pl.ds(at, piece), :]))
    for copy in flying:
        copy.wait()


def row_grads(pieces, me, C):
    piece, width = pieces[0][2].shape
    return pl.pallas_call(
        functools.partial(row_grads_kernel, C, [x[:2] for x in pieces]),
        out_shape=pltpu.HBM((C * piece, width), f32),
        in_specs=[SMEM] + [HBM] * len(pieces),
        out_specs=HBM,
        scratch_shapes=[
            pltpu.VMEM((C, piece, width), bf16),
            pltpu.VMEM((C, piece, width), f32),
            pltpu.SemaphoreType.DMA((len(pieces),)),
            pltpu.SemaphoreType.DMA((C,)),
        ],
        compiler_params=pltpu.CompilerParams(vmem_limit_bytes=16 * MIB),
        cost_estimate=cost(0, 4 * C * piece * width),
        name="row_grads",
    )(me.reshape(1), *in_hbm(*[x[2] for x in pieces]))


def middle_forward_kernel(C, Z, piece, info_ref, *refs):
    R = C // 2
    mine_refs, other_refs, w_refs = refs[:R], refs[R:C], refs[C : 2 * C]
    own_hbm, hidden_ref, gain_ref = refs[2 * C : 2 * C + 3]
    middle_ref, normed_ref, att_ref, out_hbm = refs[2 * C + 3 : 2 * C + 7]
    out_ref, low_ref, high_ref, sems = refs[2 * C + 7 :]
    me, line = info_ref[0], info_ref[1]
    rows_z = C * piece
    own_at = pl.ds(pl.multiple_of(line * rows_z, rows_z), rows_z)
    here = started(sems, 1, (own_hbm, out_ref.at[own_at, :]))
    core = me % 2
    tokens, half = hidden_ref.shape[0], mine_refs[0].shape[1]
    for i in range(C):
        for j in range(1, Z):
            at = pl.multiple_of((line ^ j) * rows_z + (me ^ i) * piece, piece)
            out_ref[pl.ds(at, piece), :] = w_refs[i][(j - 1) * piece : j * piece, :]
    for copy in here:
        copy.wait()
    saved = started(sems, 0, (out_ref, out_hbm))
    low_ref[...] = jnp.zeros_like(low_ref)
    high_ref[...] = jnp.zeros_like(high_ref)
    for s in range(R):
        own = mine_refs[s][:tokens, :].astype(f32)
        other = other_refs[s][tokens:, :].astype(f32)
        low_ref[:, :half] = jnp.where(core == 0, own, other)
        high_ref[:, :half] = jnp.where(core == 0, other, own)
        pair = low_ref[...] + pltpu.roll(high_ref[...], half, 1)
        at = pl.multiple_of(((me // 2) ^ s) * 2 * half, 2 * half)
        att_ref[:, pl.ds(at, 2 * half)] = pair.astype(bf16)
    middle = hidden_ref[...] + times(att_ref[...], out_ref[...])
    middle_ref[...] = middle
    normed_ref[...] = (middle * norm_scale(middle) * gain_ref[...]).astype(bf16)
    for copy in saved:
        copy.wait()


def middle_forward(mine, other, w_blocks, w_own, hidden, gain, me, line, Z):
    C = len(w_blocks)
    tokens, width = hidden.shape
    half = mine[0].shape[1]
    piece = w_own.shape[0] // C
    if piece % 16 or (2 * half) % LANES:
        rows = jnp.stack(unsort([x.reshape(Z - 1, piece, width) for x in w_blocks], me), axis=1)
        rows = jnp.concatenate([w_own[None], rows.reshape(Z - 1, C * piece, width)])
        out_all = jnp.concatenate([pick(rows, line ^ j) for j in range(Z)], axis=0)
        heads = []
        for a, b in zip(mine, other, strict=True):
            heads += [a[:tokens], b[tokens:]]
        attended = jnp.concatenate(unsort(heads, me), axis=1)
        middle = hidden + times(attended, out_all)
        return middle, (middle * norm_scale(middle) * gain).astype(bf16), attended, out_all
    return pl.pallas_call(
        functools.partial(middle_forward_kernel, C, Z, piece),
        out_shape=[
            jax.ShapeDtypeStruct((tokens, width), f32),
            jax.ShapeDtypeStruct((tokens, width), bf16),
            jax.ShapeDtypeStruct((tokens, width), bf16),
            pltpu.HBM((width, width), bf16),
        ],
        in_specs=[SMEM] + [VMEM] * 2 * C + [HBM] + [VMEM] * 2,
        out_specs=[VMEM] * 3 + [HBM],
        scratch_shapes=[
            pltpu.VMEM((width, width), bf16),
            pltpu.VMEM((tokens, 2 * half), f32),
            pltpu.VMEM((tokens, 2 * half), f32),
            pltpu.SemaphoreType.DMA((2,)),
        ],
        compiler_params=pltpu.CompilerParams(vmem_limit_bytes=16 * MIB),
        cost_estimate=cost(tokens * width * width, 3 * width * width),
        name="middle_forward",
    )(jnp.stack([me, line]), *mine, *other, *w_blocks, *in_hbm(w_own), hidden, gain.reshape(1, width))


def middle_backward_kernel(R, info_ref, *refs):
    own_ref, got_refs = refs[0], refs[1:R]
    middle_ref, gain_ref, grad_out_ref, out_hbm = refs[R : R + 4]
    grad_ref, low_ref, gain_grad_ref = refs[R + 4 : R + 7]
    pair_refs, (att_ref, out_ref, sems) = refs[R + 7 : 2 * R + 7], refs[2 * R + 7 :]
    copies = started(sems, 0, (out_hbm, out_ref))
    upstream = own_ref[...]
    for ref in got_refs:
        upstream = upstream + ref[...].astype(f32)
    middle = middle_ref[...]
    back, gain_grad = norm_back(upstream, middle, norm_scale(middle), gain_ref[...])
    gain_grad_ref[...] = gain_grad.reshape(gain_grad_ref.shape)
    grad = grad_out_ref[...] + back
    grad_ref[...] = grad
    low = grad.astype(bf16)
    low_ref[...] = low
    for copy in copies:
        copy.wait()
    att_ref[...] = times_transposed(low, out_ref[...]).astype(bf16)
    pair_cols = pair_refs[0].shape[1]
    for s in range(R):
        at = pl.multiple_of(((info_ref[0] // 2) ^ s) * pair_cols, pair_cols)
        pair_refs[s][...] = att_ref[:, pl.ds(at, pair_cols)]


def middle_backward(own, got, middle, gain, grad_output, out_all, me):
    R = len(got) + 1
    tokens, width = middle.shape
    pair_cols = width // R
    if pair_cols % LANES:
        upstream = total(own, got)
        back, gain_grad = norm_back(upstream, middle, norm_scale(middle), gain)
        grad = grad_output + back
        low = grad.astype(bf16)
        cut = times_transposed(low, out_all).astype(bf16).reshape(tokens, R, pair_cols)
        return grad, low, gain_grad[None], *[pick(cut, (me // 2) ^ s, 1) for s in range(R)]
    result = pl.pallas_call(
        functools.partial(middle_backward_kernel, R),
        out_shape=[
            jax.ShapeDtypeStruct((tokens, width), f32),
            jax.ShapeDtypeStruct((tokens, width), bf16),
            jax.ShapeDtypeStruct((1, width), f32),
        ]
        + [pltpu.VMEM((tokens, pair_cols), bf16)] * R,
        in_specs=[SMEM] + [VMEM] * (R + 3) + [HBM],
        out_specs=[VMEM] * (3 + R),
        scratch_shapes=[
            pltpu.VMEM((tokens, width), bf16),
            pltpu.VMEM((width, width), bf16),
            pltpu.SemaphoreType.DMA((1,)),
        ],
        compiler_params=pltpu.CompilerParams(vmem_limit_bytes=16 * MIB),
        cost_estimate=cost(tokens * width * width, 3 * width * width),
        name="middle_backward",
    )(me.reshape(1), own, *got, middle, gain.reshape(1, width), grad_output, *in_hbm(out_all))
    return result


def out_grads_kernel(C, Z, piece, info_ref, att_ref, low_ref, *refs):
    keep_refs, give_refs, sum_ref = refs[: C // 2], refs[C // 2 : C], refs[C]
    me = info_ref[0]
    rows_z = C * piece
    sum_ref[...] = transposed_times(att_ref[...], low_ref[...])
    for i in range(C):
        ref = (give_refs if i % 2 else keep_refs)[i // 2]
        for j in range(Z):
            at = pl.multiple_of(j * rows_z + (me ^ i) * piece, piece)
            ref[j * piece : (j + 1) * piece, :] = sum_ref[pl.ds(at, piece), :].astype(bf16)


def out_grads(attended, low, me, C, Z):
    width = attended.shape[1]
    piece = width // (C * Z)
    if piece % 16:
        grad = transposed_times(attended, low).astype(bf16).reshape(Z, C, piece, width)
        grad = [pick(grad, me ^ i, 1).reshape(Z * piece, width) for i in range(C)]
        return grad[0::2], grad[1::2]
    result = pl.pallas_call(
        functools.partial(out_grads_kernel, C, Z, piece),
        out_shape=[pltpu.VMEM((Z * piece, width), bf16)] * C,
        in_specs=[SMEM, VMEM, VMEM],
        out_specs=[VMEM] * C,
        scratch_shapes=[pltpu.VMEM((width, width), f32)],
        compiler_params=pltpu.CompilerParams(vmem_limit_bytes=18 * MIB),
        cost_estimate=cost(2 * attended.shape[0] * width * width, 3 * width * width),
        name="out_grads",
    )(me.reshape(1), attended, low)
    return result[: C // 2], result[C // 2 :]


EXTRA = 16


def attention_packs_kernel(Z, C, info_ref, *refs):
    R = C // 2
    grad_ref, out_refs = refs[0], refs[1 : R + 1]
    gain_one_ref, gain_two_ref, error_ref, pack_hbm, token_ref = refs[R + 1 : R + 6]
    sum_ref, tall_ref, sems = refs[R + 6 :]
    token_ref[...] = jnp.zeros_like(token_ref)
    width, cols = grad_ref.shape
    rows, tall = width // Z, tall_ref.shape[0] // Z
    piece = sum_ref.shape[0] // Z
    out = out_refs[0][...]
    for ref in out_refs[1:]:
        out = out + ref[...].astype(f32)
    sum_ref[...] = out.astype(bf16)
    line = info_ref[0]
    row = lax.broadcasted_iota(jnp.int32, (EXTRA, cols), 0)
    lane = lax.broadcasted_iota(jnp.int32, (EXTRA, cols), 1)
    error = error_ref[0, 0]
    high = error.astype(bf16).astype(f32)
    error = jnp.where(lane == 2 * line, high, jnp.where(lane == 2 * line + 1, error - high, 0.0))
    for j in range(Z):
        under = j * tall + rows
        for n in range(width // cols):
            at = slice(n * cols, (n + 1) * cols)
            tall_ref[under + n * piece : under + (n + 1) * piece, :] = sum_ref[
                j * piece : (j + 1) * piece, at
            ]
        at = slice(j * rows, (j + 1) * rows)
        extra = jnp.where(row == 0, gain_one_ref[0:1, at], jnp.where(row == 1, gain_two_ref[0:1, at], 0.0))
        extra = jnp.where(row == 2, error, extra)
        tall_ref[(j + 1) * tall - EXTRA : (j + 1) * tall, :] = extra.astype(bf16)

    @pl.loop(0, rows // 16)
    def _(n):
        for j in range(Z):
            at = pl.ds(pl.multiple_of(j * rows + n * 16, 16), 16)
            to = pl.ds(pl.multiple_of(j * tall + n * 16, 16), 16)
            tall_ref[to, :] = grad_ref[at, :]

    for copy in started(sems, 0, (tall_ref, pack_hbm)):
        copy.wait()


def attention_packs(grad, out_parts, gain_one, gain_two, error, line, Z, C):
    width, cols = grad.shape
    rows = width // Z
    tall, parts = out_parts[0].shape[0], C // 2
    piece = tall // Z
    if rows != cols or piece % 16:
        grad_out = total(out_parts[0], out_parts[1:]).astype(bf16)
        lane = jnp.arange(cols, dtype=jnp.int32)
        high = error.astype(bf16)
        low = (error - high.astype(f32)).astype(bf16)
        zero = jnp.zeros((), bf16)
        error_row = jnp.where(lane == 2 * line, high, jnp.where(lane == 2 * line + 1, low, zero))
        packs = []
        for j in range(Z):
            at = slice(j * rows, (j + 1) * rows)
            out = grad_out[j * piece : (j + 1) * piece]
            gains = [jnp.pad(x[at].astype(bf16), (0, cols - rows)) for x in (gain_one[0], gain_two[0])]
            extra = jnp.pad(jnp.stack([*gains, error_row]), ((0, EXTRA - 3), (0, 0)))
            packs += [grad[at], *[out[:, c : c + cols] for c in range(0, width, cols)], extra]
        return jnp.concatenate(packs, axis=0), jnp.zeros((8, LANES), f32)
    shape = (Z * (rows + piece * width // cols + EXTRA), cols)
    return pl.pallas_call(
        functools.partial(attention_packs_kernel, Z, C),
        out_shape=[pltpu.HBM(shape, bf16), jax.ShapeDtypeStruct((8, LANES), f32)],
        in_specs=[SMEM] + [VMEM] * (parts + 4),
        out_specs=[HBM, VMEM],
        scratch_shapes=[
            pltpu.VMEM((tall, width), bf16),
            pltpu.VMEM(shape, bf16),
            pltpu.SemaphoreType.DMA((1,)),
        ],
        compiler_params=pltpu.CompilerParams(vmem_limit_bytes=16 * MIB),
        cost_estimate=cost(0, 3 * width * width),
        name="attention_packs",
    )(line.reshape(1), grad, *out_parts, gain_one, gain_two, error.reshape(1, 1))


def attention_grads_kernel(C, rows, q_cols, kv_cols, places, me_ref, *refs):
    count = len(places)
    gain_ref, rows_gain_ref, valid_ref = refs[count : count + 3]
    *grads_hbm, gains_ref, loss_ref = refs[count + 3 : count + 9]
    low_ref, extra_ref, query_ref, key_ref, value_ref, out_ref, in_sems, out_sems = refs[count + 9 :]
    me = me_ref[0]
    cols = low_ref.shape[2]
    strips = out_ref.shape[1] // cols
    piece = (low_ref.shape[1] - rows - EXTRA) // strips
    arriving = arrived([(*place, ref) for place, ref in zip(places, refs)], low_ref, in_sems)
    for i in range(C):
        for copy in arriving[i]:
            copy.wait()
        at = pl.ds(pl.multiple_of((me ^ i) * piece, piece), piece)
        for c in range(strips):
            strip = low_ref[i, rows + c * piece : rows + (c + 1) * piece, :]
            out_ref[at, c * cols : (c + 1) * cols] = strip.astype(f32)
        extra_ref[me ^ i] = low_ref[i, low_ref.shape[1] - EXTRA :, :].astype(f32)
    leaving = started(out_sems, 3, (out_ref, grads_hbm[3]))
    extra = extra_ref[0]
    for b in range(1, C):
        extra = extra + extra_ref[b]
    row = lax.broadcasted_iota(jnp.int32, gains_ref.shape, 0)
    gains_ref[...] = extra[:8, :] / jnp.where(row == 0, gain_ref[...], 1.0)
    loss_ref[...] = jnp.sum(extra[2:3, :], axis=1, keepdims=True) / valid_ref[0, 0]
    lane = lax.broadcasted_iota(jnp.int32, (rows, cols), 1)
    for n, (ref, first, size) in enumerate(
        (
            (query_ref, 0, q_cols),
            (key_ref, q_cols, kv_cols),
            (value_ref, q_cols + kv_cols, kv_cols),
        )
    ):
        many = cols // size
        for group in range(C // many):
            whole = None
            for j in range(many):
                x = low_ref[me ^ (group * many + j), :rows, :].astype(f32) * rows_gain_ref[...]
                shift = (j * size - first) % cols
                x = pltpu.roll(x, shift, 1) if shift else x
                whole = x if whole is None else jnp.where(lane < j * size, whole, x)
            ref[:, group * cols : (group + 1) * cols] = whole
        leaving += started(out_sems, n, (ref, grads_hbm[n]))
    for copy in leaving:
        copy.wait()


def attention_grads(pieces, me, gain, valid_count, C, rows, width, q_cols, kv_cols, kv_copies):
    tall, cols = pieces[0][2].shape
    strips = width // cols
    piece = (tall - rows - EXTRA) // strips
    many = C // kv_copies
    if kv_copies > 1 or cols % q_cols or cols % kv_cols or q_cols + 2 * kv_cols != cols or rows != cols or piece % 16:
        parts = unsort([x[2] for x in pieces], me)

        def kv_final(start):
            own = [part[:rows, start : start + kv_cols].astype(f32) * gain[:, None] for part in parts]
            own = [sum(own[n : n + kv_copies]) for n in range(0, C, kv_copies)]
            return jnp.concatenate(own, axis=1)

        query = jnp.concatenate([part[:rows, :q_cols] for part in parts], axis=1).astype(f32) * gain[:, None]
        outs = [part[rows : tall - EXTRA].reshape(strips, piece, cols).transpose(1, 0, 2) for part in parts]
        out = jnp.concatenate([x.reshape(piece, width) for x in outs], axis=0).astype(f32)
        extra = sum([part[tall - EXTRA :].astype(f32) for part in parts])
        gains = extra[0, :rows] / gain, extra[1, :rows]
        loss = jnp.sum(extra[2]) / valid_count
        return query, kv_final(q_cols), kv_final(q_cols + kv_cols), out, *gains, loss
    shapes = [(rows, C * q_cols), (rows, many * kv_cols), (rows, many * kv_cols), (C * piece, width)]
    *grads, gains, loss = pl.pallas_call(
        functools.partial(
            attention_grads_kernel, C, rows, q_cols, kv_cols, [x[:2] for x in pieces]
        ),
        out_shape=[
            *[pltpu.HBM(x, f32) for x in shapes],
            jax.ShapeDtypeStruct((8, cols), f32),
            jax.ShapeDtypeStruct((1, 1), f32),
        ],
        in_specs=[SMEM] + [HBM] * len(pieces) + [VMEM] * 3,
        out_specs=[HBM] * 4 + [VMEM] * 2,
        scratch_shapes=[
            pltpu.VMEM((C, tall, cols), bf16),
            pltpu.VMEM((C, EXTRA, cols), f32),
            *[pltpu.VMEM(x, f32) for x in shapes],
            pltpu.SemaphoreType.DMA((len(pieces),)),
            pltpu.SemaphoreType.DMA((4,)),
        ],
        compiler_params=pltpu.CompilerParams(vmem_limit_bytes=24 * MIB),
        cost_estimate=cost(0, 8 * rows * C * cols),
        name="attention_grads",
    )(
        me.reshape(1),
        *in_hbm(*[x[2] for x in pieces]),
        gain.reshape(1, rows),
        gain.reshape(rows, 1),
        valid_count.reshape(1, 1),
    )
    return *grads, gains[0], gains[1], loss[0, 0]


def local(
    inputs,
    teacher,
    lengths,
    w_query,
    w_key,
    w_value,
    w_out,
    w_gate,
    w_up,
    w_down,
    gain_attn,
    gain_ffn,
):
    hidden_in = inputs[0]
    target = teacher[0]
    seq_length = lengths[0]
    tokens, width = hidden_in.shape
    C = lax.axis_size("ctx")
    Z = lax.axis_size("fsdp")
    R = C // 2
    p = lax.axis_index("ctx")
    z = lax.axis_index("fsdp")
    core = p % 2
    rows_z = width // Z
    seq = C * tokens
    q_heads = HEADS // C
    kv_heads = max(1, KV_HEADS // C)
    kv_copies = max(1, C // KV_HEADS)
    q_cols = q_heads * HEAD_DIM
    kv_cols = kv_heads * HEAD_DIM
    qkv_cols = q_cols + 2 * kv_cols
    positions = p * tokens + jnp.arange(tokens, dtype=jnp.int32)

    kv_start = (p * KV_HEADS // C) * HEAD_DIM
    out_piece = rows_z // C
    qkv_own = jnp.concatenate(
        [
            lax.dynamic_slice_in_dim(w_query, p * q_cols, q_cols, 1),
            lax.dynamic_slice_in_dim(w_key, kv_start, kv_cols, 1),
            lax.dynamic_slice_in_dim(w_value, kv_start, kv_cols, 1),
            jnp.zeros((rows_z, -qkv_cols % LANES), bf16),
        ],
        axis=1,
    )
    out_own = lax.dynamic_slice_in_dim(w_out, p * out_piece, out_piece, 0)

    qkv_own = (qkv_own.astype(f32) * gain_attn.astype(f32)[:, None]).astype(bf16)
    scale_one = norm_scale(hidden_in)
    normed_one = (hidden_in * scale_one).astype(bf16)

    small = jnp.concatenate(
        [gain_attn.astype(f32), gain_ffn.astype(f32), jnp.full((LANES,), seq_length).astype(f32)]
    )
    small = after(small.reshape(1, -1), qkv_own, normed_one)
    ff = w_gate.shape[1]
    ff_piece, own = ff // (Z * C), ff // C
    packed_ffn = ff_piece % LANES == 0
    if packed_ffn:
        cuts = Z
        gate_up_own, down_own = ffn_slices(w_gate, w_up, w_down, p, C, Z)
    else:
        cuts = 1
        gate_up_own = jnp.concatenate(
            [pick(w.reshape(rows_z, Z, C, ff_piece), p, 2).reshape(rows_z, own) for w in (w_gate, w_up)],
            axis=1,
        )
        down_own = lax.dynamic_slice_in_dim(w_down, p * ff_piece, ff_piece, 0)
    tables = rope_tables(seq)
    normed_got, weights, tables = lax.optimization_barrier(
        (plane_sends(normed_one), line_sends(qkv_own), tables)
    )
    normed_blocks = together(core_blocks([normed_one] + normed_got))
    gate_up_own, down_own = after((gate_up_own, down_own), weights)
    gate_up = lax.all_gather(gate_up_own, "fsdp", axis=0, tiled=True)
    down_rows = lax.all_gather(down_own, "fsdp", axis=0, tiled=True)
    out_line = line_sends(after(out_own, weights))
    small_got = line_sends(after(small, weights))
    (normed_all, *saved), mine = attention_forward(
        normed_blocks, [qkv_own] + weights, tables, p, seq_length, z, q_heads, kv_heads
    )

    out_line, small_got, normed_all = lax.optimization_barrier((out_line, small_got, normed_all))
    small = jnp.stack(unsort([small] + small_got, z)).reshape(Z, -1)
    gain_two = small[:, rows_z : 2 * rows_z].reshape(width)
    valid_count = jnp.sum(small[:, 2 * rows_z])
    out_line = jnp.concatenate(out_line, axis=0)
    out_blocks = together(core_blocks([out_line] + together(plane_sends(out_line))))
    mine = after(mine, out_blocks)
    mine = [mine[0]] + together([partner(mine[s], "ctx", 2 * s) for s in range(1, R)])
    other = [partner(x, "ctx", 1) for x in mine]
    middle, normed_two_own, attended_tokens, out_all = middle_forward(
        mine, other, out_blocks, w_out, hidden_in, gain_two, p, z, Z
    )

    normed_two, coef, activated = ffn_units(plane_blocks(normed_two_own), gate_up, cuts)
    keep, give = ffn_forward(activated, after(down_rows, activated), C)
    output = middle + plane_reduce(keep, give)

    valid_rows = (positions < seq_length).astype(f32)
    residual_error = output - target
    squares = jnp.sum(valid_rows[:, None] * residual_error * residual_error)
    grad_output = valid_rows[:, None] * (2.0 * residual_error) / valid_count

    (grad_low, grad_gu), keep, give = ffn_backward(
        plane_blocks(grad_output.astype(bf16)), gate_up, down_rows, coef, cuts
    )
    chips = chip_sums(keep, give)
    grad_gate_up = transposed_times(normed_two, after(grad_gu, chips)).astype(bf16)
    grad_down = transposed_times(activated, after(grad_low, grad_gate_up)).astype(bf16)
    shard_gate_up = lax.psum_scatter(grad_gate_up, "fsdp", scatter_dimension=0, tiled=True)
    shard_down = lax.psum_scatter(grad_down, "fsdp", scatter_dimension=0, tiled=True)
    grad_middle, m_low, grad_gain_two, *pairs = middle_backward(
        chips[0], after(chip_sends(chips), grad_down), middle, gain_two, grad_output, out_all, p
    )

    out_keep, out_give = out_grads(attended_tokens, after(m_low, pairs), p, C, Z)
    out_chips = chip_sums(out_keep, out_give)
    mine = [partner(pairs[s], "ctx", 2 * s) for s in range(1, R)]
    mine = [pairs[0]] + list(after(mine, out_chips))
    other = [partner(x, "ctx", 1) for x in mine]
    grad_qkv, gain_part, keep, give = attention_backward(
        mine, other, (normed_all, *saved), tables, p, seq_length, q_heads, kv_heads
    )
    chips = chip_sums(keep, give)
    square = packed_ffn and C == 8
    out_got, grad_qkv = lax.optimization_barrier((chip_sends(out_chips), grad_qkv))
    packs, token = attention_packs(
        grad_qkv, [out_chips[0]] + out_got, gain_part, grad_gain_two, squares, z, Z, C
    )
    shard_packs = lax.psum_scatter(packs, "fsdp", scatter_dimension=0, tiled=True)
    normed_got = [partner(x, "ctx", 2 * (s + 1)) for s, x in enumerate(after(chips[1:], out_got))]
    near = near_sends(after(shard_gate_up, out_got)) if square else []
    normed_got, near, token = lax.optimization_barrier((normed_got, near, token))
    grad_normed_one = total(chips[0], normed_got)
    back_one, _ = norm_back(grad_normed_one, hidden_in, scale_one, 1.0)
    grad_hidden = grad_middle + back_one


    if square:
        down_near = near_sends(after(shard_down, normed_got))
        far, down_near = lax.optimization_barrier((far_sends(near), down_near))
        pieces = square_pieces(shard_gate_up, near, far)
        final_gate, final_up = column_grads(pieces, p, C, Z)
        pack_near = near_sends(after(shard_packs, far))
        down_far, pack_near, final_gate = lax.optimization_barrier(
            (far_sends(down_near), pack_near, final_gate)
        )
        final_down = row_grads(square_pieces(shard_down, down_near, down_far), p, C)
        pack_far, final_down, grad_hidden = lax.optimization_barrier(
            (far_sends(pack_near), final_down, grad_hidden)
        )
        pieces = square_pieces(shard_packs, pack_near, pack_far)
    else:
        pieces = [(i, 0, block) for i, block in enumerate(plane_blocks(shard_packs))]
        gate_up, down = [
            jnp.stack(unsort(plane_blocks(x), p)).astype(f32) for x in (shard_gate_up, shard_down)
        ]
        gate_up = gate_up.reshape(C, rows_z, 2, Z, ff_piece).transpose(2, 1, 3, 0, 4)
        final_gate, final_up = gate_up.reshape(2, rows_z, ff)
        final_down = down.reshape(C * ff_piece, width)
    final_query, final_key, final_value, final_out, *final_gains, loss_value = attention_grads(
        pieces,
        p,
        gain_attn.astype(f32),
        valid_count,
        C,
        rows_z,
        width,
        q_cols,
        kv_cols,
        kv_copies,
    )

    return (
        output[None],
        loss_value,
        grad_hidden[None],
        final_query,
        final_key,
        final_value,
        final_out,
        final_gate,
        final_up,
        final_down,
        *final_gains,
    )


def solution(mesh):
    return jax.shard_map(
        local,
        mesh=mesh,
        in_specs=(
            P("fsdp", "ctx", None),
            P("fsdp", "ctx", None),
            P("fsdp"),
            P("fsdp", None),
            P("fsdp", None),
            P("fsdp", None),
            P("fsdp", None),
            P("fsdp", None),
            P("fsdp", None),
            P("fsdp", None),
            P("fsdp"),
            P("fsdp"),
        ),
        out_specs=(
            P("fsdp", "ctx", None),
            P(),
            P("fsdp", "ctx", None),
            P("fsdp", None),
            P("fsdp", None),
            P("fsdp", None),
            P("fsdp", None),
            P("fsdp", None),
            P("fsdp", None),
            P("fsdp", None),
            P("fsdp"),
            P("fsdp"),
        ),
        check_vma=False,
    )
```
